32 devices in a mesh: groups: 2 (over y), space: 4 (over z), chan: 4 (over x, core).
Axes of the slice: x: 2, y: 2, z: 4, core: 2. Of those that a mesh axis runs over, the one named last changes fastest.
Arguments:
- labels: int32 [32, 32, 512], P(('groups', 'space'), 'chan'), parts along dimension 0, may hold values from 0 to 1023
- table: bfloat16 [1024, 16], replicated, may hold values from -6 to 6
- fine_weight: bfloat16 [27, 16, 16], replicated, may hold values from -0.3125 to 0.3125
- fine_cot: bfloat16 [16, 32, 32, 512], P(None, ('groups', 'space'), 'chan'), parts along dimension 1, may hold values from -6 to 6
- bott_in: bfloat16 [512, 16, 128], P('chan', ('groups', 'space')), parts along dimension 1, may hold values from -6 to 6
- bott_weight: bfloat16 [512, 27, 512], P('chan'), may hold values from -0.0625 to 0.0625
- bott_cot: bfloat16 [512, 16, 128], P('chan', ('groups', 'space')), parts along dimension 1, may hold values from -6 to 6
Outputs:
- fine_out: bfloat16 [16, 32, 32, 512], P(None, ('groups', 'space'), 'chan'), parts along dimension 1
- fine_wgrad: float32 [54, 16, 16], P('groups'), parts along dimension 0
- bott_out: bfloat16 [512, 16, 128], P('chan', ('groups', 'space')), parts along dimension 1
- bott_dgrad: bfloat16 [512, 16, 128], P('chan', ('groups', 'space')), parts along dimension 1
- bott_wgrad: float32 [1024, 27, 512], P(('groups', 'chan')), parts along dimension 0
The draws below stay inside these ranges and needn't reach their ends.
There are 2 independent parts, one for each index of `groups`. The reference program is written for one: setup_inputs(seed, part) draws one part's arguments, and reference() takes and returns one part's arrays. A program takes and returns all parts, laid end to end along the dimension named above; an argument that names none is the same for every part. Nothing has to cross between parts.
All inputs are finite; a program needn't handle non-finite values.
Results may differ from the reference program's by a relative error of at most 0.005.
Values may be sent and summed in bfloat16 or wider, within the bound.
No kernel may reach another device: no remote copies, remote signals or barrier semaphores. Data moves between devices by JAX's collectives and lax.ppermute only.
A program may use at most 128 MiB of HBM per device.

```python
import jax
import jax.numpy as jnp
from jax import lax

CF = 16
C = 512
NGRAIN = 1024
FW = 512
BY = 4
BW = 32
FX = 16
FY = 32
BX = 8


def set_ends(entries, rng, least, largest):
    longest = entries.shape.index(max(entries.shape))
    spots = []
    for shift in (0, 1):
        where = [jax.random.randint(jax.random.fold_in(rng, axis), (), 0, length) for axis, length in enumerate(entries.shape)]
        where[longest] = (where[longest] + shift) % entries.shape[longest]
        spots.append(tuple(where))
    return entries.at[spots[0]].set(least).at[spots[1]].set(largest)


def spiked(drawn, own_key, source, target, parts, factor):
    owner, partner = [(jnp.arange(drawn.shape[axis_at]) // (drawn.shape[axis_at] // parts)).reshape([-1 if axis == axis_at else 1 for axis in range(drawn.ndim)]) for axis_at in (source, target)]
    chosen = jax.random.permutation(own_key, parts)[partner]
    strong = (owner == chosen) | (owner == (partner + parts // 2) % parts)
    return jnp.where(strong, factor * drawn, drawn)


def block_scale(own_key, dims, pieces, least, top_value):
    def one(dim, shards_of):
        steps = jax.random.uniform(jax.random.fold_in(jax.random.fold_in(own_key, 6), dim), (shards_of,), jnp.float32, least / len(pieces), top_value / len(pieces))
        return jnp.repeat(jnp.exp(steps), dims[dim] // shards_of).reshape((-1,) + (1,) * (len(dims) - dim - 1))

    level = one(*pieces[0])
    for cut in pieces[1:]:
        level = level * one(*cut)
    return level


def noise(key, extent, deviation, most, split=(), kind=jnp.bfloat16):
    result = jax.random.normal(key, extent, jnp.float32) * deviation
    if len(split) > 0:
        result = block_scale(key, extent, split, -0.22, 0.18) * result
    return jnp.clip(result, min=-most, max=most).astype(kind)


def heavy_noise(rng, dims, scale, limit, shards, heavy, held_as=jnp.bfloat16):
    values = scale * jax.random.normal(rng, dims, jnp.float32)
    if shards:
        values = values * block_scale(rng, dims, shards, -0.22, 0.18)
    return jnp.clip(spiked(values, jax.random.fold_in(rng, 3), *heavy), -limit, limit).astype(held_as)


def setup_inputs(seed: int = 0, part: int = 0) -> dict:
    arg_keys = jax.random.split(jax.random.key(seed), 8)
    own_keys = jax.random.split(jax.random.fold_in(arg_keys[7], part), 8)
    labels = set_ends(jax.random.randint(own_keys[0], (FX, FY, FW), 0, NGRAIN), jax.random.fold_in(own_keys[0], 1), 0, NGRAIN - 1).astype(jnp.int32)
    table = noise(arg_keys[1], (NGRAIN, CF), 1.0, 6.0)
    fine_weight = noise(arg_keys[2], (27, CF, CF), (27 * CF) ** -0.5, 0.3125)
    fine_cot = noise(own_keys[3], (CF, FX, FY, FW), 1.0, 6.0, ((1, 4), (2, 4)))
    bott_in = heavy_noise(own_keys[4], (C, BX, BY * BW), 1.0, 6.0, ((0, 4), (1, 4)), (1, 0, 4, 2.0))
    bott_weight = heavy_noise(arg_keys[5], (C, 27, C), (27 * C) ** -0.5, 0.0625, ((0, 4),), (0, 2, 4, 2.0))
    bott_cot = noise(own_keys[6], (C, BX, BY * BW), 1.0, 6.0, ((0, 4), (1, 4)))
    return dict(labels=labels, table=table, fine_weight=fine_weight, fine_cot=fine_cot, bott_in=bott_in, bott_weight=bott_weight, bott_cot=bott_cot)


def shift_flat(block, step_y, step_w, width):
    total = block.shape[-1]
    reach = width + 1
    padded = jnp.pad(block, [(0, 0)] * (block.ndim - 1) + [(reach, reach)])
    offset = reach + step_y * width + step_w
    moved = lax.slice_in_dim(padded, offset, offset + total, axis=block.ndim - 1)
    column = jnp.arange(total, dtype=jnp.int32) % width + step_w
    inside = (column >= 0) & (column < width)
    return jnp.where(inside, moved, jnp.zeros_like(moved))


def offset_number(step_x, step_y, step_w):
    return 9 * (step_x + 1) + 3 * (step_y + 1) + (step_w + 1)


def silu_parts(pre_act):
    sigmoid_val = jax.nn.sigmoid(pre_act)
    return pre_act * sigmoid_val, sigmoid_val * (1.0 + pre_act * (1.0 - sigmoid_val))


def reference(labels, table, fine_weight, fine_cot, bott_in, bott_weight, bott_cot):
    feats = jnp.take(table.T, labels, axis=1)
    framed = jnp.pad(feats, ((0, 0), (1, 1), (1, 1), (1, 1))).astype(jnp.float32)
    fine_kernel = fine_weight.astype(jnp.float32)
    fine_pre = jnp.zeros((CF, FX, FY, FW), jnp.float32)
    for step_x in (-1, 0, 1):
        for step_y in (-1, 0, 1):
            for step_w in (-1, 0, 1):
                piece = framed[:, 1 + step_x:1 + step_x + FX, 1 + step_y:1 + step_y + FY, 1 + step_w:1 + step_w + FW]
                fine_pre = fine_pre + jnp.einsum("cxyw,co->oxyw", piece, fine_kernel[offset_number(step_x, step_y, step_w)])
    fine_act, fine_slope = silu_parts(fine_pre)
    fine_out = fine_act.astype(jnp.bfloat16)
    fine_delta = (fine_cot.astype(jnp.float32) * fine_slope).astype(jnp.bfloat16).astype(jnp.float32)
    fine_scale = (FX * FY * FW) ** -0.5
    fine_terms = [None] * 27
    for step_x in (-1, 0, 1):
        for step_y in (-1, 0, 1):
            for step_w in (-1, 0, 1):
                piece = framed[:, 1 + step_x:1 + step_x + FX, 1 + step_y:1 + step_y + FY, 1 + step_w:1 + step_w + FW]
                fine_terms[offset_number(step_x, step_y, step_w)] = jnp.einsum("cxyw,oxyw->co", piece, fine_delta) * fine_scale
    fine_wgrad = jnp.stack(fine_terms, axis=0)

    kernel = bott_weight.astype(jnp.float32)
    slabs = jnp.pad(bott_in, ((0, 0), (1, 1), (0, 0))).astype(jnp.float32)
    bott_pre = jnp.zeros((C, BX, BY * BW), jnp.float32)
    for step_y in (-1, 0, 1):
        for step_w in (-1, 0, 1):
            moved = shift_flat(slabs, step_y, step_w, BW)
            for step_x in (-1, 0, 1):
                plane = moved[:, 1 + step_x:1 + step_x + BX]
                bott_pre = bott_pre + jnp.einsum("cpv,oc->opv", plane, kernel[:, offset_number(step_x, step_y, step_w), :])
    bott_act, bott_slope = silu_parts(bott_pre)
    bott_out = bott_act.astype(jnp.bfloat16)
    bott_delta = (bott_cot.astype(jnp.float32) * bott_slope).astype(jnp.bfloat16).astype(jnp.float32)
    delta_slabs = jnp.pad(bott_delta, ((0, 0), (1, 1), (0, 0)))
    dgrad = jnp.zeros((C, BX, BY * BW), jnp.float32)
    bott_scale = (BX * BY * BW) ** -0.5
    bott_terms = [None] * 27
    for step_y in (-1, 0, 1):
        for step_w in (-1, 0, 1):
            back = shift_flat(delta_slabs, -step_y, -step_w, BW)
            moved = shift_flat(slabs, step_y, step_w, BW)
            for step_x in (-1, 0, 1):
                number = offset_number(step_x, step_y, step_w)
                plane = back[:, 1 - step_x:1 - step_x + BX]
                dgrad = dgrad + jnp.einsum("opv,oc->cpv", plane, kernel[:, number, :])
                source = moved[:, 1 + step_x:1 + step_x + BX]
                bott_terms[number] = jnp.einsum("cpv,opv->oc", source, bott_delta) * bott_scale
    bott_dgrad = dgrad.astype(jnp.bfloat16)
    bott_wgrad = jnp.stack(bott_terms, axis=1)
    return (fine_out, fine_wgrad, bott_out, bott_dgrad, bott_wgrad)
```

```python
import functools
import jax
import jax.numpy as jnp
import numpy as np
from jax import lax
from jax.experimental import pallas as pl
from jax.experimental.pallas import tpu as pltpu
from jax.sharding import PartitionSpec as P

BW = 32
F32 = jnp.float32
BF16 = jnp.bfloat16
VM = pl.BlockSpec(memory_space=pltpu.VMEM)
HB = pl.BlockSpec(memory_space=pl.ANY)


def silu_parts(pre):
    s = jax.nn.sigmoid(pre)
    return pre * s, s * (1.0 + pre * (1.0 - s))


def dot_nt(a, b):
    return lax.dot_general(a, b, (((1,), (1,)), ((), ())), preferred_element_type=F32)


def call(body, outs, specs, scratch, flops, nbytes, mb, out_specs=None):
    return pl.pallas_call(
        body,
        out_shape=outs,
        in_specs=specs,
        out_specs=out_specs if out_specs is not None else [VM] * len(outs),
        scratch_shapes=scratch,
        compiler_params=pltpu.CompilerParams(vmem_limit_bytes=mb << 20),
        cost_estimate=pl.CostEstimate(flops=int(flops), bytes_accessed=int(nbytes), transcendentals=0),
    )


def fine_body(scale, own, below, above, left, right, table, kernel, cot, out, part, feats, grads):
    depth, rows, cols = own.shape
    ch = table.shape[0] // 8
    place, count = lax.axis_index("space"), lax.axis_size("space")
    lane, lanes = lax.axis_index("chan"), lax.axis_size("chan")
    key = lax.broadcasted_iota(jnp.int32, (128, cols), 0)
    for x in range(depth + 2):
        for y in range(rows + 2):
            if y == 0:
                ids = left[x]
                ids = jnp.where(lane == 0, 1024, ids)
            elif y == rows + 1:
                ids = right[x]
                ids = jnp.where(lane == lanes - 1, 1024, ids)
            elif x == 0:
                ids = below[0, y - 1 : y]
            elif x == depth + 1:
                ids = above[0, y - 1 : y]
            else:
                ids = own[x - 1, y - 1 : y]
            if x == 0:
                ids = jnp.where(place == 0, 1024, ids)
            if x == depth + 1:
                ids = jnp.where(place == count - 1, 1024, ids)
            low = (ids & 127) | ((ids >> 3) & 128)
            hot = (key == low).astype(F32).astype(BF16)
            picked = jnp.dot(table[...], hot, preferred_element_type=F32)
            for bit in (9, 8, 7):
                half = picked.shape[0] // 2
                picked = jnp.where(((ids >> bit) & 1) == 1, picked[half:], picked[:half])
            at = (x * (rows + 2) + y) * ch
            feats[at : at + ch, :] = picked.astype(BF16)
    group = ch * rows
    step = (rows + 2) * ch
    w = lax.broadcasted_iota(jnp.int32, (1, cols), 1)
    first, last = w == 0, w == cols - 1
    for x in range(depth):
        window = feats[x * step : (x + 3) * step, :]
        q = jnp.dot(kernel[...], window, preferred_element_type=F32)
        pre = q[group : 2 * group]
        pre = pre + jnp.where(first, 0.0, pltpu.roll(q[:group], 1, 1))
        pre = pre + jnp.where(last, 0.0, pltpu.roll(q[2 * group :], cols - 1, 1))
        act, slope = silu_parts(pre)
        out[:, x] = act.reshape(ch, rows, cols).astype(BF16)
        delta = cot[:, x].astype(F32).reshape(group, cols) * slope
        shifted = jnp.concatenate(
            [
                jnp.where(last, 0.0, pltpu.roll(delta, cols - 1, 1)).astype(BF16),
                delta.astype(BF16),
                jnp.where(first, 0.0, pltpu.roll(delta, 1, 1)).astype(BF16),
            ],
            axis=0,
        )
        term = dot_nt(shifted, window)
        grads[...] = term if x == 0 else grads[...] + term
    total = grads[...]
    wide = total.shape[1]
    y_out = lax.broadcasted_iota(jnp.int32, total.shape, 0) % rows
    y_in = (lax.broadcasted_iota(jnp.int32, total.shape, 1) % step) // ch
    fold_from = lax.broadcasted_iota(jnp.int32, (wide, 3 * ch), 0)
    fold_to = lax.broadcasted_iota(jnp.int32, (wide, 3 * ch), 1)
    fold = ((fold_from // step == fold_to // ch) & (fold_from % ch == fold_to % ch)).astype(F32).astype(BF16)
    for b in range(3):
        kept = jnp.where(y_in - y_out == b, total, 0.0)
        kept = kept.reshape(3 * ch, rows, wide).sum(axis=1)
        high = kept.astype(BF16)
        rest = kept - high.astype(F32)
        middle = rest.astype(BF16)
        lowest = (rest - middle.astype(F32)).astype(BF16)
        folded = jnp.dot(high, fold, preferred_element_type=F32)
        folded = folded + jnp.dot(middle, fold, preferred_element_type=F32)
        folded = folded + jnp.dot(lowest, fold, preferred_element_type=F32)
        part[b] = folded * scale


def fine_call(scale, own, below, above, left, right, table, kernel, cot):
    depth, rows, cols = own.shape
    ch = table.shape[0] // 8
    body = functools.partial(fine_body, scale)
    macs = 3 * ch * rows * 3 * ch * (rows + 2) * cols * depth * 2
    return call(
        body,
        [
            jax.ShapeDtypeStruct((ch, depth, rows, cols), BF16),
            jax.ShapeDtypeStruct((3, 3 * ch, 3 * ch), F32),
        ],
        [VM] * 8,
        [
            pltpu.VMEM(((depth + 2) * (rows + 2) * ch, cols), BF16),
            pltpu.VMEM((3 * ch * rows, 3 * ch * (rows + 2)), F32),
        ],
        2 * macs,
        4 << 20,
        24,
    )(own, below, above, left, right, table, kernel, cot)


def shift_masks(width, sign):
    lane = lax.broadcasted_iota(jnp.int32, (1, width), 1)
    y, w = lane // BW, lane % BW
    masks = []
    for b in (-1, 0, 1):
        for e in (-1, 0, 1):
            yy, ww = y + sign * b, w + sign * e
            masks.append((yy >= 0) & (yy < width // BW) & (ww >= 0) & (ww < BW))
    return masks


def bott_body(pieces, *refs):
    weight, cots = refs[0], refs[1]
    ins = refs[2 : 2 + pieces]
    own_out, delta_out, full, share, mine, padded, deltas, rows_t, sums = refs[2 + pieces :]
    slabs, cb, lanes = ins[0].shape
    planes = own_out.shape[1]
    width = lanes // planes
    c_all = cb * pieces
    o_own = own_out.shape[0]
    total = slabs * planes
    place = lax.axis_index("space")
    chan = lax.axis_index("chan")
    padded[:, :width] = jnp.zeros((c_all, width), BF16)
    padded[:, (total + 1) * width :] = jnp.zeros((c_all, width), BF16)
    for j in range(pieces):
        row = pl.multiple_of((chan ^ j) * cb, cb)
        for r in range(slabs):
            slab = lax.rem(place - r + slabs, slabs)
            at = pl.multiple_of(slab * lanes + width, width)
            padded[pl.ds(row, cb), pl.ds(at, lanes)] = ins[j][r]
    full[...] = padded[:, width : (total + 1) * width]
    deltas[:, :width] = jnp.zeros((o_own, width), F32)
    deltas[:, (total + 1) * width :] = jnp.zeros((o_own, width), F32)
    masks = shift_masks(width, 1)
    for n in range(slabs):
        base = n * lanes
        for a in range(3):
            win = padded[:, base + a * width : base + a * width + lanes]
            term = jnp.dot(weight[a * 9 * o_own : (a + 1) * 9 * o_own, :], win, preferred_element_type=F32)
            sums[...] = term if a == 0 else sums[...] + term
        cot = cots[lax.rem(place - n + slabs, slabs)].astype(F32)
        for p in range(planes):
            pre = jnp.zeros((o_own, width), F32)
            for k, (b, e) in enumerate([(b, e) for b in (-1, 0, 1) for e in (-1, 0, 1)]):
                block = sums[k * o_own : (k + 1) * o_own, p * width : (p + 1) * width]
                turn = -(b * BW + e) % width
                if turn:
                    block = jnp.where(masks[k], pltpu.roll(block, turn, 1), 0.0)
                pre = pre + block
            act, slope = silu_parts(pre)

            @pl.when(n == place)
            def _():
                own_out[:, p, :] = act.astype(BF16)

            delta = (cot[:, p * width : (p + 1) * width] * slope).astype(BF16).astype(F32)
            at = base + (p + 1) * width
            deltas[:, at : at + width] = delta
    delta_out[...] = deltas[:, width : (total + 1) * width]
    near = (planes + 2) * width
    turned = deltas[:, pl.ds(pl.multiple_of(place * lanes, width), near)].T
    w = lax.broadcasted_iota(jnp.int32, (near, 1), 0) % BW
    gap = width + 2 * BW
    for e in (-1, 0, 1):
        moved = turned
        if e:
            moved = jnp.where((w - e >= 0) & (w - e < BW), pltpu.roll(turned, e % near, 0), 0.0)
        moved = moved.astype(BF16)
        for p in range(planes + 2):
            rows_t[e + 1, p * gap : p * gap + BW, :] = jnp.zeros((BW, o_own), BF16)
            rows_t[e + 1, p * gap + BW : p * gap + BW + width, :] = moved[p * width : (p + 1) * width]
            rows_t[e + 1, p * gap + BW + width : (p + 1) * gap, :] = jnp.zeros((BW, o_own), BF16)
    blocks = []
    for a in (-1, 0, 1):
        for b in (-1, 0, 1):
            for e in (-1, 0, 1):
                per_plane = []
                for p in range(planes):
                    start = (1 + p - a) * gap + BW - b * BW
                    per_plane.append(rows_t[e + 1, start : start + width, :])
                blocks.append(jnp.concatenate(per_plane, axis=0))
    left = jnp.concatenate(blocks, axis=1)
    back = jnp.dot(left, weight[...], preferred_element_type=F32)
    for j in range(pieces):
        block = back[:, j * cb : (j + 1) * cb]
        to = lax.rem(j - chan + pieces, pieces)
        share[to] = block.astype(BF16)

        @pl.when(chan == j)
        def _():
            mine[...] = block


def bott_call(weight, cots, ins, planes):
    slabs, cb, lanes = ins[0].shape
    pieces = len(ins)
    o_own = cots.shape[1]
    c_all = pieces * cb
    width = lanes // planes
    total = slabs * planes
    S = jax.ShapeDtypeStruct
    macs = 27 * o_own * c_all * (total + planes) * width
    return call(
        functools.partial(bott_body, pieces),
        [
            S((o_own, planes, width), BF16),
            S((o_own, total * width), F32),
            S((c_all, total * width), BF16),
            S((pieces, lanes, cb), BF16),
            S((lanes, cb), F32),
        ],
        [VM] * (2 + pieces),
        [
            pltpu.VMEM((c_all, (total + 2) * width), BF16),
            pltpu.VMEM((o_own, (total + 2) * width), F32),
            pltpu.VMEM((3, (planes + 2) * (width + 2 * BW), o_own), BF16),
            pltpu.VMEM((9 * o_own, lanes), F32),
        ],
        2 * macs,
        8 << 20,
        32,
    )(weight, cots, *ins)


def wgrad_body(scale, delta, full, out, shifted, stage, sems):
    o_own, length = delta.shape
    c_all = full.shape[0]
    width = 4 * BW
    total = length // width
    masks = shift_masks(width, -1)
    shifted[:, :width] = jnp.zeros((9 * o_own, width), BF16)
    shifted[:, (total + 1) * width :] = jnp.zeros((9 * o_own, width), BF16)
    for p in range(total):
        block = delta[:, p * width : (p + 1) * width]
        for k, (b, e) in enumerate([(b, e) for b in (-1, 0, 1) for e in (-1, 0, 1)]):
            turn = (b * BW + e) % width
            moved = jnp.where(masks[k], pltpu.roll(block, turn, 1), 0.0) if turn else block
            shifted[k * o_own : (k + 1) * o_own, (p + 1) * width : (p + 2) * width] = moved.astype(BF16)
    chunk = stage.shape[3]
    copies = []
    for n in range(c_all // chunk):
        slot = n % 2
        if n >= 2:
            copies[n - 2].wait()
        right = full[n * chunk : (n + 1) * chunk, :]
        for a in range(3):
            left = shifted[:, (2 - a) * width : (2 - a) * width + length]
            term = dot_nt(left, right) * scale
            for k in range(9):
                stage[slot, :, a * 9 + k, :] = term[k * o_own : (k + 1) * o_own, :]
        copy = pltpu.make_async_copy(stage.at[slot], out.at[:, :, pl.ds(n * chunk, chunk)], sems.at[slot])
        copy.start()
        copies.append(copy)
    for copy in copies[-2:]:
        copy.wait()


def wgrad_call(scale, delta, full, chunk=256):
    o_own, length = delta.shape
    c_all = full.shape[0]
    width = 4 * BW
    total = length // width
    return call(
        functools.partial(wgrad_body, scale),
        [jax.ShapeDtypeStruct((o_own, 27, c_all), F32)],
        [VM] * 2,
        [
            pltpu.VMEM((9 * o_own, (total + 2) * width), BF16),
            pltpu.VMEM((2, o_own, 27, chunk), F32),
            pltpu.SemaphoreType.DMA((2,)),
        ],
        2 * 27 * o_own * c_all * length,
        8 << 20,
        40,
        [HB],
    )(delta, full)[0]


def last_body(count, *refs):
    mine, others, out = refs[0], refs[1 : 1 + count], refs[1 + count]
    total = mine[...]
    for other in others:
        total = total + other[...].astype(F32)
    turned = total.T
    planes = out.shape[1]
    width = turned.shape[1] // planes
    for p in range(planes):
        out[:, p, :] = turned[:, p * width : (p + 1) * width].astype(BF16)


def last_call(mine, others, planes):
    lanes, cb = mine.shape
    return call(
        functools.partial(last_body, len(others)),
        [jax.ShapeDtypeStruct((cb, planes, lanes // planes), BF16)],
        [VM] * (1 + len(others)),
        [],
        lanes * cb * 4,
        lanes * cb * 12,
        16,
    )(mine, *others)[0]


def hop(x, axis, offset):
    count = lax.axis_size(axis)
    return lax.ppermute(x, axis, [(i, (i + offset) % count) for i in range(count)])


def swap(x, axis, bit):
    count = lax.axis_size(axis)
    return lax.ppermute(x, axis, [(i, i ^ bit) for i in range(count)])


def shards(labels, table, fine_weight, fine_cot, bott_in, bott_weight, bott_cot):
    depth, rows, cols = labels.shape
    ch = fine_weight.shape[2]
    spaces, chans = lax.axis_size("space"), lax.axis_size("chan")
    cb, planes, width = bott_in.shape
    lanes = planes * width
    o_own = bott_cot.shape[0]

    below = hop(labels[-1:], "space", 1)
    above = hop(labels[:1], "space", spaces - 1)
    slab = bott_in.reshape(cb, lanes)
    slabs = jnp.stack([slab] + [hop(slab, "space", r) for r in range(1, spaces)])
    framed = jnp.concatenate([below, labels, above], axis=0)
    left = hop(framed[:, -1:], "chan", 1)
    right = hop(framed[:, :1], "chan", chans - 1)
    pieces = {0: slabs}
    bits = [1 << i for i in range(chans.bit_length() - 1)]
    for bit in bits[1:] + bits[:1]:
        pieces.update({j ^ bit: swap(x, "chan", bit) for j, x in list(pieces.items())})
    ins = [pieces[j] for j in range(chans)]
    cot = bott_cot.reshape(o_own, lanes)
    cots = jnp.stack([cot] + [hop(cot, "space", r) for r in range(1, spaces)])

    lookup = table.reshape(8, 128, ch).transpose(0, 2, 1).reshape(8 * ch, 128)
    taps = fine_weight.reshape(3, 3, 3, ch, ch)
    band = np.zeros((3, rows, rows + 2), np.float32)
    for b in range(3):
        for y in range(rows):
            band[b, y, y + b] = 1
    kernel = sum(
        taps[:, b].transpose(1, 3, 0, 2)[:, :, None, :, None, :] * band[b][None, None, :, None, :, None].astype(BF16)
        for b in range(3)
    ).reshape(3 * ch * rows, 3 * (rows + 2) * ch)
    scale = (depth * spaces * rows * chans * cols) ** -0.5
    fine_out, part = fine_call(scale, labels, below, above, left, right, lookup, kernel, fine_cot)
    part = part + sum(hop(part, "chan", r) for r in range(1, chans))
    part = part + sum(hop(part, "space", r) for r in range(1, spaces))
    fine_wgrad = part.reshape(3, 3, ch, 3, ch).transpose(3, 0, 1, 4, 2).reshape(27, ch, ch)

    weight = bott_weight.transpose(1, 0, 2).reshape(27 * o_own, cb * chans)
    bott_out, delta, full, share, mine = bott_call(weight, cots, ins, planes)
    others = [hop(share[r], "chan", r) for r in range(1, chans)]
    bott_wgrad = wgrad_call((planes * spaces * width) ** -0.5, delta, full)
    bott_dgrad = last_call(mine, others, planes)
    return fine_out, fine_wgrad, bott_out, bott_dgrad, bott_wgrad


def solution(mesh):
    placed = (
        P(("groups", "space"), "chan", None),
        P(),
        P(),
        P(None, ("groups", "space"), "chan", None),
        P("chan", ("groups", "space"), None),
        P("chan", None, None),
        P("chan", ("groups", "space"), None),
    )
    return jax.shard_map(
        shards,
        mesh=mesh,
        in_specs=placed,
        out_specs=(
            P(None, ("groups", "space"), "chan", None),
            P("groups", None, None),
            P("chan", ("groups", "space"), None),
            P("chan", ("groups", "space"), None),
            P(("groups", "chan"), None, None),
        ),
        check_vma=False,
    )
```

```python
import functools
import jax
import jax.numpy as jnp
import numpy as np
from jax import lax
from jax.experimental import pallas as pl
from jax.experimental.pallas import tpu as pltpu
from jax.sharding import PartitionSpec as P

BW = 32
LOW = 256
F32 = jnp.float32
BF16 = jnp.bfloat16
VM = pl.BlockSpec(memory_space=pltpu.VMEM)
HB = pl.BlockSpec(memory_space=pltpu.HBM)
STEPS = [(b, e) for b in (-1, 0, 1) for e in (-1, 0, 1)]


def silu_parts(pre):
    s = jax.nn.sigmoid(pre)
    return pre * s, s * (1.0 + pre * (1.0 - s))


def dot_nt(a, b):
    return lax.dot_general(a, b, (((1,), (1,)), ((), ())), preferred_element_type=F32)


def call(body, outs, specs, scratch, flops, nbytes, mb, out_specs=None):
    return pl.pallas_call(
        body,
        out_shape=outs,
        in_specs=specs,
        out_specs=out_specs if out_specs is not None else [VM] * len(outs),
        scratch_shapes=scratch,
        compiler_params=pltpu.CompilerParams(vmem_limit_bytes=mb << 20),
        cost_estimate=pl.CostEstimate(flops=int(flops), bytes_accessed=int(nbytes), transcendentals=0),
    )


def iota(shape, dim):
    return lax.broadcasted_iota(jnp.int32, shape, dim)


def prep_body(rows, taps, table, kernel, lookup):
    ch = table.shape[0]
    shape = kernel.shape
    step = (rows + 2) * ch
    spread = (iota((shape[0], 3 * ch), 0) // rows == iota((shape[0], 3 * ch), 1)).astype(F32).astype(BF16)
    m, n = iota((3 * ch, shape[1]), 0), iota((3 * ch, shape[1]), 1)
    repeat = ((m // ch == n // step) & (m % ch == n % ch)).astype(F32).astype(BF16)
    gap = (iota(shape, 1) % step) // ch - iota(shape, 0) % rows
    total = jnp.zeros(shape, F32)
    for b in range(3):
        tall = jnp.dot(spread, taps[b], preferred_element_type=F32).astype(BF16)
        total = jnp.where(gap == b, jnp.dot(tall, repeat, preferred_element_type=F32), total)
    kernel[...] = total.astype(BF16)
    low = lookup.shape[1]
    for high in range(table.shape[1] // low):
        lookup[high * ch : (high + 1) * ch, :] = table[:, high * low : (high + 1) * low]


def prep_call(taps, table, rows):
    ch, grains = table.shape
    return call(
        functools.partial(prep_body, rows),
        [
            jax.ShapeDtypeStruct((3 * ch * rows, 3 * (rows + 2) * ch), BF16),
            jax.ShapeDtypeStruct((grains // LOW * ch, LOW), BF16),
        ],
        [VM] * 2,
        [],
        2e9,
        1 << 20,
        16,
    )(taps, table)


def fine_body(scale, own, below, above, left, right, table, kernel, cot, out, part, feats, grads):
    depth, rows, cols = own.shape
    ch = out.shape[0]
    place, count = lax.axis_index("space"), lax.axis_size("space")
    lane, lanes = lax.axis_index("chan"), lax.axis_size("chan")
    key = iota((LOW, cols), 0).astype(F32).astype(BF16)
    one, none = jnp.ones((), BF16), jnp.zeros((), BF16)
    for x in range(depth + 2):
        for y in range(rows + 2):
            if y == 0:
                ids = left[x]
                ids = jnp.where(lane == 0, -1, ids)
            elif y == rows + 1:
                ids = right[x]
                ids = jnp.where(lane == lanes - 1, -1, ids)
            elif x == 0:
                ids = below[0, y - 1 : y]
            elif x == depth + 1:
                ids = above[0, y - 1 : y]
            else:
                ids = own[x - 1, y - 1 : y]
            if x == 0:
                ids = jnp.where(place == 0, -1, ids)
            if x == depth + 1:
                ids = jnp.where(place == count - 1, -1, ids)
            low = jnp.where(ids < 0, -1, ids & (LOW - 1))
            hot = jnp.where(key == low.astype(F32).astype(BF16), one, none)
            picked = jnp.dot(table[...], hot, preferred_element_type=F32)
            bit = 9
            while picked.shape[0] > ch:
                half = picked.shape[0] // 2
                picked = jnp.where(((ids >> bit) & 1) == 1, picked[half:], picked[:half])
                bit -= 1
            at = (x * (rows + 2) + y) * ch
            feats[at : at + ch, :] = picked.astype(BF16)
    group = ch * rows
    step = (rows + 2) * ch
    w = lax.broadcasted_iota(jnp.int32, (1, cols), 1)
    first, last = w == 0, w == cols - 1
    for x in range(depth):
        window = feats[x * step : (x + 3) * step, :]
        q = jnp.dot(kernel[...], window, preferred_element_type=F32)
        pre = q[group : 2 * group]
        pre = pre + jnp.where(first, 0.0, pltpu.roll(q[:group], 1, 1))
        pre = pre + jnp.where(last, 0.0, pltpu.roll(q[2 * group :], cols - 1, 1))
        act, slope = silu_parts(pre)
        out[:, x] = act.reshape(ch, rows, cols).astype(BF16)
        delta = cot[:, x].astype(F32).reshape(group, cols) * slope
        shifted = jnp.concatenate(
            [
                jnp.where(last, 0.0, pltpu.roll(delta, cols - 1, 1)).astype(BF16),
                delta.astype(BF16),
                jnp.where(first, 0.0, pltpu.roll(delta, 1, 1)).astype(BF16),
            ],
            axis=0,
        )
        term = dot_nt(shifted, window)
        grads[...] = term if x == 0 else grads[...] + term
    total = grads[...]
    wide = total.shape[1]
    y_out = lax.broadcasted_iota(jnp.int32, total.shape, 0) % rows
    y_in = (lax.broadcasted_iota(jnp.int32, total.shape, 1) % step) // ch
    fold_from = lax.broadcasted_iota(jnp.int32, (wide, 3 * ch), 0)
    fold_to = lax.broadcasted_iota(jnp.int32, (wide, 3 * ch), 1)
    fold = ((fold_from // step == fold_to // ch) & (fold_from % ch == fold_to % ch)).astype(F32).astype(BF16)
    for b in range(3):
        kept = jnp.where(y_in - y_out == b, total, 0.0)
        kept = kept.reshape(3 * ch, rows, wide).sum(axis=1)
        high = kept.astype(BF16)
        rest = kept - high.astype(F32)
        middle = rest.astype(BF16)
        lowest = (rest - middle.astype(F32)).astype(BF16)
        folded = jnp.dot(high, fold, preferred_element_type=F32)
        folded = folded + jnp.dot(middle, fold, preferred_element_type=F32)
        folded = folded + jnp.dot(lowest, fold, preferred_element_type=F32)
        part[b] = folded * scale


def fine_call(scale, own, below, above, left, right, table, kernel, cot):
    depth, rows, cols = own.shape
    ch = cot.shape[0]
    body = functools.partial(fine_body, scale)
    macs = 3 * ch * rows * 3 * ch * (rows + 2) * cols * depth * 2
    return call(
        body,
        [
            jax.ShapeDtypeStruct((ch, depth, rows, cols), BF16),
            jax.ShapeDtypeStruct((3, 3 * ch, 3 * ch), F32),
        ],
        [VM] * 8,
        [
            pltpu.VMEM(((depth + 2) * (rows + 2) * ch, cols), BF16),
            pltpu.VMEM((3 * ch * rows, 3 * ch * (rows + 2)), F32),
        ],
        2 * macs,
        4 << 20,
        24,
    )(own, below, above, left, right, table, kernel, cot)


def shift_masks(width, sign):
    lane = lax.broadcasted_iota(jnp.int32, (1, width), 1)
    y, w = lane // BW, lane % BW
    masks = []
    for b, e in STEPS:
        yy, ww = y + sign * b, w + sign * e
        masks.append((yy >= 0) & (yy < width // BW) & (ww >= 0) & (ww < BW))
    return masks


def bott_body(pieces, planes, *refs):
    weight, cots = refs[0], refs[1]
    ins = refs[2 : 2 + pieces]
    own_out, deltas, padded, share, mine, acts, rows_t = refs[2 + pieces :]
    slabs, cb, lanes = ins[0].shape
    width = lanes // planes
    c_all = cb * pieces
    o_own = own_out.shape[0]
    total = slabs * planes
    place = lax.axis_index("space")
    chan = lax.axis_index("chan")
    padded[:, :width] = jnp.zeros((c_all, width), BF16)
    padded[:, (total + 1) * width :] = jnp.zeros((c_all, width), BF16)
    for j in range(pieces):
        row = pl.multiple_of((chan ^ j) * cb, cb)
        for r in range(slabs):
            slab = lax.rem(place - r + slabs, slabs)
            at = pl.multiple_of(slab * lanes + width, width)
            padded[pl.ds(row, cb), pl.ds(at, lanes)] = ins[j][r]
    deltas[:, :width] = jnp.zeros((o_own, width), F32)
    deltas[:, (total + 1) * width :] = jnp.zeros((o_own, width), F32)
    masks = shift_masks(width, 1)
    for n in range(slabs):
        base = n * lanes
        pre = [jnp.zeros((o_own, width), F32) for _ in range(planes)]
        for k, (b, e) in enumerate(STEPS):
            term = jnp.zeros((o_own, lanes), F32)
            for a in range(3):
                at = (a * 9 + k) * o_own
                win = padded[:, base + a * width : base + a * width + lanes]
                term = term + jnp.dot(weight[at : at + o_own, :], win, preferred_element_type=F32)
            turn = -(b * BW + e) % width
            for p in range(planes):
                block = term[:, p * width : (p + 1) * width]
                if turn:
                    block = jnp.where(masks[k], pltpu.roll(block, turn, 1), 0.0)
                pre[p] = pre[p] + block
        cot = cots[lax.rem(place - n + slabs, slabs)].astype(F32)
        for p in range(planes):
            act, slope = silu_parts(pre[p])
            acts[n, :, p * width : (p + 1) * width] = act
            delta = (cot[:, p * width : (p + 1) * width] * slope).astype(BF16).astype(F32)
            deltas[:, base + (p + 1) * width : base + (p + 2) * width] = delta
    near = (planes + 2) * width
    turned = deltas[:, pl.ds(pl.multiple_of(place * lanes, width), near)].T
    w = lax.broadcasted_iota(jnp.int32, (near, 1), 0) % BW
    gap = width + 2 * BW
    for e in (-1, 0, 1):
        moved = turned
        if e:
            moved = jnp.where((w - e >= 0) & (w - e < BW), pltpu.roll(turned, e % near, 0), 0.0)
        moved = moved.astype(BF16)
        for p in range(planes + 2):
            rows_t[e + 1, p * gap : p * gap + BW, :] = jnp.zeros((BW, o_own), BF16)
            rows_t[e + 1, p * gap + BW : p * gap + BW + width, :] = moved[p * width : (p + 1) * width]
            rows_t[e + 1, p * gap + BW + width : (p + 1) * gap, :] = jnp.zeros((BW, o_own), BF16)
    blocks = []
    for a in (-1, 0, 1):
        for b, e in STEPS:
            starts = [(1 + p - a) * gap + BW - b * BW for p in range(planes)]
            blocks.append(jnp.concatenate([rows_t[e + 1, s : s + width, :] for s in starts], axis=0))
    back = jnp.dot(jnp.concatenate(blocks, axis=1), weight[...], preferred_element_type=F32)
    for j in range(pieces):
        block = back[:, j * cb : (j + 1) * cb]
        to = lax.rem(j - chan + pieces, pieces)
        mine[to] = block
        share[to] = block.astype(BF16)
    act = acts[place]
    for p in range(planes):
        own_out[:, p, :] = act[:, p * width : (p + 1) * width].astype(BF16)


def bott_call(weight, cots, ins, planes):
    slabs, cb, lanes = ins[0].shape
    pieces = len(ins)
    o_own = cots.shape[1]
    c_all = pieces * cb
    width = lanes // planes
    total = slabs * planes
    S = jax.ShapeDtypeStruct
    macs = 27 * o_own * c_all * (total + planes) * width
    return call(
        functools.partial(bott_body, pieces, planes),
        [
            S((o_own, planes, width), BF16),
            S((o_own, (total + 2) * width), F32),
            S((c_all, (total + 2) * width), BF16),
            S((pieces, lanes, cb), BF16),
            S((pieces, lanes, cb), F32),
        ],
        [VM] * (2 + pieces),
        [
            pltpu.VMEM((slabs, o_own, lanes), F32),
            pltpu.VMEM((3, (planes + 2) * (width + 2 * BW), o_own), BF16),
        ],
        2 * macs,
        8 << 20,
        24,
    )(weight, cots, *ins)


def wgrad_body(scale, delta, full, out, shifted, stage, sems):
    o_own, length = delta.shape[0], delta.shape[1] - 8 * BW
    width = 4 * BW
    total = length // width
    masks = shift_masks(width, -1)
    shifted[:, :width] = jnp.zeros((9 * o_own, width), BF16)
    shifted[:, (total + 1) * width :] = jnp.zeros((9 * o_own, width), BF16)
    for p in range(total):
        block = delta[:, (p + 1) * width : (p + 2) * width]
        for k, (b, e) in enumerate(STEPS):
            turn = (b * BW + e) % width
            moved = jnp.where(masks[k], pltpu.roll(block, turn, 1), 0.0) if turn else block
            shifted[k * o_own : (k + 1) * o_own, (p + 1) * width : (p + 2) * width] = moved.astype(BF16)
    copies = []
    for a in range(3):
        if a >= 2:
            copies[a - 2].wait()
        left = shifted[:, (2 - a) * width : (2 - a) * width + length]
        term = dot_nt(left, full[:, width : width + length]) * scale
        stage[a % 2] = term.reshape(stage.shape[1:])
        copy = pltpu.make_async_copy(stage.at[a % 2], out.at[a * 9 : (a + 1) * 9], sems.at[a % 2])
        copy.start()
        copies.append(copy)
    for copy in copies[1:]:
        copy.wait()


def wgrad_call(scale, delta, full):
    o_own, length = delta.shape
    c_all = full.shape[0]
    return call(
        functools.partial(wgrad_body, scale),
        [jax.ShapeDtypeStruct((27, o_own, c_all), F32)],
        [VM] * 2,
        [
            pltpu.VMEM((9 * o_own, length), BF16),
            pltpu.VMEM((2, 9, o_own, c_all), F32),
            pltpu.SemaphoreType.DMA((2,)),
        ],
        2 * 27 * o_own * c_all * length,
        8 << 20,
        32,
        [HB],
    )(delta, full)[0]


def last_body(count, *refs):
    mine, others, out = refs[0], refs[1 : 1 + count], refs[1 + count]
    total = mine[0]
    for other in others:
        total = total + other[...].astype(F32)
    turned = total.T
    planes = out.shape[1]
    width = turned.shape[1] // planes
    for p in range(planes):
        out[:, p, :] = turned[:, p * width : (p + 1) * width].astype(BF16)


def last_call(mine, others, planes):
    lanes, cb = mine.shape[1:]
    return call(
        functools.partial(last_body, len(others)),
        [jax.ShapeDtypeStruct((cb, planes, lanes // planes), BF16)],
        [VM] * (1 + len(others)),
        [],
        lanes * cb * 4,
        lanes * cb * 12,
        16,
    )(mine, *others)[0]


def hop(x, axis, offset):
    count = lax.axis_size(axis)
    return lax.ppermute(x, axis, [(i, (i + offset) % count) for i in range(count)])


def swap(x, axis, bit):
    count = lax.axis_size(axis)
    return lax.ppermute(x, axis, [(i, i ^ bit) for i in range(count)])


def shards(labels, table, fine_weight, fine_cot, bott_in, bott_weight, bott_cot):
    depth, rows, cols = labels.shape
    ch = fine_weight.shape[2]
    spaces, chans = lax.axis_size("space"), lax.axis_size("chan")
    cb, planes, width = bott_in.shape
    lanes = planes * width
    o_own = bott_cot.shape[0]

    below = hop(labels[-1:], "space", 1)
    above = hop(labels[:1], "space", spaces - 1)
    slab = bott_in.reshape(cb, lanes)
    slabs = jnp.stack([slab] + [hop(slab, "space", r) for r in range(1, spaces)])
    framed = jnp.concatenate([below, labels, above], axis=0)
    left = hop(framed[:, -1:], "chan", 1)
    right = hop(framed[:, :1], "chan", chans - 1)
    pieces = {0: slabs}
    bits = [1 << i for i in range(chans.bit_length() - 1)]
    for bit in bits[1:] + bits[:1]:
        pieces.update({j ^ bit: swap(x, "chan", bit) for j, x in list(pieces.items())})
    ins = [pieces[j] for j in range(chans)]
    cot = bott_cot.reshape(o_own, lanes)
    cots = jnp.stack([cot] + [hop(cot, "space", r) for r in range(1, spaces)])

    taps = fine_weight.reshape(3, 3, 3, ch, ch).transpose(1, 2, 4, 0, 3).reshape(3, 3 * ch, 3 * ch)
    kernel, lookup = prep_call(taps, table.T, rows)
    scale = (depth * spaces * rows * chans * cols) ** -0.5
    fine_out, part = fine_call(scale, labels, below, above, left, right, lookup, kernel, fine_cot)
    part = part + sum(hop(part, "chan", r) for r in range(1, chans))
    part = part + sum(hop(part, "space", r) for r in range(1, spaces))
    fine_wgrad = part.reshape(3, 3, ch, 3, ch).transpose(3, 0, 1, 4, 2).reshape(27, ch, ch)

    weight = bott_weight.transpose(1, 0, 2).reshape(27 * o_own, cb * chans)
    bott_out, delta, full, share, mine = bott_call(weight, cots, ins, planes)
    others = [hop(share[r], "chan", r) for r in range(1, chans)]
    bott_wgrad = wgrad_call((planes * spaces * width) ** -0.5, delta, full).transpose(1, 0, 2)
    bott_dgrad = last_call(mine, others, planes)
    return fine_out, fine_wgrad, bott_out, bott_dgrad, bott_wgrad


def solution(mesh):
    placed = (
        P(("groups", "space"), "chan", None),
        P(),
        P(),
        P(None, ("groups", "space"), "chan", None),
        P("chan", ("groups", "space"), None),
        P("chan", None, None),
        P("chan", ("groups", "space"), None),
    )
    return jax.shard_map(
        shards,
        mesh=mesh,
        in_specs=placed,
        out_specs=(
            P(None, ("groups", "space"), "chan", None),
            P("groups", None, None),
            P("chan", ("groups", "space"), None),
            P("chan", ("groups", "space"), None),
            P(("groups", "chan"), None, None),
        ),
        check_vma=False,
    )
```

```python
import functools
import jax
import jax.numpy as jnp
import numpy as np
from jax import lax
from jax.experimental import pallas as pl
from jax.experimental.pallas import tpu as pltpu
from jax.sharding import PartitionSpec as P

BW = 32
TAPS = 32
LOW = 128
F32 = jnp.float32
BF16 = jnp.bfloat16
VM = pl.BlockSpec(memory_space=pltpu.VMEM)
HB = pl.BlockSpec(memory_space=pltpu.HBM)
STEPS = [(b, e) for b in (-1, 0, 1) for e in (-1, 0, 1)]


def silu_parts(pre):
    s = jax.nn.sigmoid(pre)
    return pre * s, s * (1.0 + pre * (1.0 - s))


def dot_nt(a, b):
    return lax.dot_general(a, b, (((1,), (1,)), ((), ())), preferred_element_type=F32)


def call(body, outs, specs, scratch, flops, nbytes, mb, out_specs=None):
    return pl.pallas_call(
        body,
        out_shape=outs,
        in_specs=specs,
        out_specs=out_specs if out_specs is not None else [VM] * len(outs),
        scratch_shapes=scratch,
        compiler_params=pltpu.CompilerParams(vmem_limit_bytes=mb << 20),
        cost_estimate=pl.CostEstimate(flops=int(flops), bytes_accessed=int(nbytes), transcendentals=0),
    )


def iota(shape, dim):
    return lax.broadcasted_iota(jnp.int32, shape, dim)


def hot(condition):
    return condition.astype(F32).astype(BF16)


def pack_body(labels, cells, cots, slab, first, last, cot, ids, raw_cells, raw_cots, sems):
    copies = [
        pltpu.make_async_copy(cells, raw_cells, sems.at[0]),
        pltpu.make_async_copy(labels, ids, sems.at[1]),
        pltpu.make_async_copy(cots, raw_cots, sems.at[2]),
    ]
    for copy in copies:
        copy.start()
    cb, planes, width = cells.shape
    lanes = planes * width
    cols = labels.shape[2]
    copies[0].wait()
    for p in range(planes):
        block = raw_cells[:, p, :]
        for to in (slab, first, last):
            to[:cb, p * width : (p + 1) * width] = block
    copies[1].wait()
    for to, plane in ((first, ids[0]), (last, ids[labels.shape[0] - 1])):
        parts = [plane & 255, plane >> 8]
        rows = jnp.concatenate([part[:, i : i + lanes] for part in parts for i in range(0, cols, lanes)], axis=0)
        to[cb:, :] = rows.astype(F32).astype(BF16)
    copies[2].wait()
    for p in range(planes):
        cot[:, p * width : (p + 1) * width] = raw_cots[:, p, :]


def pack_call(labels, cells, cots):
    depth, rows, cols = labels.shape
    cb, planes, width = cells.shape
    lanes = planes * width
    more = 2 * rows * cols // lanes
    S = jax.ShapeDtypeStruct
    outs = [S((cb, lanes), BF16), S((cb + more, lanes), BF16), S((cb + more, lanes), BF16)]
    outs += [S((cb, lanes), BF16), S(labels.shape, jnp.int32)]
    scratch = [pltpu.VMEM(cells.shape, BF16), pltpu.VMEM(cots.shape, BF16), pltpu.SemaphoreType.DMA((3,))]
    return call(pack_body, outs, [HB] * 3, scratch, 1e9, 1 << 18, 56)(labels, cells, cots)


def unpack_body(count, *refs):
    labels, slab, got = refs[0], refs[1], refs[2 : 2 + count]
    slabs, below, above, top, bottom = refs[3 + count :]
    cb, lanes = slab.shape
    depth, rows, cols = labels.shape
    slabs[0] = slab[...]
    for r in range(count):
        slabs[r + 1] = got[r][:cb, :]
    planes = []
    for ref in (got[0], got[count - 1]):
        rest = ref[cb:, :].astype(F32)
        pieces = [rest[i * rows : (i + 1) * rows] for i in range(rest.shape[0] // rows)]
        half = len(pieces) // 2
        low, high = (jnp.concatenate(part, axis=1) for part in (pieces[:half], pieces[half:]))
        planes.append((low + 256.0 * high).astype(jnp.int32))
    below[...] = planes[0]
    above[...] = planes[1]
    all_planes = [planes[0]] + [labels[x] for x in range(depth)] + [planes[1]]
    top[...] = jnp.concatenate([plane[:1] for plane in all_planes], axis=0)
    bottom[...] = jnp.concatenate([plane[rows - 1 :] for plane in all_planes], axis=0)


def unpack_call(labels, slab, got, after):
    depth, rows, cols = labels.shape
    cb, lanes = slab.shape
    S = jax.ShapeDtypeStruct
    outs = [S((len(got) + 1, cb, lanes), BF16)]
    outs += [S((rows, cols), jnp.int32)] * 2 + [S((depth + 2, cols), jnp.int32)] * 2
    body = functools.partial(unpack_body, len(got))
    return call(body, outs, [VM] * (3 + len(got)), [], 2e8, 1 << 18, 12)(labels, slab, *got, after)


def prep_body(rows, taps, table, kernel, lookup):
    ch = table.shape[0]
    shape = kernel.shape
    step = (rows + 2) * ch
    spread = hot(iota((shape[0], 3 * ch), 0) // rows == iota((shape[0], 3 * ch), 1))
    m, n = iota((3 * ch, shape[1]), 0), iota((3 * ch, shape[1]), 1)
    repeat = hot((m // ch == n // step) & (m % ch == n % ch))
    gap = (iota(shape, 1) % step) // ch - iota(shape, 0) % rows
    total = jnp.zeros(shape, F32)
    for b in range(3):
        tall = jnp.dot(spread, taps[b], preferred_element_type=F32).astype(BF16)
        total = jnp.where(gap == b, jnp.dot(tall, repeat, preferred_element_type=F32), total)
    kernel[...] = total.astype(BF16)
    for high in range(table.shape[1] // LOW):
        lookup[high * ch : (high + 1) * ch, :] = table[:, high * LOW : (high + 1) * LOW]


def prep_call(taps, table, rows):
    ch, grains = table.shape
    return call(
        functools.partial(prep_body, rows),
        [
            jax.ShapeDtypeStruct((3 * ch * rows, 3 * (rows + 2) * ch), BF16),
            jax.ShapeDtypeStruct((grains // LOW * ch, LOW), BF16),
        ],
        [VM] * 2,
        [],
        1.2e9,
        1 << 18,
        16,
    )(taps, table)


def split(x):
    high = x.astype(BF16)
    return high, (x - high.astype(F32)).astype(BF16)


def fine_body(scale, own, below, above, left, right, table, kernel, cot, out, part, feats, grads):
    depth, rows, cols = own.shape
    ch = out.shape[0]
    place, count = lax.axis_index("space"), lax.axis_size("space")
    lane, lanes = lax.axis_index("chan"), lax.axis_size("chan")
    key = iota((LOW, cols), 0).astype(F32).astype(BF16)
    one, none = jnp.ones((), BF16), jnp.zeros((), BF16)
    for x in range(depth + 2):
        for y in range(rows + 2):
            if y == 0:
                ids = jnp.where(lane == 0, -1, left[x : x + 1])
            elif y == rows + 1:
                ids = jnp.where(lane == lanes - 1, -1, right[x : x + 1])
            elif x == 0:
                ids = below[y - 1 : y]
            elif x == depth + 1:
                ids = above[y - 1 : y]
            else:
                ids = own[x - 1, y - 1 : y]
            if x == 0:
                ids = jnp.where(place == 0, -1, ids)
            if x == depth + 1:
                ids = jnp.where(place == count - 1, -1, ids)
            low = jnp.where(ids < 0, -1, ids & (LOW - 1))
            match = jnp.where(key == low.astype(F32).astype(BF16), one, none)
            picked = jnp.dot(table[...], match, preferred_element_type=F32)
            bit = 9
            while picked.shape[0] > ch:
                half = picked.shape[0] // 2
                picked = jnp.where(((ids >> bit) & 1) == 1, picked[half:], picked[:half])
                bit -= 1
            at = (x * (rows + 2) + y) * ch
            feats[at : at + ch, :] = picked.astype(BF16)
    group = ch * rows
    step = (rows + 2) * ch
    w = lax.broadcasted_iota(jnp.int32, (1, cols), 1)
    first, last = w == 0, w == cols - 1
    for x in range(depth):
        window = feats[x * step : (x + 3) * step, :]
        q = jnp.dot(kernel[...], window, preferred_element_type=F32)
        pre = q[group : 2 * group]
        pre = pre + jnp.where(first, 0.0, pltpu.roll(q[:group], 1, 1))
        pre = pre + jnp.where(last, 0.0, pltpu.roll(q[2 * group :], cols - 1, 1))
        act, slope = silu_parts(pre)
        out[:, x] = act.reshape(ch, rows, cols).astype(BF16)
        delta = cot[:, x].astype(F32).reshape(group, cols) * slope
        shifted = jnp.concatenate(
            [
                jnp.where(last, 0.0, pltpu.roll(delta, cols - 1, 1)).astype(BF16),
                delta.astype(BF16),
                jnp.where(first, 0.0, pltpu.roll(delta, 1, 1)).astype(BF16),
            ],
            axis=0,
        )
        term = dot_nt(shifted, window)
        grads[...] = term if x == 0 else grads[...] + term
    total = grads[...]
    shape = total.shape
    gap = (iota(shape, 1) % step) // ch - iota(shape, 0) % rows
    gather = hot(iota((3 * ch, shape[0]), 0) == iota((3 * ch, shape[0]), 1) // rows)
    m, n = iota((shape[1], 3 * ch), 0), iota((shape[1], 3 * ch), 1)
    fold = hot((m // step == n // ch) & (m % ch == n % ch))
    high, rest = split(total)
    sums = []
    for b in range(3):
        keep = hot(gap == b)
        kept = jnp.dot(gather, high * keep, preferred_element_type=F32)
        kept = kept + jnp.dot(gather, rest * keep, preferred_element_type=F32)
        sums.append(kept)
    tall = jnp.concatenate([piece for b in range(3) for piece in split(sums[b])], axis=0)
    tall = jnp.dot(tall, fold, preferred_element_type=F32)
    m, n = iota((3 * ch, ch * TAPS), 0), iota((3 * ch, ch * TAPS), 1)
    spot = jnp.where(m % ch == n // TAPS, n % TAPS - 9 * (m // ch), -1)
    result = jnp.zeros((ch, ch * TAPS), F32)
    for b in range(3):
        block = tall[6 * b * ch : (6 * b + 3) * ch] + tall[(6 * b + 3) * ch : (6 * b + 6) * ch]
        for e in range(3):
            both = jnp.concatenate(split(block[e * ch : (e + 1) * ch]), axis=0)
            moved = jnp.dot(both, hot(spot == 3 * b + e), preferred_element_type=F32)
            result = result + (moved[:ch] + moved[ch:])
    part[...] = result * scale


def fine_call(scale, own, below, above, left, right, table, kernel, cot):
    depth, rows, cols = own.shape
    ch = cot.shape[0]
    body = functools.partial(fine_body, scale)
    return call(
        body,
        [
            jax.ShapeDtypeStruct((ch, depth, rows, cols), BF16),
            jax.ShapeDtypeStruct((ch, ch * TAPS), F32),
        ],
        [VM] * 8,
        [
            pltpu.VMEM(((depth + 2) * (rows + 2) * ch, cols), BF16),
            pltpu.VMEM((3 * ch * rows, 3 * ch * (rows + 2)), F32),
        ],
        7.4e9,
        4 << 20,
        20,
    )(own, below, above, left, right, table, kernel, cot)


def shift_masks(width, sign):
    lane = lax.broadcasted_iota(jnp.int32, (1, width), 1)
    y, w = lane // BW, lane % BW
    masks = []
    for b, e in STEPS:
        yy, ww = y + sign * b, w + sign * e
        masks.append((yy >= 0) & (yy < width // BW) & (ww >= 0) & (ww < BW))
    return masks


def bott_body(pieces, slabs, planes, *refs):
    weight, refs = refs[0], refs[1:]
    cots, refs = refs[:slabs], refs[slabs:]
    ins, refs = refs[:pieces], refs[pieces:]
    parts, refs = refs[:pieces], refs[pieces:]
    own_out, deltas, padded, share, mine, part_sum, acts, rows_t, cot_at = refs
    slabs, cb, lanes = ins[0].shape
    width = lanes // planes
    c_all = cb * pieces
    o_own = own_out.shape[0]
    total = slabs * planes
    place = lax.axis_index("space")
    chan = lax.axis_index("chan")
    part_sum[...] = sum((part[...] for part in parts[1:]), parts[0][...])
    for r in range(slabs):
        cot_at[lax.rem(place - r + slabs, slabs)] = cots[r][...]
    padded[:, :width] = jnp.zeros((c_all, width), BF16)
    padded[:, (total + 1) * width :] = jnp.zeros((c_all, width), BF16)
    for j in range(pieces):
        row = pl.multiple_of((chan ^ j) * cb, cb)
        for r in range(slabs):
            slab = lax.rem(place - r + slabs, slabs)
            at = pl.multiple_of(slab * lanes + width, width)
            padded[pl.ds(row, cb), pl.ds(at, lanes)] = ins[j][r]
    deltas[:, :width] = jnp.zeros((o_own, width), F32)
    deltas[:, (total + 1) * width :] = jnp.zeros((o_own, width), F32)
    masks = shift_masks(width, 1)
    for n in range(slabs):
        base = n * lanes
        pre = [jnp.zeros((o_own, width), F32) for _ in range(planes)]
        for k, (b, e) in enumerate(STEPS):
            term = jnp.zeros((o_own, lanes), F32)
            for a in range(3):
                at = (a * 9 + k) * o_own
                win = padded[:, base + a * width : base + a * width + lanes]
                term = term + jnp.dot(weight[at : at + o_own, :], win, preferred_element_type=F32)
            turn = -(b * BW + e) % width
            for p in range(planes):
                block = term[:, p * width : (p + 1) * width]
                if turn:
                    block = jnp.where(masks[k], pltpu.roll(block, turn, 1), 0.0)
                pre[p] = pre[p] + block
        cot = cot_at[n].astype(F32)
        for p in range(planes):
            act, slope = silu_parts(pre[p])
            acts[n, :, p * width : (p + 1) * width] = act
            delta = (cot[:, p * width : (p + 1) * width] * slope).astype(BF16).astype(F32)
            deltas[:, base + (p + 1) * width : base + (p + 2) * width] = delta
    near = (planes + 2) * width
    turned = deltas[:, pl.ds(pl.multiple_of(place * lanes, width), near)].T
    w = lax.broadcasted_iota(jnp.int32, (near, 1), 0) % BW
    gap = width + 2 * BW
    for e in (-1, 0, 1):
        moved = turned
        if e:
            moved = jnp.where((w - e >= 0) & (w - e < BW), pltpu.roll(turned, e % near, 0), 0.0)
        moved = moved.astype(BF16)
        for p in range(planes + 2):
            rows_t[e + 1, p * gap : p * gap + BW, :] = jnp.zeros((BW, o_own), BF16)
            rows_t[e + 1, p * gap + BW : p * gap + BW + width, :] = moved[p * width : (p + 1) * width]
            rows_t[e + 1, p * gap + BW + width : (p + 1) * gap, :] = jnp.zeros((BW, o_own), BF16)
    blocks = []
    for a in (-1, 0, 1):
        for b, e in STEPS:
            starts = [(1 + p - a) * gap + BW - b * BW for p in range(planes)]
            blocks.append(jnp.concatenate([rows_t[e + 1, s : s + width, :] for s in starts], axis=0))
    back = jnp.dot(jnp.concatenate(blocks, axis=1), weight[...], preferred_element_type=F32)
    for j in range(pieces):
        block = back[:, j * cb : (j + 1) * cb]
        to = lax.rem(j - chan + pieces, pieces)
        mine[to] = block
        share[to] = block.astype(BF16)
    act = acts[place]
    for p in range(planes):
        own_out[:, p, :] = act[:, p * width : (p + 1) * width].astype(BF16)


def bott_call(weight, cots, ins, parts, planes):
    slabs, cb, lanes = ins[0].shape
    pieces = len(ins)
    o_own = cots[0].shape[0]
    c_all = pieces * cb
    width = lanes // planes
    total = slabs * planes
    S = jax.ShapeDtypeStruct
    return call(
        functools.partial(bott_body, pieces, slabs, planes),
        [
            S((o_own, planes, width), BF16),
            S((o_own, (total + 2) * width), F32),
            S((c_all, (total + 2) * width), BF16),
            S((pieces, lanes, cb), BF16),
            S((pieces, lanes, cb), F32),
            S(parts[0].shape, F32),
        ],
        [VM] * (1 + slabs + 2 * pieces),
        [
            pltpu.VMEM((slabs, o_own, lanes), F32),
            pltpu.VMEM((3, (planes + 2) * (width + 2 * BW), o_own), BF16),
            pltpu.VMEM((slabs, o_own, lanes), BF16),
        ],
        6.6e9,
        8 << 20,
        24,
    )(weight, *cots, *ins, *parts)


def wgrad_body(scale, delta, full, out, shifted, stage, sems):
    o_own, length = delta.shape[0], delta.shape[1] - 8 * BW
    width = 4 * BW
    total = length // width
    masks = shift_masks(width, -1)
    shifted[:, :width] = jnp.zeros((9 * o_own, width), BF16)
    shifted[:, (total + 1) * width :] = jnp.zeros((9 * o_own, width), BF16)
    for p in range(total):
        block = delta[:, (p + 1) * width : (p + 2) * width]
        for k, (b, e) in enumerate(STEPS):
            turn = (b * BW + e) % width
            moved = jnp.where(masks[k], pltpu.roll(block, turn, 1), 0.0) if turn else block
            shifted[k * o_own : (k + 1) * o_own, (p + 1) * width : (p + 2) * width] = moved.astype(BF16)
    copies = []
    for a in range(3):
        if a >= 2:
            copies[a - 2].wait()
        left = shifted[:, (2 - a) * width : (2 - a) * width + length]
        term = dot_nt(left, full[:, width : width + length]) * scale
        stage[a % 2] = term.reshape(stage.shape[1:])
        copy = pltpu.make_async_copy(stage.at[a % 2], out.at[a * 9 : (a + 1) * 9], sems.at[a % 2])
        copy.start()
        copies.append(copy)
    for copy in copies[1:]:
        copy.wait()


def wgrad_call(scale, delta, full):
    o_own, length = delta.shape
    c_all = full.shape[0]
    return call(
        functools.partial(wgrad_body, scale),
        [jax.ShapeDtypeStruct((27, o_own, c_all), F32)],
        [VM] * 2,
        [
            pltpu.VMEM((9 * o_own, length), BF16),
            pltpu.VMEM((2, 9, o_own, c_all), F32),
            pltpu.SemaphoreType.DMA((2,)),
        ],
        6.6e9,
        8 << 20,
        32,
        [HB],
    )(delta, full)[0]


def last_body(count, spaces, *refs):
    mine, refs = refs[0], refs[1:]
    others, refs = refs[:count], refs[count:]
    parts, (out, taps) = refs[:spaces], refs[spaces:]
    total = mine[0]
    for other in others:
        total = total + other[...].astype(F32)
    turned = total.T
    planes = out.shape[1]
    width = turned.shape[1] // planes
    for p in range(planes):
        out[:, p, :] = turned[:, p * width : (p + 1) * width].astype(BF16)
    grad = sum((part[...] for part in parts[1:]), parts[0][...])
    for c in range(taps.shape[0]):
        taps[c] = grad[:, c * TAPS : c * TAPS + taps.shape[2]]


def last_call(mine, others, parts, planes):
    lanes, cb = mine.shape[1:]
    ch = parts[0].shape[0]
    return call(
        functools.partial(last_body, len(others), len(parts)),
        [
            jax.ShapeDtypeStruct((cb, planes, lanes // planes), BF16),
            jax.ShapeDtypeStruct((ch, ch, 27), F32),
        ],
        [VM] * (1 + len(others) + len(parts)),
        [],
        lanes * cb * 4,
        lanes * cb * 12,
        12,
    )(mine, *others, *parts)


def hop(x, axis, offset):
    count = lax.axis_size(axis)
    return lax.ppermute(x, axis, [(i, (i + offset) % count) for i in range(count)])


def swap(x, axis, bit):
    count = lax.axis_size(axis)
    return lax.ppermute(x, axis, [(i, i ^ bit) for i in range(count)])


def shards(labels, table, fine_weight, fine_cot, bott_in, bott_weight, bott_cot):
    depth, rows, cols = labels.shape
    ch = fine_weight.shape[2]
    spaces, chans = lax.axis_size("space"), lax.axis_size("chan")
    cb, planes, width = bott_in.shape
    lanes = planes * width
    o_own = bott_cot.shape[0]

    slab, first, last, cot, ids = pack_call(labels, bott_in, bott_cot)
    taps = fine_weight.reshape(3, 3, 3, ch, ch).transpose(1, 2, 4, 0, 3).reshape(3, 3 * ch, 3 * ch)
    kernel, lookup = prep_call(taps, table.T, rows)
    sends = [last] + [slab] * (spaces - 3) + [first]
    got = [hop(x, "space", r + 1) for r, x in enumerate(sends)]
    slabs, below, above, top, bottom = unpack_call(ids, slab, got, kernel)
    left = hop(bottom, "chan", 1)
    right = hop(top, "chan", chans - 1)
    pieces = {0: slabs}
    bits = [1 << i for i in range(chans.bit_length() - 1)]
    for bit in bits[1:] + bits[:1]:
        pieces.update({j ^ bit: swap(x, "chan", bit) for j, x in list(pieces.items())})
    ins = [pieces[j] for j in range(chans)]
    cots = [cot] + [hop(cot, "space", r) for r in range(1, spaces)]

    weight = bott_weight.transpose(1, 0, 2).reshape(27 * o_own, cb * chans)
    scale = (depth * spaces * rows * chans * cols) ** -0.5
    fine_out, part = fine_call(scale, ids, below, above, left, right, lookup, kernel, fine_cot)
    parts = [part] + [hop(part, "chan", r) for r in range(1, chans)]

    bott_out, delta, full, share, mine, part = bott_call(weight, cots, ins, parts, planes)
    others = [hop(share[r], "chan", r) for r in range(1, chans)]
    parts = [part] + [hop(part, "space", r) for r in range(1, spaces)]
    bott_wgrad = wgrad_call((planes * spaces * width) ** -0.5, delta, full).transpose(1, 0, 2)
    bott_dgrad, fine_wgrad = last_call(mine, others, parts, planes)
    return fine_out, fine_wgrad.transpose(2, 0, 1), bott_out, bott_dgrad, bott_wgrad


def solution(mesh):
    placed = (
        P(("groups", "space"), "chan", None),
        P(),
        P(),
        P(None, ("groups", "space"), "chan", None),
        P("chan", ("groups", "space"), None),
        P("chan", None, None),
        P("chan", ("groups", "space"), None),
    )
    return jax.shard_map(
        shards,
        mesh=mesh,
        in_specs=placed,
        out_specs=(
            P(None, ("groups", "space"), "chan", None),
            P("groups", None, None),
            P("chan", ("groups", "space"), None),
            P("chan", ("groups", "space"), None),
            P(("groups", "chan"), None, None),
        ),
        check_vma=False,
    )
```

```python
import functools
import jax
import jax.numpy as jnp
import numpy as np
from jax import lax
from jax.experimental import pallas as pl
from jax.experimental.pallas import tpu as pltpu
from jax.sharding import PartitionSpec as P

BW = 32
TAPS = 32
LOW = 128
F32 = jnp.float32
BF16 = jnp.bfloat16
VM = pl.BlockSpec(memory_space=pltpu.VMEM)
HB = pl.BlockSpec(memory_space=pltpu.HBM)
STEPS = [(b, e) for b in (-1, 0, 1) for e in (-1, 0, 1)]


def silu_parts(pre):
    s = jax.nn.sigmoid(pre)
    return pre * s, s * (1.0 + pre * (1.0 - s))


def dot_nt(a, b):
    return lax.dot_general(a, b, (((1,), (1,)), ((), ())), preferred_element_type=F32)


def call(body, outs, specs, scratch, flops, nbytes, mb, out_specs=None):
    return pl.pallas_call(
        body,
        out_shape=outs,
        in_specs=specs,
        out_specs=out_specs if out_specs is not None else [VM] * len(outs),
        scratch_shapes=scratch,
        compiler_params=pltpu.CompilerParams(vmem_limit_bytes=mb << 20),
        cost_estimate=pl.CostEstimate(flops=int(flops), bytes_accessed=int(nbytes), transcendentals=0),
    )


def iota(shape, dim):
    return lax.broadcasted_iota(jnp.int32, shape, dim)


def hot(condition):
    return condition.astype(F32).astype(BF16)


def pick_rows(rows, count, which, turned=False):
    shape = (rows * count, rows) if turned else (rows, rows * count)
    far, near = (0, 1) if turned else (1, 0)
    return hot(iota(shape, far) == count * iota(shape, near) + which)


def apart(x, planes):
    rows = x.shape[0] // planes
    parts = [jnp.dot(pick_rows(rows, planes, p), x, preferred_element_type=F32) for p in range(planes)]
    return jnp.concatenate(parts, axis=1).astype(BF16)


def together(x, planes):
    width = x.shape[1] // planes
    x = x.astype(BF16)
    parts = [
        jnp.dot(pick_rows(x.shape[0], planes, p, True), x[:, p * width : (p + 1) * width], preferred_element_type=F32)
        for p in range(planes)
    ]
    return sum(parts[1:], parts[0]).astype(BF16)


def pack_body(planes, labels, cells, slab, first, last, ids, raw_cells, sems):
    copies = [
        pltpu.make_async_copy(cells, raw_cells, sems.at[0]),
        pltpu.make_async_copy(labels, ids, sems.at[1]),
    ]
    for copy in copies:
        copy.start()
    cb, lanes = slab.shape
    cols = labels.shape[2]
    copies[0].wait()
    block = apart(raw_cells[...], planes)
    for to in (slab, first, last):
        to[:cb, :] = block
    copies[1].wait()
    for to, plane in ((first, ids[0]), (last, ids[labels.shape[0] - 1])):
        parts = [plane & 255, plane >> 8]
        rows = jnp.concatenate([part[:, i : i + lanes] for part in parts for i in range(0, cols, lanes)], axis=0)
        to[cb:, :] = rows.astype(F32).astype(BF16)


def pack_call(labels, cells, planes):
    depth, rows, cols = labels.shape
    cb, lanes = cells.shape[0] // planes, cells.shape[1] * planes
    more = 2 * rows * cols // lanes
    S = jax.ShapeDtypeStruct
    outs = [S((cb, lanes), BF16), S((cb + more, lanes), BF16), S((cb + more, lanes), BF16)]
    outs += [S(labels.shape, jnp.int32)]
    scratch = [pltpu.VMEM(cells.shape, BF16), pltpu.SemaphoreType.DMA((2,))]
    return call(functools.partial(pack_body, planes), outs, [HB] * 2, scratch, 1e9, 1 << 18, 56)(labels, cells)


def unpack_body(count, *refs):
    labels, slab, got = refs[0], refs[1], refs[2 : 2 + count]
    slabs, below, above, top, bottom = refs[3 + count :]
    cb, lanes = slab.shape
    depth, rows, cols = labels.shape
    slabs[0] = slab[...]
    for r in range(count):
        slabs[r + 1] = got[r][:cb, :]
    planes = []
    for ref in (got[0], got[count - 1]):
        rest = ref[cb:, :].astype(F32)
        pieces = [rest[i * rows : (i + 1) * rows] for i in range(rest.shape[0] // rows)]
        half = len(pieces) // 2
        low, high = (jnp.concatenate(part, axis=1) for part in (pieces[:half], pieces[half:]))
        planes.append((low + 256.0 * high).astype(jnp.int32))
    below[...] = planes[0]
    above[...] = planes[1]
    all_planes = [planes[0]] + [labels[x] for x in range(depth)] + [planes[1]]
    top[...] = jnp.concatenate([plane[:1] for plane in all_planes], axis=0)
    bottom[...] = jnp.concatenate([plane[rows - 1 :] for plane in all_planes], axis=0)


def unpack_call(labels, slab, got, after):
    depth, rows, cols = labels.shape
    cb, lanes = slab.shape
    S = jax.ShapeDtypeStruct
    outs = [S((len(got) + 1, cb, lanes), BF16)]
    outs += [S((rows, cols), jnp.int32)] * 2 + [S((depth + 2, cols), jnp.int32)] * 2
    body = functools.partial(unpack_body, len(got))
    return call(body, outs, [VM] * (3 + len(got)), [], 2e8, 1 << 18, 12)(labels, slab, *got, after)


def prep_body(rows, taps, table, kernel, lookup):
    ch = table.shape[0]
    shape = kernel.shape
    step = (rows + 2) * ch
    spread = hot(iota((shape[0], 3 * ch), 0) // rows == iota((shape[0], 3 * ch), 1))
    m, n = iota((3 * ch, shape[1]), 0), iota((3 * ch, shape[1]), 1)
    repeat = hot((m // ch == n // step) & (m % ch == n % ch))
    gap = (iota(shape, 1) % step) // ch - iota(shape, 0) % rows
    total = jnp.zeros(shape, F32)
    for b in range(3):
        tall = jnp.dot(spread, taps[b], preferred_element_type=F32).astype(BF16)
        total = jnp.where(gap == b, jnp.dot(tall, repeat, preferred_element_type=F32), total)
    kernel[...] = total.astype(BF16)
    for high in range(table.shape[1] // LOW):
        lookup[high * ch : (high + 1) * ch, :] = table[:, high * LOW : (high + 1) * LOW]


def prep_call(taps, table, rows):
    ch, grains = table.shape
    return call(
        functools.partial(prep_body, rows),
        [
            jax.ShapeDtypeStruct((3 * ch * rows, 3 * (rows + 2) * ch), BF16),
            jax.ShapeDtypeStruct((grains // LOW * ch, LOW), BF16),
        ],
        [VM] * 2,
        [],
        1.2e9,
        1 << 18,
        16,
    )(taps, table)


def split(x):
    high = x.astype(BF16)
    return high, (x - high.astype(F32)).astype(BF16)


def fold_lanes(blocks, lanes):
    return jnp.concatenate([b[:, i : i + lanes] for b in blocks for i in range(0, b.shape[1], lanes)], axis=0)


def unfold_lanes(x, rows, wide):
    count = wide // x.shape[1]
    cut = [x[i * rows : (i + 1) * rows].astype(F32) for i in range(2 * count)]
    return jnp.concatenate(cut[:count], axis=1) + jnp.concatenate(cut[count:], axis=1)


def fine_body(scale, planes, own, below, above, left, right, table, kernel, cot, bott_cot, out, part, message, feats, grads):
    depth, rows, cols = own.shape
    ch = out.shape[0]
    place, count = lax.axis_index("space"), lax.axis_size("space")
    lane, lanes = lax.axis_index("chan"), lax.axis_size("chan")
    key = iota((LOW, cols), 0).astype(F32).astype(BF16)
    one, none = jnp.ones((), BF16), jnp.zeros((), BF16)
    def find(x):
        for y in range(rows + 2):
            if y == 0:
                ids = jnp.where(lane == 0, -1, left[x : x + 1])
            elif y == rows + 1:
                ids = jnp.where(lane == lanes - 1, -1, right[x : x + 1])
            elif x == 0:
                ids = below[y - 1 : y]
            elif x == depth + 1:
                ids = above[y - 1 : y]
            else:
                ids = own[x - 1, y - 1 : y]
            if x == 0:
                ids = jnp.where(place == 0, -1, ids)
            if x == depth + 1:
                ids = jnp.where(place == count - 1, -1, ids)
            low = jnp.where(ids < 0, -1, ids & (LOW - 1))
            match = jnp.where(key == low.astype(F32).astype(BF16), one, none)
            picked = jnp.dot(table[...], match, preferred_element_type=F32)
            bit = 9
            while picked.shape[0] > ch:
                half = picked.shape[0] // 2
                picked = jnp.where(((ids >> bit) & 1) == 1, picked[half:], picked[:half])
                bit -= 1
            at = (x * (rows + 2) + y) * ch
            feats[at : at + ch, :] = picked.astype(BF16)

    group = ch * rows
    step = (rows + 2) * ch
    w = lax.broadcasted_iota(jnp.int32, (1, cols), 1)
    first, last = w == 0, w == cols - 1
    for x in range(depth):
        if x == 0:
            find(0)
            find(1)
        find(x + 2)
        window = feats[x * step : (x + 3) * step, :]
        q = jnp.dot(kernel[...], window, preferred_element_type=F32)
        pre = q[group : 2 * group]
        pre = pre + jnp.where(first, 0.0, pltpu.roll(q[:group], 1, 1))
        pre = pre + jnp.where(last, 0.0, pltpu.roll(q[2 * group :], cols - 1, 1))
        act, slope = silu_parts(pre)
        out[:, x] = act.reshape(ch, rows, cols).astype(BF16)
        delta = cot[:, x].astype(F32).reshape(group, cols) * slope
        shifted = jnp.concatenate(
            [
                jnp.where(last, 0.0, pltpu.roll(delta, cols - 1, 1)).astype(BF16),
                delta.astype(BF16),
                jnp.where(first, 0.0, pltpu.roll(delta, 1, 1)).astype(BF16),
            ],
            axis=0,
        )
        term = dot_nt(shifted, window)
        grads[...] = term if x == 0 else grads[...] + term
    total = grads[...]
    shape = total.shape
    gap = (iota(shape, 1) % step) // ch - iota(shape, 0) % rows
    gather = hot(iota((3 * ch, shape[0]), 0) == iota((3 * ch, shape[0]), 1) // rows)
    m, n = iota((shape[1], 3 * ch), 0), iota((shape[1], 3 * ch), 1)
    fold = hot((m // step == n // ch) & (m % ch == n % ch))
    high, rest = split(total)
    sums = []
    for b in range(3):
        keep = hot(gap == b)
        kept = jnp.dot(gather, high * keep, preferred_element_type=F32)
        kept = kept + jnp.dot(gather, rest * keep, preferred_element_type=F32)
        sums.append(kept)
    tall = jnp.concatenate([piece for b in range(3) for piece in split(sums[b])], axis=0)
    tall = jnp.dot(tall, fold, preferred_element_type=F32)
    m, n = iota((3 * ch, ch * TAPS), 0), iota((3 * ch, ch * TAPS), 1)
    spot = jnp.where(m % ch == n // TAPS, n % TAPS - 9 * (m // ch), -1)
    result = jnp.zeros((ch, ch * TAPS), F32)
    for b in range(3):
        block = tall[6 * b * ch : (6 * b + 3) * ch] + tall[(6 * b + 3) * ch : (6 * b + 6) * ch]
        for e in range(3):
            both = jnp.concatenate(split(block[e * ch : (e + 1) * ch]), axis=0)
            moved = jnp.dot(both, hot(spot == 3 * b + e), preferred_element_type=F32)
            result = result + (moved[:ch] + moved[ch:])
    result = result * scale
    part[...] = result
    o_own = bott_cot.shape[0] // planes
    message[:o_own, :] = apart(bott_cot[...], planes)
    message[o_own:, :] = fold_lanes(split(result), message.shape[1])


def fine_call(scale, own, below, above, left, right, table, kernel, cot, bott_cot, planes):
    depth, rows, cols = own.shape
    ch = cot.shape[0]
    o_own, lanes = bott_cot.shape[0] // planes, bott_cot.shape[1] * planes
    body = functools.partial(fine_body, scale, planes)
    return call(
        body,
        [
            jax.ShapeDtypeStruct((ch, depth, rows, cols), BF16),
            jax.ShapeDtypeStruct((ch, ch * TAPS), F32),
            jax.ShapeDtypeStruct((o_own + 2 * ch * ch * TAPS // lanes, lanes), BF16),
        ],
        [VM] * 9,
        [
            pltpu.VMEM(((depth + 2) * (rows + 2) * ch, cols), BF16),
            pltpu.VMEM((3 * ch * rows, 3 * ch * (rows + 2)), F32),
        ],
        7.4e9,
        4 << 20,
        20,
    )(own, below, above, left, right, table, kernel, cot, bott_cot)


def shift_masks(width, sign):
    lane = lax.broadcasted_iota(jnp.int32, (1, width), 1)
    y, w = lane // BW, lane % BW
    masks = []
    for b, e in STEPS:
        yy, ww = y + sign * b, w + sign * e
        masks.append((yy >= 0) & (yy < width // BW) & (ww >= 0) & (ww < BW))
    return masks


def bott_body(pieces, planes, *refs):
    weight, ins, (pre_out, padded) = refs[0], refs[1 : 1 + pieces], refs[1 + pieces :]
    slabs, cb, lanes = ins[0].shape
    width = lanes // planes
    c_all = cb * pieces
    o_own = pre_out.shape[0]
    total = slabs * planes
    place = lax.axis_index("space")
    chan = lax.axis_index("chan")
    padded[:, :width] = jnp.zeros((c_all, width), BF16)
    padded[:, (total + 1) * width :] = jnp.zeros((c_all, width), BF16)
    for j in range(pieces):
        row = pl.multiple_of((chan ^ j) * cb, cb)
        for r in range(slabs):
            slab = lax.rem(place - r + slabs, slabs)
            at = pl.multiple_of(slab * lanes + width, width)
            padded[pl.ds(row, cb), pl.ds(at, lanes)] = ins[j][r]
    masks = shift_masks(width, 1)
    for n in range(slabs):
        base = n * lanes
        pre = [jnp.zeros((o_own, width), F32) for _ in range(planes)]
        for k, (b, e) in enumerate(STEPS):
            term = jnp.zeros((o_own, lanes), F32)
            for a in range(3):
                at = (a * 9 + k) * o_own
                win = padded[:, base + a * width : base + a * width + lanes]
                term = term + jnp.dot(weight[at : at + o_own, :], win, preferred_element_type=F32)
            turn = -(b * BW + e) % width
            for p in range(planes):
                block = term[:, p * width : (p + 1) * width]
                if turn:
                    block = jnp.where(masks[k], pltpu.roll(block, turn, 1), 0.0)
                pre[p] = pre[p] + block
        for p in range(planes):
            pre_out[:, base + p * width : base + (p + 1) * width] = pre[p]


def bott_call(weight, ins, planes):
    slabs, cb, lanes = ins[0].shape
    pieces = len(ins)
    o_own = weight.shape[0] // 27
    S = jax.ShapeDtypeStruct
    return call(
        functools.partial(bott_body, pieces, planes),
        [S((o_own, slabs * lanes), F32), S((pieces * cb, (slabs + 1) * lanes), BF16)],
        [VM] * (1 + pieces),
        [],
        5e9,
        1 << 20,
        16,
    )(weight, *ins)


def back_body(slabs, planes, weight, pre, part, *refs):
    messages, (own_out, deltas, share, mine, part_sum, rows_t) = refs[:slabs], refs[slabs:]
    pieces, lanes, cb = mine.shape
    o_own = deltas.shape[0]
    width = lanes // planes
    total = slabs * planes
    place = lax.axis_index("space")
    chan = lax.axis_index("chan")
    deltas[:, :width] = jnp.zeros((o_own, width), F32)
    deltas[:, (total + 1) * width :] = jnp.zeros((o_own, width), F32)
    for r in range(slabs):
        at = pl.multiple_of(lax.rem(place - r + slabs, slabs) * lanes, lanes)
        act, slope = silu_parts(pre[:, pl.ds(at, lanes)])
        delta = (messages[r][:o_own, :].astype(F32) * slope).astype(BF16).astype(F32)
        deltas[:, pl.ds(pl.multiple_of(at + width, width), lanes)] = delta
        if r == 0:
            own_out[...] = together(act, planes)
    near = (planes + 2) * width
    turned = deltas[:, pl.ds(pl.multiple_of(place * lanes, width), near)].T
    w = iota((near, 1), 0) % BW
    gap = width + 2 * BW
    for e in (-1, 0, 1):
        moved = turned
        if e:
            moved = jnp.where((w - e >= 0) & (w - e < BW), pltpu.roll(turned, e % near, 0), 0.0)
        moved = moved.astype(BF16)
        for p in range(planes + 2):
            rows_t[e + 1, p * gap : p * gap + BW, :] = jnp.zeros((BW, o_own), BF16)
            rows_t[e + 1, p * gap + BW : p * gap + BW + width, :] = moved[p * width : (p + 1) * width]
            rows_t[e + 1, p * gap + BW + width : (p + 1) * gap, :] = jnp.zeros((BW, o_own), BF16)
    blocks = []
    for a in (-1, 0, 1):
        for b, e in STEPS:
            starts = [(1 + p - a) * gap + BW - b * BW for p in range(planes)]
            blocks.append(jnp.concatenate([rows_t[e + 1, s : s + width, :] for s in starts], axis=0))
    back = jnp.dot(jnp.concatenate(blocks, axis=1), weight[...], preferred_element_type=F32)
    grad = part[...]
    for r in range(1, slabs):
        grad = grad + unfold_lanes(messages[r][o_own:, :], *grad.shape)
    part_sum[...] = grad
    rest = fold_lanes(split(grad), cb)
    for j in range(pieces):
        block = back[:, j * cb : (j + 1) * cb]
        to = lax.rem(j - chan + pieces, pieces)
        mine[to] = block
        share[to, :lanes, :] = block.astype(BF16)
        share[j, lanes:, :] = rest


def back_call(weight, pre, part, messages, pieces, planes):
    slabs = len(messages)
    o_own, length = pre.shape
    lanes = length // slabs
    width = lanes // planes
    cb = weight.shape[1] // pieces
    S = jax.ShapeDtypeStruct
    return call(
        functools.partial(back_body, slabs, planes),
        [
            S((o_own * planes, width), BF16),
            S((o_own, length + 2 * width), F32),
            S((pieces, lanes + 2 * part.size // cb, cb), BF16),
            S((pieces, lanes, cb), F32),
            S(part.shape, F32),
        ],
        [VM] * (3 + slabs),
        [pltpu.VMEM((3, (planes + 2) * (width + 2 * BW), o_own), BF16)],
        2.3e9,
        1 << 20,
        16,
    )(weight, pre, part, *messages)


PLAN = ((0, 0, 4), (0, 4, 9), (1, 0, 9), (2, 0, 5), (2, 5, 9))


def wgrad_body(scale, delta, full, out, shifted, stage, sems):
    o_own, length = delta.shape[0], delta.shape[1] - 8 * BW
    width = 4 * BW
    total = length // width
    masks = shift_masks(width, -1)
    shifted[:, :width] = jnp.zeros((9 * o_own, width), BF16)
    shifted[:, (total + 1) * width :] = jnp.zeros((9 * o_own, width), BF16)

    def build(some):
        for k in some:
            b, e = STEPS[k]
            turn = (b * BW + e) % width
            for p in range(total):
                moved = delta[:, (p + 1) * width : (p + 2) * width]
                if turn:
                    moved = jnp.where(masks[k], pltpu.roll(moved, turn, 1), 0.0)
                shifted[k * o_own : (k + 1) * o_own, (p + 1) * width : (p + 2) * width] = moved.astype(BF16)

    busy = [[], []]
    built = 0
    right = full[:, width : width + length]
    for a, low, high in PLAN:
        build(range(built, max(built, high)))
        built = max(built, high)
        if low == 0:
            for copy in busy[a % 2]:
                copy.wait()
            busy[a % 2] = []
        left = shifted[low * o_own : high * o_own, (2 - a) * width : (2 - a) * width + length]
        term = dot_nt(left, right) * scale
        stage[a % 2, low:high] = term.reshape((high - low,) + stage.shape[2:])
        to = out.at[a * 9 + low : a * 9 + high]
        copy = pltpu.make_async_copy(stage.at[a % 2, low:high], to, sems.at[a % 2, low])
        copy.start()
        busy[a % 2].append(copy)
    for copies in busy:
        for copy in copies:
            copy.wait()


def wgrad_call(scale, delta, full):
    o_own, length = delta.shape
    c_all = full.shape[0]
    return call(
        functools.partial(wgrad_body, scale),
        [jax.ShapeDtypeStruct((27, o_own, c_all), F32)],
        [VM] * 2,
        [
            pltpu.VMEM((9 * o_own, length), BF16),
            pltpu.VMEM((2, 9, o_own, c_all), F32),
            pltpu.SemaphoreType.DMA((2, 9)),
        ],
        6.6e9,
        8 << 20,
        32,
        [HB],
    )(delta, full)[0]


def last_body(count, mine, part, *refs):
    others, (out, taps) = refs[:count], refs[count:]
    lanes = mine.shape[1]
    total = mine[0]
    grad = part[...]
    for other in others:
        total = total + other[:lanes, :].astype(F32)
        grad = grad + unfold_lanes(other[lanes:, :], *grad.shape)
    out[...] = together(total.T, out.shape[0] // total.shape[1])
    for c in range(taps.shape[0]):
        taps[c] = grad[:, c * TAPS : c * TAPS + taps.shape[2]]


def last_call(mine, part, others, planes):
    lanes, cb = mine.shape[1:]
    ch = part.shape[0]
    return call(
        functools.partial(last_body, len(others)),
        [
            jax.ShapeDtypeStruct((cb * planes, lanes // planes), BF16),
            jax.ShapeDtypeStruct((ch, ch, 27), F32),
        ],
        [VM] * (2 + len(others)),
        [],
        1e9,
        1 << 18,
        12,
    )(mine, part, *others)


def hop(x, axis, offset):
    count = lax.axis_size(axis)
    return lax.ppermute(x, axis, [(i, (i + offset) % count) for i in range(count)])


def swap(x, axis, bit):
    count = lax.axis_size(axis)
    return lax.ppermute(x, axis, [(i, i ^ bit) for i in range(count)])


def shards(labels, table, fine_weight, fine_cot, bott_in, bott_weight, bott_cot):
    depth, rows, cols = labels.shape
    ch = fine_weight.shape[2]
    spaces, chans = lax.axis_size("space"), lax.axis_size("chan")
    cb, planes, width = bott_in.shape
    lanes = planes * width
    o_own = bott_cot.shape[0]

    slab, first, last, ids = pack_call(labels, bott_in.reshape(cb * planes, width), planes)
    taps = fine_weight.reshape(3, 3, 3, ch, ch).transpose(1, 2, 4, 0, 3).reshape(3, 3 * ch, 3 * ch)
    kernel, lookup = prep_call(taps, table.T, rows)
    sends = [last] + [slab] * (spaces - 3) + [first]
    got = [hop(x, "space", r + 1) for r, x in enumerate(sends)]
    slabs, below, above, top, bottom = unpack_call(ids, slab, got, kernel)
    left = hop(bottom, "chan", 1)
    right = hop(top, "chan", chans - 1)
    scale = (depth * spaces * rows * chans * cols) ** -0.5
    cot = bott_cot.reshape(o_own * planes, width)
    fine_out, part, message = fine_call(
        scale, ids, below, above, left, right, lookup, kernel, fine_cot, cot, planes
    )
    messages = [message] + [hop(message, "space", r) for r in range(1, spaces)]
    pieces = {0: slabs}
    bits = [1 << i for i in range(chans.bit_length() - 1)]
    for bit in bits[1:] + bits[:1]:
        for j, x in list(pieces.items()):
            if bit == 1 and j:
                x, part = lax.optimization_barrier((x, part))
            pieces[j ^ bit] = swap(x, "chan", bit)
    ins = [pieces[j] for j in range(chans)]

    weight = bott_weight.transpose(1, 0, 2).reshape(27 * o_own, cb * chans)
    pre, full = bott_call(weight, ins, planes)
    bott_out, delta, share, mine, part = back_call(weight, pre, part, messages, chans, planes)
    others = [hop(share[r], "chan", r) for r in range(1, chans)]
    bott_wgrad = wgrad_call((planes * spaces * width) ** -0.5, delta, full).transpose(1, 0, 2)
    bott_dgrad, fine_wgrad = last_call(mine, part, others, planes)
    fine_wgrad = fine_wgrad.transpose(2, 0, 1)
    return fine_out, fine_wgrad, bott_out.reshape(bott_cot.shape), bott_dgrad.reshape(bott_in.shape), bott_wgrad


def solution(mesh):
    placed = (
        P(("groups", "space"), "chan", None),
        P(),
        P(),
        P(None, ("groups", "space"), "chan", None),
        P("chan", ("groups", "space"), None),
        P("chan", None, None),
        P("chan", ("groups", "space"), None),
    )
    return jax.shard_map(
        shards,
        mesh=mesh,
        in_specs=placed,
        out_specs=(
            P(None, ("groups", "space"), "chan", None),
            P("groups", None, None),
            P("chan", ("groups", "space"), None),
            P("chan", ("groups", "space"), None),
            P(("groups", "chan"), None, None),
        ),
        check_vma=False,
    )
```

```python
import functools
import jax
import jax.numpy as jnp
import numpy as np
from jax import lax
from jax.experimental import pallas as pl
from jax.experimental.pallas import tpu as pltpu
from jax.sharding import PartitionSpec as P

BW = 32
TAPS = 32
LOW = 128
F32 = jnp.float32
BF16 = jnp.bfloat16
VM = pl.BlockSpec(memory_space=pltpu.VMEM)
HB = pl.BlockSpec(memory_space=pltpu.HBM)
STEPS = [(b, e) for b in (-1, 0, 1) for e in (-1, 0, 1)]


def silu_parts(pre):
    s = jax.nn.sigmoid(pre)
    return pre * s, s * (1.0 + pre * (1.0 - s))


def dot_nt(a, b):
    return lax.dot_general(a, b, (((1,), (1,)), ((), ())), preferred_element_type=F32)


def call(body, outs, specs, scratch, flops, nbytes, mb, out_specs=None):
    return pl.pallas_call(
        body,
        out_shape=outs,
        in_specs=specs,
        out_specs=out_specs if out_specs is not None else [VM] * len(outs),
        scratch_shapes=scratch,
        compiler_params=pltpu.CompilerParams(vmem_limit_bytes=mb << 20),
        cost_estimate=pl.CostEstimate(flops=int(flops), bytes_accessed=int(nbytes), transcendentals=0),
    )


def iota(shape, dim):
    return lax.broadcasted_iota(jnp.int32, shape, dim)


def hot(condition):
    return condition.astype(F32).astype(BF16)


def pick_rows(rows, count, which, turned=False):
    shape = (rows * count, rows) if turned else (rows, rows * count)
    far, near = (0, 1) if turned else (1, 0)
    return hot(iota(shape, far) == count * iota(shape, near) + which)


def apart(x, planes):
    rows = x.shape[0] // planes
    parts = [jnp.dot(pick_rows(rows, planes, p), x, preferred_element_type=F32) for p in range(planes)]
    return jnp.concatenate(parts, axis=1).astype(BF16)


def together(x, planes):
    width = x.shape[1] // planes
    x = x.astype(BF16)
    parts = [
        jnp.dot(pick_rows(x.shape[0], planes, p, True), x[:, p * width : (p + 1) * width], preferred_element_type=F32)
        for p in range(planes)
    ]
    return sum(parts[1:], parts[0]).astype(BF16)


def pack_body(planes, labels, cells, cots, table, slab, first, last, cot, ids, near_table, raw_cells, raw_cots, sems):
    copies = [
        pltpu.make_async_copy(cells, raw_cells, sems.at[0]),
        pltpu.make_async_copy(labels, ids, sems.at[1]),
        pltpu.make_async_copy(cots, raw_cots, sems.at[2]),
        pltpu.make_async_copy(table, near_table, sems.at[3]),
    ]
    for copy in copies:
        copy.start()
    cb, lanes = slab.shape
    cols = labels.shape[2]
    copies[0].wait()
    block = apart(raw_cells[...], planes)
    for to in (slab, first, last):
        to[:cb, :] = block
    copies[1].wait()
    for to, plane in ((first, ids[0]), (last, ids[labels.shape[0] - 1])):
        parts = [plane & 255, plane >> 8]
        rows = jnp.concatenate([part[:, i : i + lanes] for part in parts for i in range(0, cols, lanes)], axis=0)
        to[cb:, :] = rows.astype(F32).astype(BF16)
    copies[2].wait()
    cot[...] = apart(raw_cots[...], planes)
    copies[3].wait()


def pack_call(labels, cells, cots, table, planes):
    depth, rows, cols = labels.shape
    cb, lanes = cells.shape[0] // planes, cells.shape[1] * planes
    more = 2 * rows * cols // lanes
    S = jax.ShapeDtypeStruct
    outs = [S((cb, lanes), BF16), S((cb + more, lanes), BF16), S((cb + more, lanes), BF16)]
    outs += [S((cots.shape[0] // planes, lanes), BF16), S(labels.shape, jnp.int32), S(table.shape, BF16)]
    scratch = [pltpu.VMEM(cells.shape, BF16), pltpu.VMEM(cots.shape, BF16), pltpu.SemaphoreType.DMA((4,))]
    body = functools.partial(pack_body, planes)
    args = [pltpu.with_memory_space_constraint(x, pltpu.HBM) for x in (labels, cells, cots, table)]
    return call(body, outs, [HB] * 4, scratch, 1e9, 1 << 18, 8)(*args)


def unpack_body(count, *refs):
    labels, slab, got = refs[0], refs[1], refs[2 : 2 + count]
    slabs, below, above, top, bottom = refs[3 + count :]
    cb, lanes = slab.shape
    depth, rows, cols = labels.shape
    slabs[0] = slab[...]
    for r in range(count):
        slabs[r + 1] = got[r][:cb, :]
    planes = []
    for ref in (got[0], got[count - 1]):
        rest = ref[cb:, :].astype(F32)
        pieces = [rest[i * rows : (i + 1) * rows] for i in range(rest.shape[0] // rows)]
        half = len(pieces) // 2
        low, high = (jnp.concatenate(part, axis=1) for part in (pieces[:half], pieces[half:]))
        planes.append((low + 256.0 * high).astype(jnp.int32))
    below[...] = planes[0]
    above[...] = planes[1]
    all_planes = [planes[0]] + [labels[x] for x in range(depth)] + [planes[1]]
    top[...] = jnp.concatenate([plane[:1] for plane in all_planes], axis=0)
    bottom[...] = jnp.concatenate([plane[rows - 1 :] for plane in all_planes], axis=0)


def unpack_call(labels, slab, got, after):
    depth, rows, cols = labels.shape
    cb, lanes = slab.shape
    S = jax.ShapeDtypeStruct
    outs = [S((len(got) + 1, cb, lanes), BF16)]
    outs += [S((rows, cols), jnp.int32)] * 2 + [S((depth + 2, cols), jnp.int32)] * 2
    body = functools.partial(unpack_body, len(got))
    return call(body, outs, [VM] * (3 + len(got)), [], 2e8, 1 << 18, 12)(labels, slab, *got, after)


def find(lookup, ids, ch):
    low = jnp.where(ids < 0, -1, ids & (LOW - 1)).astype(F32).astype(BF16)
    key = iota((LOW, ids.shape[1]), 0).astype(F32).astype(BF16)
    match = jnp.where(key == low, jnp.ones((), BF16), jnp.zeros((), BF16))
    picked = jnp.dot(lookup[...], match, preferred_element_type=F32)
    bit = 9
    while picked.shape[0] > ch:
        half = picked.shape[0] // 2
        picked = jnp.where(((ids >> bit) & 1) == 1, picked[half:], picked[:half])
        bit -= 1
    return picked.astype(BF16)


def prep_body(taps, table, ids, kernel, lookup, feats):
    ch = table.shape[0]
    depth, rows, cols = ids.shape
    shape = kernel.shape
    step = (rows + 2) * ch
    spread = hot(iota((shape[0], 3 * ch), 0) // rows == iota((shape[0], 3 * ch), 1))
    m, n = iota((3 * ch, shape[1]), 0), iota((3 * ch, shape[1]), 1)
    repeat = hot((m // ch == n // step) & (m % ch == n % ch))
    gap = (iota(shape, 1) % step) // ch - iota(shape, 0) % rows
    total = jnp.zeros(shape, F32)
    for b in range(3):
        tall = jnp.dot(spread, taps[b], preferred_element_type=F32).astype(BF16)
        total = jnp.where(gap == b, jnp.dot(tall, repeat, preferred_element_type=F32), total)
    kernel[...] = total.astype(BF16)
    for high in range(table.shape[1] // LOW):
        lookup[high * ch : (high + 1) * ch, :] = table[:, high * LOW : (high + 1) * LOW]
    for x in range(depth):
        for y in range(rows):
            at = (x * rows + y) * ch
            feats[at : at + ch, :] = find(lookup, ids[x, y : y + 1], ch)


def prep_call(taps, table, ids):
    ch, grains = table.shape
    depth, rows, cols = ids.shape
    return call(
        prep_body,
        [
            jax.ShapeDtypeStruct((3 * ch * rows, 3 * (rows + 2) * ch), BF16),
            jax.ShapeDtypeStruct((grains // LOW * ch, LOW), BF16),
            jax.ShapeDtypeStruct((depth * rows * ch, cols), BF16),
        ],
        [VM] * 3,
        [],
        2.5e9,
        1 << 18,
        16,
    )(taps, table, ids)


def split(x):
    high = x.astype(BF16)
    return high, (x - high.astype(F32)).astype(BF16)


def fold_lanes(blocks, lanes):
    return jnp.concatenate([b[:, i : i + lanes] for b in blocks for i in range(0, b.shape[1], lanes)], axis=0)


def unfold_lanes(x, rows, wide):
    count = wide // x.shape[1]
    cut = [x[i * rows : (i + 1) * rows].astype(F32) for i in range(x.shape[0] // rows)]
    wides = [jnp.concatenate(cut[i : i + count], axis=1) for i in range(0, len(cut), count)]
    return sum(wides[1:], wides[0])


def fine_body(scale, known, below, above, left, right, table, kernel, cot, bott_cot, after, *refs):
    out, part, message, feats, grads, stage, sems = refs
    ch, depth, rows, cols = out.shape
    place, count = lax.axis_index("space"), lax.axis_size("space")
    lane, lanes = lax.axis_index("chan"), lax.axis_size("chan")

    def fill(x):
        outer = ((0, left, lane == 0), (rows + 1, right, lane == lanes - 1))
        ids = [(y, jnp.where(off, -1, ref[x : x + 1])) for y, ref, off in outer]
        if 0 < x <= depth:
            at = (x * (rows + 2) + 1) * ch
            feats[at : at + rows * ch, :] = known[(x - 1) * rows * ch : x * rows * ch, :]
        else:
            ref, off = (below, place == 0) if x == 0 else (above, place == count - 1)
            ids = ids + [(y + 1, ref[y : y + 1]) for y in range(rows)]
            ids = [(y, jnp.where(off, -1, row)) for y, row in ids]
        for y, row in ids:
            at = (x * (rows + 2) + y) * ch
            feats[at : at + ch, :] = find(table, row, ch)

    group = ch * rows
    step = (rows + 2) * ch
    w = lax.broadcasted_iota(jnp.int32, (1, cols), 1)
    first, last = w == 0, w == cols - 1
    for x in range(depth):
        if x == 0:
            fill(0)
            fill(1)
        fill(x + 2)
        window = feats[x * step : (x + 3) * step, :]
        q = jnp.dot(kernel[...], window, preferred_element_type=F32)
        pre = q[group : 2 * group]
        pre = pre + jnp.where(first, 0.0, pltpu.roll(q[:group], 1, 1))
        pre = pre + jnp.where(last, 0.0, pltpu.roll(q[2 * group :], cols - 1, 1))
        act, slope = silu_parts(pre)
        stage[:, x] = act.reshape(ch, rows, cols).astype(BF16)
        pltpu.make_async_copy(stage.at[:, x], out.at[:, x], sems.at[x]).start()
        delta = cot[:, x].astype(F32).reshape(group, cols) * slope
        shifted = jnp.concatenate(
            [
                jnp.where(last, 0.0, pltpu.roll(delta, cols - 1, 1)).astype(BF16),
                delta.astype(BF16),
                jnp.where(first, 0.0, pltpu.roll(delta, 1, 1)).astype(BF16),
            ],
            axis=0,
        )
        term = dot_nt(shifted, window)
        grads[...] = term if x == 0 else grads[...] + term
    total = grads[...]
    shape = total.shape
    gap = (iota(shape, 1) % step) // ch - iota(shape, 0) % rows
    gather = hot(iota((3 * ch, shape[0]), 0) == iota((3 * ch, shape[0]), 1) // rows)
    m, n = iota((shape[1], 3 * ch), 0), iota((shape[1], 3 * ch), 1)
    fold = hot((m // step == n // ch) & (m % ch == n % ch))
    high, rest = split(total)
    sums = []
    for b in range(3):
        keep = hot(gap == b)
        kept = jnp.dot(gather, high * keep, preferred_element_type=F32)
        kept = kept + jnp.dot(gather, rest * keep, preferred_element_type=F32)
        sums.append(kept)
    tall = jnp.concatenate([piece for b in range(3) for piece in split(sums[b])], axis=0)
    tall = jnp.dot(tall, fold, preferred_element_type=F32)
    m, n = iota((3 * ch, ch * TAPS), 0), iota((3 * ch, ch * TAPS), 1)
    spot = jnp.where(m % ch == n // TAPS, n % TAPS - 9 * (m // ch), -1)
    result = jnp.zeros((ch, ch * TAPS), F32)
    for b in range(3):
        block = tall[6 * b * ch : (6 * b + 3) * ch] + tall[(6 * b + 3) * ch : (6 * b + 6) * ch]
        for e in range(3):
            both = jnp.concatenate(split(block[e * ch : (e + 1) * ch]), axis=0)
            moved = jnp.dot(both, hot(spot == 3 * b + e), preferred_element_type=F32)
            result = result + (moved[:ch] + moved[ch:])
    result = result * scale
    part[...] = result
    o_own, wide = bott_cot.shape
    message[:o_own, :] = bott_cot[...]
    message[o_own:, :] = fold_lanes([result.astype(BF16)], wide)
    for x in range(depth):
        pltpu.make_async_copy(stage.at[:, x], out.at[:, x], sems.at[x]).wait()


def fine_call(scale, known, below, above, left, right, table, kernel, cot, bott_cot, after):
    ch, depth, rows, cols = cot.shape
    o_own, lanes = bott_cot.shape
    more = ch * ch * TAPS // lanes
    S = jax.ShapeDtypeStruct
    return call(
        functools.partial(fine_body, scale),
        [
            S((ch, depth, rows, cols), BF16),
            S((ch, ch * TAPS), F32),
            S((o_own + more, lanes), BF16),
        ],
        [VM] * 10,
        [
            pltpu.VMEM(((depth + 2) * (rows + 2) * ch, cols), BF16),
            pltpu.VMEM((3 * ch * rows, 3 * ch * (rows + 2)), F32),
            pltpu.VMEM((ch, depth, rows, cols), BF16),
            pltpu.SemaphoreType.DMA((depth,)),
        ],
        6e9,
        4 << 20,
        20,
        [HB, VM, VM],
    )(known, below, above, left, right, table, kernel, cot, bott_cot, after)


def shift_masks(width, sign):
    lane = lax.broadcasted_iota(jnp.int32, (1, width), 1)
    y, w = lane // BW, lane % BW
    masks = []
    for b, e in STEPS:
        yy, ww = y + sign * b, w + sign * e
        masks.append((yy >= 0) & (yy < width // BW) & (ww >= 0) & (ww < BW))
    return masks


def bott_body(pieces, planes, *refs):
    weight, ins, (pre_out, padded) = refs[0], refs[1 : 1 + pieces], refs[1 + pieces :]
    slabs, cb, lanes = ins[0].shape
    width = lanes // planes
    c_all = cb * pieces
    o_own = pre_out.shape[0]
    total = slabs * planes
    place = lax.axis_index("space")
    chan = lax.axis_index("chan")
    padded[:, :width] = jnp.zeros((c_all, width), BF16)
    padded[:, (total + 1) * width :] = jnp.zeros((c_all, width), BF16)
    for j in range(pieces):
        row = pl.multiple_of((chan ^ j) * cb, cb)
        for r in range(slabs):
            slab = lax.rem(place - r + slabs, slabs)
            at = pl.multiple_of(slab * lanes + width, width)
            padded[pl.ds(row, cb), pl.ds(at, lanes)] = ins[j][r]
    masks = shift_masks(width, 1)
    for n in range(slabs):
        base = n * lanes
        pre = [jnp.zeros((o_own, width), F32) for _ in range(planes)]
        for k, (b, e) in enumerate(STEPS):
            term = jnp.zeros((o_own, lanes), F32)
            for a in range(3):
                at = (a * 9 + k) * o_own
                win = padded[:, base + a * width : base + a * width + lanes]
                term = term + jnp.dot(weight[at : at + o_own, :], win, preferred_element_type=F32)
            turn = -(b * BW + e) % width
            for p in range(planes):
                block = term[:, p * width : (p + 1) * width]
                if turn:
                    block = jnp.where(masks[k], pltpu.roll(block, turn, 1), 0.0)
                pre[p] = pre[p] + block
        for p in range(planes):
            pre_out[:, base + p * width : base + (p + 1) * width] = pre[p]


def bott_call(weight, ins, planes):
    slabs, cb, lanes = ins[0].shape
    pieces = len(ins)
    o_own = weight.shape[0] // 27
    S = jax.ShapeDtypeStruct
    return call(
        functools.partial(bott_body, pieces, planes),
        [S((o_own, slabs * lanes), F32), S((pieces * cb, (slabs + 1) * lanes), BF16)],
        [VM] * (1 + pieces),
        [],
        5e9,
        1 << 20,
        16,
    )(weight, *ins)


def back_body(slabs, planes, weight, pre, part, *refs):
    cots, refs = refs[:slabs], refs[slabs:]
    own_out, deltas, share, mine, part_sum, rows_t, stage, sem = refs
    send = pltpu.make_async_copy(stage, own_out, sem)
    pieces, lanes, cb = mine.shape
    o_own = deltas.shape[0]
    width = lanes // planes
    total = slabs * planes
    place = lax.axis_index("space")
    chan = lax.axis_index("chan")
    deltas[:, :width] = jnp.zeros((o_own, width), F32)
    deltas[:, (total + 1) * width :] = jnp.zeros((o_own, width), F32)
    for r in range(slabs):
        at = pl.multiple_of(lax.rem(place - r + slabs, slabs) * lanes, lanes)
        act, slope = silu_parts(pre[:, pl.ds(at, lanes)])
        delta = (cots[r][:o_own, :].astype(F32) * slope).astype(BF16).astype(F32)
        deltas[:, pl.ds(pl.multiple_of(at + width, width), lanes)] = delta
        if r == 0:
            stage[...] = together(act, planes)
            send.start()
    near = (planes + 2) * width
    turned = deltas[:, pl.ds(pl.multiple_of(place * lanes, width), near)].T
    w = iota((near, 1), 0) % BW
    gap = width + 2 * BW
    for e in (-1, 0, 1):
        moved = turned
        if e:
            moved = jnp.where((w - e >= 0) & (w - e < BW), pltpu.roll(turned, e % near, 0), 0.0)
        moved = moved.astype(BF16)
        for p in range(planes + 2):
            rows_t[e + 1, p * gap : p * gap + BW, :] = jnp.zeros((BW, o_own), BF16)
            rows_t[e + 1, p * gap + BW : p * gap + BW + width, :] = moved[p * width : (p + 1) * width]
            rows_t[e + 1, p * gap + BW + width : (p + 1) * gap, :] = jnp.zeros((BW, o_own), BF16)
    blocks = []
    for a in (-1, 0, 1):
        for b, e in STEPS:
            starts = [(1 + p - a) * gap + BW - b * BW for p in range(planes)]
            blocks.append(jnp.concatenate([rows_t[e + 1, s : s + width, :] for s in starts], axis=0))
    back = jnp.dot(jnp.concatenate(blocks, axis=1), weight[...], preferred_element_type=F32)
    grad = part[...]
    for r in range(1, slabs):
        grad = grad + unfold_lanes(cots[r][o_own:, :], *grad.shape)
    part_sum[...] = grad
    rest = fold_lanes([grad.astype(BF16)], cb)
    for j in range(pieces):
        block = back[:, j * cb : (j + 1) * cb]
        to = lax.rem(j - chan + pieces, pieces)
        mine[to] = block
        share[to, :lanes, :] = block.astype(BF16)
        share[j, lanes:, :] = rest
    send.wait()


def back_call(weight, pre, part, cots, pieces, planes):
    slabs = len(cots)
    o_own, length = pre.shape
    lanes = length // slabs
    width = lanes // planes
    cb = weight.shape[1] // pieces
    S = jax.ShapeDtypeStruct
    return call(
        functools.partial(back_body, slabs, planes),
        [
            S((o_own * planes, width), BF16),
            S((o_own, length + 2 * width), F32),
            S((pieces, lanes + part.size // cb, cb), BF16),
            S((pieces, lanes, cb), F32),
            S(part.shape, F32),
        ],
        [VM] * (3 + slabs),
        [
            pltpu.VMEM((3, (planes + 2) * (width + 2 * BW), o_own), BF16),
            pltpu.VMEM((o_own * planes, width), BF16),
            pltpu.SemaphoreType.DMA,
        ],
        1.8e9,
        1 << 20,
        16,
        [HB, VM, VM, VM, VM],
    )(weight, pre, part, *cots)


PLAN = ((0, 0, 4), (0, 4, 9), (1, 0, 9), (2, 0, 4), (2, 4, 7), (2, 7, 9))


def wgrad_body(scale, delta, full, out, shifted, stage, sems):
    o_own, length = delta.shape[0], delta.shape[1] - 8 * BW
    width = 4 * BW
    total = length // width
    masks = shift_masks(width, -1)
    shifted[:, :width] = jnp.zeros((9 * o_own, width), BF16)
    shifted[:, (total + 1) * width :] = jnp.zeros((9 * o_own, width), BF16)

    def build(some):
        for k in some:
            b, e = STEPS[k]
            turn = (b * BW + e) % width
            for p in range(total):
                moved = delta[:, (p + 1) * width : (p + 2) * width]
                if turn:
                    moved = jnp.where(masks[k], pltpu.roll(moved, turn, 1), 0.0)
                shifted[k * o_own : (k + 1) * o_own, (p + 1) * width : (p + 2) * width] = moved.astype(BF16)

    busy = [[], []]
    built = 0
    right = full[:, width : width + length]
    for a, low, high in PLAN:
        build(range(built, max(built, high)))
        built = max(built, high)
        if low == 0:
            for copy in busy[a % 2]:
                copy.wait()
            busy[a % 2] = []
        left = shifted[low * o_own : high * o_own, (2 - a) * width : (2 - a) * width + length]
        term = dot_nt(left, right) * scale
        stage[a % 2, low:high] = term.reshape((high - low,) + stage.shape[2:])
        to = out.at[a * 9 + low : a * 9 + high]
        copy = pltpu.make_async_copy(stage.at[a % 2, low:high], to, sems.at[a % 2, low])
        copy.start()
        busy[a % 2].append(copy)
    for copies in busy:
        for copy in copies:
            copy.wait()


def wgrad_call(scale, delta, full):
    o_own, length = delta.shape
    c_all = full.shape[0]
    return call(
        functools.partial(wgrad_body, scale),
        [jax.ShapeDtypeStruct((27, o_own, c_all), F32)],
        [VM] * 2,
        [
            pltpu.VMEM((9 * o_own, length), BF16),
            pltpu.VMEM((2, 9, o_own, c_all), F32),
            pltpu.SemaphoreType.DMA((2, 9)),
        ],
        6.6e9,
        8 << 20,
        32,
        [HB],
    )(delta, full)[0]


def last_body(count, mine, part, *refs):
    others, (out, taps) = refs[:count], refs[count:]
    lanes = mine.shape[1]
    total = mine[0]
    grad = part[...]
    for other in others:
        total = total + other[:lanes, :].astype(F32)
        grad = grad + unfold_lanes(other[lanes:, :], *grad.shape)
    out[...] = together(total.T, out.shape[0] // total.shape[1])
    for c in range(taps.shape[0]):
        taps[c] = grad[:, c * TAPS : c * TAPS + taps.shape[2]]


def last_call(mine, part, others, planes):
    lanes, cb = mine.shape[1:]
    ch = part.shape[0]
    return call(
        functools.partial(last_body, len(others)),
        [
            jax.ShapeDtypeStruct((cb * planes, lanes // planes), BF16),
            jax.ShapeDtypeStruct((ch, ch, 27), F32),
        ],
        [VM] * (2 + len(others)),
        [],
        1e9,
        1 << 18,
        12,
    )(mine, part, *others)


def hop(x, axis, offset):
    count = lax.axis_size(axis)
    return lax.ppermute(x, axis, [(i, (i + offset) % count) for i in range(count)])


def swap(x, axis, bit):
    count = lax.axis_size(axis)
    return lax.ppermute(x, axis, [(i, i ^ bit) for i in range(count)])


def shards(labels, table, fine_weight, fine_cot, bott_in, bott_weight, bott_cot):
    depth, rows, cols = labels.shape
    ch = fine_weight.shape[2]
    spaces, chans = lax.axis_size("space"), lax.axis_size("chan")
    cb, planes, width = bott_in.shape
    lanes = planes * width
    o_own = bott_cot.shape[0]

    flat_in, flat_cot = bott_in.reshape(cb * planes, width), bott_cot.reshape(o_own * planes, width)
    slab, first, last, cot, ids, near_table = pack_call(labels, flat_in, flat_cot, table.T, planes)
    taps = fine_weight.reshape(3, 3, 3, ch, ch).transpose(1, 2, 4, 0, 3).reshape(3, 3 * ch, 3 * ch)
    kernel, lookup, known = prep_call(taps, near_table, ids)
    sends = [last] + [slab] * (spaces - 3) + [first]
    got = [hop(x, "space", r + 1) for r, x in enumerate(sends)]
    slabs, below, above, top, bottom = unpack_call(ids, slab, got, kernel)
    left = hop(bottom, "chan", 1)
    right = hop(top, "chan", chans - 1)
    scale = (depth * spaces * rows * chans * cols) ** -0.5
    mate = swap(slabs, "chan", 1)
    fine_out, part, message = fine_call(
        scale, known, below, above, left, right, lookup, kernel, fine_cot, cot, mate
    )
    cots = [cot] + [hop(message, "space", r) for r in range(1, spaces)]
    pieces = {0: slabs}
    bits = [1 << i for i in range(chans.bit_length() - 1)]
    for bit in bits[1:] + bits[:1]:
        for j, x in list(pieces.items()):
            if bit == 1 and j:
                x, part = lax.optimization_barrier((x, part))
            pieces[j ^ bit] = swap(x, "chan", bit) if j ^ bit > 1 else mate
    ins = [pieces[j] for j in range(chans)]

    weight = bott_weight.transpose(1, 0, 2).reshape(27 * o_own, cb * chans)
    pre, full = bott_call(weight, ins, planes)
    bott_out, delta, share, mine, part = back_call(weight, pre, part, cots, chans, planes)
    others = [hop(share[r], "chan", r) for r in range(1, chans)]
    bott_wgrad = wgrad_call((planes * spaces * width) ** -0.5, delta, full).transpose(1, 0, 2)
    bott_dgrad, fine_wgrad = last_call(mine, part, others, planes)
    fine_wgrad = fine_wgrad.transpose(2, 0, 1)
    return fine_out, fine_wgrad, bott_out.reshape(bott_cot.shape), bott_dgrad.reshape(bott_in.shape), bott_wgrad


def solution(mesh):
    placed = (
        P(("groups", "space"), "chan", None),
        P(),
        P(),
        P(None, ("groups", "space"), "chan", None),
        P("chan", ("groups", "space"), None),
        P("chan", None, None),
        P("chan", ("groups", "space"), None),
    )
    return jax.shard_map(
        shards,
        mesh=mesh,
        in_specs=placed,
        out_specs=(
            P(None, ("groups", "space"), "chan", None),
            P("groups", None, None),
            P("chan", ("groups", "space"), None),
            P("chan", ("groups", "space"), None),
            P(("groups", "chan"), None, None),
        ),
        check_vma=False,
    )
```

```python
import functools
import jax
import jax.numpy as jnp
import numpy as np
from jax import lax
from jax.experimental import pallas as pl
from jax.experimental.pallas import tpu as pltpu
from jax.sharding import PartitionSpec as P

BW = 32
TAPS = 32
LOW = 128
F32 = jnp.float32
BF16 = jnp.bfloat16
VM = pl.BlockSpec(memory_space=pltpu.VMEM)
HB = pl.BlockSpec(memory_space=pltpu.HBM)
STEPS = [(b, e) for b in (-1, 0, 1) for e in (-1, 0, 1)]


def silu_parts(pre):
    s = jax.nn.sigmoid(pre)
    return pre * s, s * (1.0 + pre * (1.0 - s))


def dot_nt(a, b):
    return lax.dot_general(a, b, (((1,), (1,)), ((), ())), preferred_element_type=F32)


def call(body, outs, specs, scratch, flops, nbytes, mb, out_specs=None):
    return pl.pallas_call(
        body,
        out_shape=outs,
        in_specs=specs,
        out_specs=out_specs if out_specs is not None else [VM] * len(outs),
        scratch_shapes=scratch,
        compiler_params=pltpu.CompilerParams(vmem_limit_bytes=mb << 20),
        cost_estimate=pl.CostEstimate(flops=int(flops), bytes_accessed=int(nbytes), transcendentals=0),
    )


def iota(shape, dim):
    return lax.broadcasted_iota(jnp.int32, shape, dim)


def hot(condition):
    return condition.astype(F32).astype(BF16)


def pick_rows(rows, count, which, turned=False):
    shape = (rows * count, rows) if turned else (rows, rows * count)
    far, near = (0, 1) if turned else (1, 0)
    return hot(iota(shape, far) == count * iota(shape, near) + which)


def apart(x, planes):
    rows = x.shape[0] // planes
    parts = [jnp.dot(pick_rows(rows, planes, p), x, preferred_element_type=F32) for p in range(planes)]
    return jnp.concatenate(parts, axis=1).astype(BF16)


def together(x, planes):
    width = x.shape[1] // planes
    x = x.astype(BF16)
    parts = [
        jnp.dot(pick_rows(x.shape[0], planes, p, True), x[:, p * width : (p + 1) * width], preferred_element_type=F32)
        for p in range(planes)
    ]
    return sum(parts[1:], parts[0]).astype(BF16)


def pack_body(planes, labels, cells, cots, table, slab, first, last, cot, ids, near_table, raw_cells, raw_cots, sems):
    copies = [
        pltpu.make_async_copy(cells, raw_cells, sems.at[0]),
        pltpu.make_async_copy(labels, ids, sems.at[1]),
        pltpu.make_async_copy(cots, raw_cots, sems.at[2]),
        pltpu.make_async_copy(table, near_table, sems.at[3]),
    ]
    for copy in copies:
        copy.start()
    cb, lanes = slab.shape
    cols = labels.shape[2]
    copies[0].wait()
    block = apart(raw_cells[...], planes)
    for to in (slab, first, last):
        to[:cb, :] = block
    copies[1].wait()
    for to, plane in ((first, ids[0]), (last, ids[labels.shape[0] - 1])):
        parts = [plane & 255, plane >> 8]
        rows = jnp.concatenate([part[:, i : i + lanes] for part in parts for i in range(0, cols, lanes)], axis=0)
        to[cb:, :] = rows.astype(F32).astype(BF16)
    copies[2].wait()
    cot[...] = apart(raw_cots[...], planes)
    copies[3].wait()


def pack_call(labels, cells, cots, table, planes):
    depth, rows, cols = labels.shape
    cb, lanes = cells.shape[0] // planes, cells.shape[1] * planes
    more = 2 * rows * cols // lanes
    S = jax.ShapeDtypeStruct
    outs = [S((cb, lanes), BF16), S((cb + more, lanes), BF16), S((cb + more, lanes), BF16)]
    outs += [S((cots.shape[0] // planes, lanes), BF16), S(labels.shape, jnp.int32), S(table.shape, BF16)]
    scratch = [pltpu.VMEM(cells.shape, BF16), pltpu.VMEM(cots.shape, BF16), pltpu.SemaphoreType.DMA((4,))]
    body = functools.partial(pack_body, planes)
    args = [pltpu.with_memory_space_constraint(x, pltpu.HBM) for x in (labels, cells, cots, table)]
    return call(body, outs, [HB] * 4, scratch, 1e9, 1 << 18, 8)(*args)


def unpack_body(count, *refs):
    labels, slab, got = refs[0], refs[1], refs[2 : 2 + count]
    slabs, below, above, top, bottom = refs[3 + count :]
    cb, lanes = slab.shape
    depth, rows, cols = labels.shape
    slabs[0] = slab[...]
    for r in range(count):
        slabs[r + 1] = got[r][:cb, :]
    planes = []
    for ref in (got[0], got[count - 1]):
        rest = ref[cb:, :].astype(F32)
        pieces = [rest[i * rows : (i + 1) * rows] for i in range(rest.shape[0] // rows)]
        half = len(pieces) // 2
        low, high = (jnp.concatenate(part, axis=1) for part in (pieces[:half], pieces[half:]))
        planes.append((low + 256.0 * high).astype(jnp.int32))
    below[...] = planes[0]
    above[...] = planes[1]
    all_planes = [planes[0]] + [labels[x] for x in range(depth)] + [planes[1]]
    top[...] = jnp.concatenate([plane[:1] for plane in all_planes], axis=0)
    bottom[...] = jnp.concatenate([plane[rows - 1 :] for plane in all_planes], axis=0)


def unpack_call(labels, slab, got, after):
    depth, rows, cols = labels.shape
    cb, lanes = slab.shape
    S = jax.ShapeDtypeStruct
    outs = [S((len(got) + 1, cb, lanes), BF16)]
    outs += [S((rows, cols), jnp.int32)] * 2 + [S((depth + 2, cols), jnp.int32)] * 2
    body = functools.partial(unpack_body, len(got))
    return call(body, outs, [VM] * (3 + len(got)), [], 2e8, 1 << 18, 12)(labels, slab, *got, after)


def find(lookup, ids, ch):
    low = jnp.where(ids < 0, -1, ids & (LOW - 1)).astype(F32).astype(BF16)
    key = iota((LOW, ids.shape[1]), 0).astype(F32).astype(BF16)
    match = jnp.where(key == low, jnp.ones((), BF16), jnp.zeros((), BF16))
    picked = jnp.dot(lookup[...], match, preferred_element_type=F32)
    bit = 9
    while picked.shape[0] > ch:
        half = picked.shape[0] // 2
        picked = jnp.where(((ids >> bit) & 1) == 1, picked[half:], picked[:half])
        bit -= 1
    return picked.astype(BF16)


def prep_body(taps, table, ids, kernel, lookup, feats):
    ch = table.shape[0]
    depth, rows, cols = ids.shape
    shape = kernel.shape
    step = (rows + 2) * ch
    spread = hot(iota((shape[0], 3 * ch), 0) // rows == iota((shape[0], 3 * ch), 1))
    m, n = iota((3 * ch, shape[1]), 0), iota((3 * ch, shape[1]), 1)
    repeat = hot((m // ch == n // step) & (m % ch == n % ch))
    gap = (iota(shape, 1) % step) // ch - iota(shape, 0) % rows
    total = jnp.zeros(shape, F32)
    for b in range(3):
        tall = jnp.dot(spread, taps[b], preferred_element_type=F32).astype(BF16)
        total = jnp.where(gap == b, jnp.dot(tall, repeat, preferred_element_type=F32), total)
    kernel[...] = total.astype(BF16)
    for high in range(table.shape[1] // LOW):
        lookup[high * ch : (high + 1) * ch, :] = table[:, high * LOW : (high + 1) * LOW]
    for x in range(depth):
        for y in range(rows):
            at = (x * rows + y) * ch
            feats[at : at + ch, :] = find(lookup, ids[x, y : y + 1], ch)


def prep_call(taps, table, ids):
    ch, grains = table.shape
    depth, rows, cols = ids.shape
    return call(
        prep_body,
        [
            jax.ShapeDtypeStruct((3 * ch * rows, 3 * (rows + 2) * ch), BF16),
            jax.ShapeDtypeStruct((grains // LOW * ch, LOW), BF16),
            jax.ShapeDtypeStruct((depth * rows * ch, cols), BF16),
        ],
        [VM] * 3,
        [],
        2.5e9,
        1 << 18,
        16,
    )(taps, table, ids)


def split(x):
    high = x.astype(BF16)
    return high, (x - high.astype(F32)).astype(BF16)


def fold_lanes(blocks, lanes):
    return jnp.concatenate([b[:, i : i + lanes] for b in blocks for i in range(0, b.shape[1], lanes)], axis=0)


def unfold_lanes(x, rows, wide):
    count = wide // x.shape[1]
    cut = [x[i * rows : (i + 1) * rows].astype(F32) for i in range(x.shape[0] // rows)]
    wides = [jnp.concatenate(cut[i : i + count], axis=1) for i in range(0, len(cut), count)]
    return sum(wides[1:], wides[0])


def fine_body(scale, known, below, above, left, right, table, kernel, cot, bott_cot, after, *refs):
    out, part, message, feats, grads, stage, sems, pres, deltas, keeps = refs
    ch, depth, rows, cols = out.shape
    place, count = lax.axis_index("space"), lax.axis_size("space")
    lane, lanes = lax.axis_index("chan"), lax.axis_size("chan")

    def fill(x):
        outer = ((0, left, lane == 0), (rows + 1, right, lane == lanes - 1))
        ids = [(y, jnp.where(off, -1, ref[x : x + 1])) for y, ref, off in outer]
        if 0 < x <= depth:
            at = (x * (rows + 2) + 1) * ch
            feats[at : at + rows * ch, :] = known[(x - 1) * rows * ch : x * rows * ch, :]
        else:
            ref, off = (below, place == 0) if x == 0 else (above, place == count - 1)
            ids = ids + [(y + 1, ref[y : y + 1]) for y in range(rows)]
            ids = [(y, jnp.where(off, -1, row)) for y, row in ids]
        for y, row in ids:
            at = (x * (rows + 2) + y) * ch
            feats[at : at + ch, :] = find(table, row, ch)

    group = ch * rows
    step = (rows + 2) * ch
    w = lax.broadcasted_iota(jnp.int32, (1, cols), 1)
    first, last = w == 0, w == cols - 1

    def forward(x):
        pres[x % 2] = jnp.dot(kernel[...], feats[x * step : (x + 3) * step, :], preferred_element_type=F32)

    def backward(x):
        term = dot_nt(deltas[x % 2], feats[x * step : (x + 3) * step, :])
        grads[...] = term if x == 0 else grads[...] + term

    gap = (iota(grads.shape, 1) % step) // ch - iota(grads.shape, 0) % rows
    for x in range(depth + 2):
        fill(x)
    for b in range(3):
        keeps[b] = hot(gap == b)
    forward(0)
    for x in range(depth):
        if x + 1 < depth:
            forward(x + 1)
        if x > 0:
            backward(x - 1)
        q = pres[x % 2]
        pre = q[group : 2 * group]
        pre = pre + jnp.where(first, 0.0, pltpu.roll(q[:group], 1, 1))
        pre = pre + jnp.where(last, 0.0, pltpu.roll(q[2 * group :], cols - 1, 1))
        act, slope = silu_parts(pre)
        stage[:, x] = act.reshape(ch, rows, cols).astype(BF16)
        pltpu.make_async_copy(stage.at[:, x], out.at[:, x], sems.at[x]).start()
        delta = cot[:, x].astype(F32).reshape(group, cols) * slope
        deltas[x % 2, :group] = jnp.where(last, 0.0, pltpu.roll(delta, cols - 1, 1)).astype(BF16)
        deltas[x % 2, group : 2 * group] = delta.astype(BF16)
        deltas[x % 2, 2 * group :] = jnp.where(first, 0.0, pltpu.roll(delta, 1, 1)).astype(BF16)
    backward(depth - 1)
    shape = grads.shape
    gather = hot(iota((3 * ch, shape[0]), 0) == iota((3 * ch, shape[0]), 1) // rows)
    m, n = iota((shape[1], 3 * ch), 0), iota((shape[1], 3 * ch), 1)
    fold = hot((m // step == n // ch) & (m % ch == n % ch))
    total = grads[...].astype(BF16)
    sums = [jnp.dot(gather, total * keeps[b], preferred_element_type=F32) for b in range(3)]
    tall = jnp.concatenate([piece for b in range(3) for piece in split(sums[b])], axis=0)
    tall = jnp.dot(tall, fold, preferred_element_type=F32)
    m, n = iota((3 * ch, ch * TAPS), 0), iota((3 * ch, ch * TAPS), 1)
    spot = jnp.where(m % ch == n // TAPS, n % TAPS - 9 * (m // ch), -1)
    result = jnp.zeros((ch, ch * TAPS), F32)
    for b in range(3):
        block = tall[6 * b * ch : (6 * b + 3) * ch] + tall[(6 * b + 3) * ch : (6 * b + 6) * ch]
        for e in range(3):
            both = jnp.concatenate(split(block[e * ch : (e + 1) * ch]), axis=0)
            moved = jnp.dot(both, hot(spot == 3 * b + e), preferred_element_type=F32)
            result = result + (moved[:ch] + moved[ch:])
    result = result * scale
    part[...] = result
    o_own, wide = bott_cot.shape
    message[:o_own, :] = bott_cot[...]
    message[o_own:, :] = fold_lanes([result.astype(BF16)], wide)
    for x in range(depth):
        pltpu.make_async_copy(stage.at[:, x], out.at[:, x], sems.at[x]).wait()


def fine_call(scale, known, below, above, left, right, table, kernel, cot, bott_cot, after):
    ch, depth, rows, cols = cot.shape
    o_own, lanes = bott_cot.shape
    more = ch * ch * TAPS // lanes
    S = jax.ShapeDtypeStruct
    return call(
        functools.partial(fine_body, scale),
        [
            S((ch, depth, rows, cols), BF16),
            S((ch, ch * TAPS), F32),
            S((o_own + more, lanes), BF16),
        ],
        [VM] * 10,
        [
            pltpu.VMEM(((depth + 2) * (rows + 2) * ch, cols), BF16),
            pltpu.VMEM((3 * ch * rows, 3 * ch * (rows + 2)), F32),
            pltpu.VMEM((ch, depth, rows, cols), BF16),
            pltpu.SemaphoreType.DMA((depth,)),
            pltpu.VMEM((2, 3 * ch * rows, cols), F32),
            pltpu.VMEM((2, 3 * ch * rows, cols), BF16),
            pltpu.VMEM((3, 3 * ch * rows, 3 * ch * (rows + 2)), BF16),
        ],
        6e9,
        4 << 20,
        20,
        [HB, VM, VM],
    )(known, below, above, left, right, table, kernel, cot, bott_cot, after)


def shift_masks(width, sign):
    lane = lax.broadcasted_iota(jnp.int32, (1, width), 1)
    y, w = lane // BW, lane % BW
    masks = []
    for b, e in STEPS:
        yy, ww = y + sign * b, w + sign * e
        masks.append((yy >= 0) & (yy < width // BW) & (ww >= 0) & (ww < BW))
    return masks


def convolve(weight, padded, chunks, before, pre_out, slabs, planes):
    o_own, lanes = pre_out.shape[0], pre_out.shape[1] // slabs
    width = lanes // planes
    masks = shift_masks(width, 1)
    for n in range(slabs):
        base = n * lanes
        at = [base + p * width for p in range(planes)]
        pre = [jnp.zeros((o_own, width), F32) if before is None else before[:, i : i + width] for i in at]
        for k, (b, e) in enumerate(STEPS):
            term = jnp.zeros((o_own, lanes), F32)
            for a in range(3):
                left = pl.ds((a * 9 + k) * o_own, o_own)
                for rows, columns in chunks:
                    win = padded[rows, base + a * width : base + a * width + lanes]
                    term = term + jnp.dot(weight[left, columns], win, preferred_element_type=F32)
            turn = -(b * BW + e) % width
            for p in range(planes):
                block = term[:, p * width : (p + 1) * width]
                if turn:
                    block = jnp.where(masks[k], pltpu.roll(block, turn, 1), 0.0)
                pre[p] = pre[p] + block
        for i, block in zip(at, pre):
            pre_out[:, i : i + width] = block


def lay(padded, row, piece, planes):
    slabs, cb, lanes = piece.shape
    width = lanes // planes
    place = lax.axis_index("space")
    rows = pl.ds(pl.multiple_of(row, cb), cb)
    padded[rows, :width] = jnp.zeros((cb, width), BF16)
    padded[rows, slabs * lanes + width :] = jnp.zeros((cb, width), BF16)
    for r in range(slabs):
        slab = lax.rem(place - r + slabs, slabs)
        padded[rows, pl.ds(pl.multiple_of(slab * lanes + width, width), lanes)] = piece[r]


def chip_body(planes, weight, after, mine, mate, pre_out, padded):
    slabs, cb, lanes = mine.shape
    chan = lax.axis_index("chan")
    lay(padded, (chan & 1) * cb, mine, planes)
    lay(padded, ((chan & 1) ^ 1) * cb, mate, planes)
    columns = pl.ds(pl.multiple_of((chan >> 1) * 2 * cb, 2 * cb), 2 * cb)
    convolve(weight, padded, [(pl.ds(0, 2 * cb), columns)], None, pre_out, slabs, planes)


def chip_call(weight, after, mine, mate, planes):
    slabs, cb, lanes = mine.shape
    return call(
        functools.partial(chip_body, planes),
        [jax.ShapeDtypeStruct((weight.shape[0] // 27, slabs * lanes), F32)],
        [VM] * 4,
        [pltpu.VMEM((2 * cb, (slabs + 1) * lanes), BF16)],
        2.5e9,
        1 << 20,
        16,
    )(weight, after, mine, mate)[0]


def bott_body(planes, weight, before, *refs):
    ins, (pre_out, padded) = refs[:-2], refs[-2:]
    slabs, cb, lanes = ins[0].shape
    chan = lax.axis_index("chan")
    for j, piece in enumerate(ins):
        lay(padded, (chan ^ j) * cb, piece, planes)
    chunks = []
    for other in range(1, len(ins) // 2):
        at = pl.ds(pl.multiple_of(((chan >> 1) ^ other) * 2 * cb, 2 * cb), 2 * cb)
        chunks.append((at, at))
    convolve(weight, padded, chunks, before, pre_out, slabs, planes)


def bott_call(weight, before, ins, planes):
    slabs, cb, lanes = ins[0].shape
    S = jax.ShapeDtypeStruct
    return call(
        functools.partial(bott_body, planes),
        [S(before.shape, F32), S((len(ins) * cb, (slabs + 1) * lanes), BF16)],
        [VM] * (2 + len(ins)),
        [],
        2.5e9,
        1 << 20,
        16,
    )(weight, before, *ins)


def back_body(slabs, planes, weight, pre, part, *refs):
    cots, refs = refs[:slabs], refs[slabs:]
    own_out, deltas, share, mine, part_sum, rows_t, stage, sem = refs
    send = pltpu.make_async_copy(stage, own_out, sem)
    pieces, lanes, cb = mine.shape
    o_own = deltas.shape[0]
    width = lanes // planes
    total = slabs * planes
    place = lax.axis_index("space")
    chan = lax.axis_index("chan")
    deltas[:, :width] = jnp.zeros((o_own, width), F32)
    deltas[:, (total + 1) * width :] = jnp.zeros((o_own, width), F32)
    for r in range(slabs):
        at = pl.multiple_of(lax.rem(place - r + slabs, slabs) * lanes, lanes)
        act, slope = silu_parts(pre[:, pl.ds(at, lanes)])
        delta = (cots[r][:o_own, :].astype(F32) * slope).astype(BF16).astype(F32)
        deltas[:, pl.ds(pl.multiple_of(at + width, width), lanes)] = delta
        if r == 0:
            stage[...] = together(act, planes)
            send.start()
    near = (planes + 2) * width
    turned = deltas[:, pl.ds(pl.multiple_of(place * lanes, width), near)].T
    w = iota((near, 1), 0) % BW
    gap = width + 2 * BW
    for e in (-1, 0, 1):
        moved = turned
        if e:
            moved = jnp.where((w - e >= 0) & (w - e < BW), pltpu.roll(turned, e % near, 0), 0.0)
        moved = moved.astype(BF16)
        for p in range(planes + 2):
            rows_t[e + 1, p * gap : p * gap + BW, :] = jnp.zeros((BW, o_own), BF16)
            rows_t[e + 1, p * gap + BW : p * gap + BW + width, :] = moved[p * width : (p + 1) * width]
            rows_t[e + 1, p * gap + BW + width : (p + 1) * gap, :] = jnp.zeros((BW, o_own), BF16)
    blocks = []
    for a in (-1, 0, 1):
        for b, e in STEPS:
            starts = [(1 + p - a) * gap + BW - b * BW for p in range(planes)]
            blocks.append(jnp.concatenate([rows_t[e + 1, s : s + width, :] for s in starts], axis=0))
    back = jnp.dot(jnp.concatenate(blocks, axis=1), weight[...], preferred_element_type=F32)
    grad = part[...]
    for r in range(1, slabs):
        grad = grad + unfold_lanes(cots[r][o_own:, :], *grad.shape)
    part_sum[...] = grad
    rest = fold_lanes([grad.astype(BF16)], cb)
    for j in range(pieces):
        block = back[:, j * cb : (j + 1) * cb]
        to = lax.rem(j - chan + pieces, pieces)
        mine[to] = block
        share[to, :lanes, :] = block.astype(BF16)
        share[j, lanes:, :] = rest
    send.wait()


def back_call(weight, pre, part, cots, pieces, planes):
    slabs = len(cots)
    o_own, length = pre.shape
    lanes = length // slabs
    width = lanes // planes
    cb = weight.shape[1] // pieces
    S = jax.ShapeDtypeStruct
    return call(
        functools.partial(back_body, slabs, planes),
        [
            S((o_own * planes, width), BF16),
            S((o_own, length + 2 * width), F32),
            S((pieces, lanes + part.size // cb, cb), BF16),
            S((pieces, lanes, cb), F32),
            S(part.shape, F32),
        ],
        [VM] * (3 + slabs),
        [
            pltpu.VMEM((3, (planes + 2) * (width + 2 * BW), o_own), BF16),
            pltpu.VMEM((o_own * planes, width), BF16),
            pltpu.SemaphoreType.DMA,
        ],
        1.8e9,
        1 << 20,
        16,
        [HB, VM, VM, VM, VM],
    )(weight, pre, part, *cots)


PLAN = ((0, 0, 4), (0, 4, 9), (1, 0, 9), (2, 0, 4), (2, 4, 7), (2, 7, 9))


def wgrad_body(scale, delta, full, out, shifted, stage, sems):
    o_own, length = delta.shape[0], delta.shape[1] - 8 * BW
    width = 4 * BW
    total = length // width
    masks = shift_masks(width, -1)
    shifted[:, :width] = jnp.zeros((9 * o_own, width), BF16)
    shifted[:, (total + 1) * width :] = jnp.zeros((9 * o_own, width), BF16)

    def build(some):
        for k in some:
            b, e = STEPS[k]
            turn = (b * BW + e) % width
            for p in range(total):
                moved = delta[:, (p + 1) * width : (p + 2) * width]
                if turn:
                    moved = jnp.where(masks[k], pltpu.roll(moved, turn, 1), 0.0)
                shifted[k * o_own : (k + 1) * o_own, (p + 1) * width : (p + 2) * width] = moved.astype(BF16)

    busy = [[], []]
    built = 0
    right = full[:, width : width + length]
    for a, low, high in PLAN:
        build(range(built, max(built, high)))
        built = max(built, high)
        if low == 0:
            for copy in busy[a % 2]:
                copy.wait()
            busy[a % 2] = []
        left = shifted[low * o_own : high * o_own, (2 - a) * width : (2 - a) * width + length]
        term = dot_nt(left, right) * scale
        stage[a % 2, low:high] = term.reshape((high - low,) + stage.shape[2:])
        to = out.at[a * 9 + low : a * 9 + high]
        copy = pltpu.make_async_copy(stage.at[a % 2, low:high], to, sems.at[a % 2, low])
        copy.start()
        busy[a % 2].append(copy)
    for copies in busy:
        for copy in copies:
            copy.wait()


def wgrad_call(scale, delta, full):
    o_own, length = delta.shape
    c_all = full.shape[0]
    return call(
        functools.partial(wgrad_body, scale),
        [jax.ShapeDtypeStruct((27, o_own, c_all), F32)],
        [VM] * 2,
        [
            pltpu.VMEM((9 * o_own, length), BF16),
            pltpu.VMEM((2, 9, o_own, c_all), F32),
            pltpu.SemaphoreType.DMA((2, 9)),
        ],
        6.6e9,
        8 << 20,
        32,
        [HB],
    )(delta, full)[0]


def last_body(count, mine, part, *refs):
    others, (out, taps) = refs[:count], refs[count:]
    lanes = mine.shape[1]
    total = mine[0]
    grad = part[...]
    for other in others:
        total = total + other[:lanes, :].astype(F32)
        grad = grad + unfold_lanes(other[lanes:, :], *grad.shape)
    out[...] = together(total.T, out.shape[0] // total.shape[1])
    for c in range(taps.shape[0]):
        taps[c] = grad[:, c * TAPS : c * TAPS + taps.shape[2]]


def last_call(mine, part, others, planes):
    lanes, cb = mine.shape[1:]
    ch = part.shape[0]
    return call(
        functools.partial(last_body, len(others)),
        [
            jax.ShapeDtypeStruct((cb * planes, lanes // planes), BF16),
            jax.ShapeDtypeStruct((ch, ch, 27), F32),
        ],
        [VM] * (2 + len(others)),
        [],
        1e9,
        1 << 18,
        12,
    )(mine, part, *others)


def hop(x, axis, offset):
    count = lax.axis_size(axis)
    return lax.ppermute(x, axis, [(i, (i + offset) % count) for i in range(count)])


def swap(x, axis, bit):
    count = lax.axis_size(axis)
    return lax.ppermute(x, axis, [(i, i ^ bit) for i in range(count)])


def shards(labels, table, fine_weight, fine_cot, bott_in, bott_weight, bott_cot):
    depth, rows, cols = labels.shape
    ch = fine_weight.shape[2]
    spaces, chans = lax.axis_size("space"), lax.axis_size("chan")
    cb, planes, width = bott_in.shape
    lanes = planes * width
    o_own = bott_cot.shape[0]

    flat_in, flat_cot = bott_in.reshape(cb * planes, width), bott_cot.reshape(o_own * planes, width)
    slab, first, last, cot, ids, near_table = pack_call(labels, flat_in, flat_cot, table.T, planes)
    taps = fine_weight.reshape(3, 3, 3, ch, ch).transpose(1, 2, 4, 0, 3).reshape(3, 3 * ch, 3 * ch)
    kernel, lookup, known = prep_call(taps, near_table, ids)
    sends = [last] + [slab] * (spaces - 3) + [first]
    got = [hop(x, "space", r + 1) for r, x in enumerate(sends)]
    slabs, below, above, top, bottom = unpack_call(ids, slab, got, kernel)
    left = hop(bottom, "chan", 1)
    right = hop(top, "chan", chans - 1)
    scale = (depth * spaces * rows * chans * cols) ** -0.5
    mate = swap(slabs, "chan", 1)
    fine_out, part, message = fine_call(
        scale, known, below, above, left, right, lookup, kernel, fine_cot, cot, mate
    )
    cots = [cot] + [hop(message, "space", r) for r in range(1, spaces)]
    ins = [slabs, mate] + [swap(slabs, "chan", j) for j in range(2, chans)]

    weight = bott_weight.transpose(1, 0, 2).reshape(27 * o_own, cb * chans)
    pre = chip_call(weight, part, slabs, mate, planes)
    pre, full = bott_call(weight, pre, ins, planes)
    bott_out, delta, share, mine, part = back_call(weight, pre, part, cots, chans, planes)
    others = [hop(share[r], "chan", r) for r in range(1, chans)]
    bott_wgrad = wgrad_call((planes * spaces * width) ** -0.5, delta, full).transpose(1, 0, 2)
    bott_dgrad, fine_wgrad = last_call(mine, part, others, planes)
    fine_wgrad = fine_wgrad.transpose(2, 0, 1)
    return fine_out, fine_wgrad, bott_out.reshape(bott_cot.shape), bott_dgrad.reshape(bott_in.shape), bott_wgrad


def solution(mesh):
    placed = (
        P(("groups", "space"), "chan", None),
        P(),
        P(),
        P(None, ("groups", "space"), "chan", None),
        P("chan", ("groups", "space"), None),
        P("chan", None, None),
        P("chan", ("groups", "space"), None),
    )
    return jax.shard_map(
        shards,
        mesh=mesh,
        in_specs=placed,
        out_specs=(
            P(None, ("groups", "space"), "chan", None),
            P("groups", None, None),
            P("chan", ("groups", "space"), None),
            P("chan", ("groups", "space"), None),
            P(("groups", "chan"), None, None),
        ),
        check_vma=False,
    )
```

```python
import functools
import jax
import jax.numpy as jnp
import numpy as np
from jax import lax
from jax.experimental import pallas as pl
from jax.experimental.pallas import tpu as pltpu
from jax.sharding import PartitionSpec as P

BW = 32
TAPS = 32
LOW = 128
F32 = jnp.float32
BF16 = jnp.bfloat16
VM = pl.BlockSpec(memory_space=pltpu.VMEM)
HB = pl.BlockSpec(memory_space=pltpu.HBM)
STEPS = [(b, e) for b in (-1, 0, 1) for e in (-1, 0, 1)]


def silu_parts(pre):
    s = jax.nn.sigmoid(pre)
    return pre * s, s * (1.0 + pre * (1.0 - s))


def dot_nt(a, b):
    return lax.dot_general(a, b, (((1,), (1,)), ((), ())), preferred_element_type=F32)


def call(body, outs, specs, scratch, flops, nbytes, mb, out_specs=None):
    return pl.pallas_call(
        body,
        out_shape=outs,
        in_specs=specs,
        out_specs=out_specs if out_specs is not None else [VM] * len(outs),
        scratch_shapes=scratch,
        compiler_params=pltpu.CompilerParams(vmem_limit_bytes=mb << 20),
        cost_estimate=pl.CostEstimate(flops=int(flops), bytes_accessed=int(nbytes), transcendentals=0),
    )


def iota(shape, dim):
    return lax.broadcasted_iota(jnp.int32, shape, dim)


def hot(condition):
    return condition.astype(F32).astype(BF16)


def pick_rows(rows, count, which, turned=False):
    shape = (rows * count, rows) if turned else (rows, rows * count)
    far, near = (0, 1) if turned else (1, 0)
    return hot(iota(shape, far) == count * iota(shape, near) + which)


def apart(x, planes):
    rows = x.shape[0] // planes
    parts = [jnp.dot(pick_rows(rows, planes, p), x, preferred_element_type=F32) for p in range(planes)]
    return jnp.concatenate(parts, axis=1).astype(BF16)


def together(x, planes):
    width = x.shape[1] // planes
    x = x.astype(BF16)
    parts = [
        jnp.dot(pick_rows(x.shape[0], planes, p, True), x[:, p * width : (p + 1) * width], preferred_element_type=F32)
        for p in range(planes)
    ]
    return sum(parts[1:], parts[0]).astype(BF16)


def pack_body(planes, labels, cells, cots, table, slab, first, last, cot, ids, near_table, raw_cells, raw_cots, sems):
    copies = [
        pltpu.make_async_copy(cells, raw_cells, sems.at[0]),
        pltpu.make_async_copy(labels, ids, sems.at[1]),
        pltpu.make_async_copy(cots, raw_cots, sems.at[2]),
        pltpu.make_async_copy(table, near_table, sems.at[3]),
    ]
    for copy in copies:
        copy.start()
    cb, lanes = slab.shape
    cols = labels.shape[2]
    copies[0].wait()
    block = apart(raw_cells[...], planes)
    for to in (slab, first, last):
        to[:cb, :] = block
    copies[1].wait()
    for to, plane in ((first, ids[0]), (last, ids[labels.shape[0] - 1])):
        parts = [plane & 255, plane >> 8]
        rows = jnp.concatenate([part[:, i : i + lanes] for part in parts for i in range(0, cols, lanes)], axis=0)
        to[cb:, :] = rows.astype(F32).astype(BF16)
    copies[2].wait()
    cot[...] = apart(raw_cots[...], planes)
    copies[3].wait()


def pack_call(labels, cells, cots, table, planes):
    depth, rows, cols = labels.shape
    cb, lanes = cells.shape[0] // planes, cells.shape[1] * planes
    more = 2 * rows * cols // lanes
    S = jax.ShapeDtypeStruct
    outs = [S((cb, lanes), BF16), S((cb + more, lanes), BF16), S((cb + more, lanes), BF16)]
    outs += [S((cots.shape[0] // planes, lanes), BF16), S(labels.shape, jnp.int32), S(table.shape, BF16)]
    scratch = [pltpu.VMEM(cells.shape, BF16), pltpu.VMEM(cots.shape, BF16), pltpu.SemaphoreType.DMA((4,))]
    body = functools.partial(pack_body, planes)
    args = [pltpu.with_memory_space_constraint(x, pltpu.HBM) for x in (labels, cells, cots, table)]
    return call(body, outs, [HB] * 4, scratch, 1e9, 1 << 18, 8)(*args)


def unpack_body(count, *refs):
    labels, slab, got = refs[0], refs[1], refs[2 : 2 + count]
    slabs, below, above, top, bottom = refs[3 + count :]
    cb, lanes = slab.shape
    depth, rows, cols = labels.shape
    slabs[0] = slab[...]
    for r in range(count):
        slabs[r + 1] = got[r][:cb, :] if r in (0, count - 1) else apart(got[r][...], lanes // got[r].shape[1])
    planes = []
    for ref in (got[0], got[count - 1]):
        rest = ref[cb:, :].astype(F32)
        pieces = [rest[i * rows : (i + 1) * rows] for i in range(rest.shape[0] // rows)]
        half = len(pieces) // 2
        low, high = (jnp.concatenate(part, axis=1) for part in (pieces[:half], pieces[half:]))
        planes.append((low + 256.0 * high).astype(jnp.int32))
    below[...] = planes[0]
    above[...] = planes[1]
    all_planes = [planes[0]] + [labels[x] for x in range(depth)] + [planes[1]]
    top[...] = jnp.concatenate([plane[:1] for plane in all_planes], axis=0)
    bottom[...] = jnp.concatenate([plane[rows - 1 :] for plane in all_planes], axis=0)


def unpack_call(labels, slab, got, after):
    depth, rows, cols = labels.shape
    cb, lanes = slab.shape
    S = jax.ShapeDtypeStruct
    outs = [S((len(got) + 1, cb, lanes), BF16)]
    outs += [S((rows, cols), jnp.int32)] * 2 + [S((depth + 2, cols), jnp.int32)] * 2
    body = functools.partial(unpack_body, len(got))
    return call(body, outs, [VM] * (3 + len(got)), [], 2e8, 1 << 18, 12)(labels, slab, *got, after)


def find(lookup, ids, ch):
    low = jnp.where(ids < 0, -1, ids & (LOW - 1)).astype(F32).astype(BF16)
    key = iota((LOW, ids.shape[1]), 0).astype(F32).astype(BF16)
    match = jnp.where(key == low, jnp.ones((), BF16), jnp.zeros((), BF16))
    picked = jnp.dot(lookup[...], match, preferred_element_type=F32)
    bit = 9
    while picked.shape[0] > ch:
        half = picked.shape[0] // 2
        picked = jnp.where(((ids >> bit) & 1) == 1, picked[half:], picked[:half])
        bit -= 1
    return picked.astype(BF16)


def prep_body(taps, table, ids, kernel, lookup, feats):
    ch = table.shape[0]
    depth, rows, cols = ids.shape
    shape = kernel.shape
    step = (rows + 2) * ch
    spread = hot(iota((shape[0], 3 * ch), 0) // rows == iota((shape[0], 3 * ch), 1))
    m, n = iota((3 * ch, shape[1]), 0), iota((3 * ch, shape[1]), 1)
    repeat = hot((m // ch == n // step) & (m % ch == n % ch))
    gap = (iota(shape, 1) % step) // ch - iota(shape, 0) % rows
    total = jnp.zeros(shape, F32)
    for b in range(3):
        tall = jnp.dot(spread, taps[b], preferred_element_type=F32).astype(BF16)
        total = jnp.where(gap == b, jnp.dot(tall, repeat, preferred_element_type=F32), total)
    kernel[...] = total.astype(BF16)
    for high in range(table.shape[1] // LOW):
        lookup[high * ch : (high + 1) * ch, :] = table[:, high * LOW : (high + 1) * LOW]
    for x in range(depth):
        for y in range(rows):
            at = (x * rows + y) * ch
            feats[at : at + ch, :] = find(lookup, ids[x, y : y + 1], ch)


def prep_call(taps, table, ids):
    ch, grains = table.shape
    depth, rows, cols = ids.shape
    return call(
        prep_body,
        [
            jax.ShapeDtypeStruct((3 * ch * rows, 3 * (rows + 2) * ch), BF16),
            jax.ShapeDtypeStruct((grains // LOW * ch, LOW), BF16),
            jax.ShapeDtypeStruct((depth * rows * ch, cols), BF16),
        ],
        [VM] * 3,
        [],
        2.5e9,
        1 << 18,
        16,
    )(taps, table, ids)


def split(x):
    high = x.astype(BF16)
    return high, (x - high.astype(F32)).astype(BF16)


def fold_lanes(blocks, lanes):
    return jnp.concatenate([b[:, i : i + lanes] for b in blocks for i in range(0, b.shape[1], lanes)], axis=0)


def unfold_lanes(x, rows, wide):
    count = wide // x.shape[1]
    cut = [x[i * rows : (i + 1) * rows].astype(F32) for i in range(x.shape[0] // rows)]
    wides = [jnp.concatenate(cut[i : i + count], axis=1) for i in range(0, len(cut), count)]
    return sum(wides[1:], wides[0])


def fine_body(scale, known, below, above, left, right, table, kernel, cot, bott_cot, after, *refs):
    out, part, message, feats, grads, stage, sems, pres, deltas, keeps, gather, fold, spread = refs
    ch, depth, rows, cols = out.shape
    place, count = lax.axis_index("space"), lax.axis_size("space")
    lane, lanes = lax.axis_index("chan"), lax.axis_size("chan")

    def fill(x):
        outer = ((0, left, lane == 0), (rows + 1, right, lane == lanes - 1))
        ids = [(y, jnp.where(off, -1, ref[x : x + 1])) for y, ref, off in outer]
        if 0 < x <= depth:
            at = (x * (rows + 2) + 1) * ch
            feats[at : at + rows * ch, :] = known[(x - 1) * rows * ch : x * rows * ch, :]
        else:
            ref, off = (below, place == 0) if x == 0 else (above, place == count - 1)
            ids = ids + [(y + 1, ref[y : y + 1]) for y in range(rows)]
            ids = [(y, jnp.where(off, -1, row)) for y, row in ids]
        for y, row in ids:
            at = (x * (rows + 2) + y) * ch
            feats[at : at + ch, :] = find(table, row, ch)

    group = ch * rows
    step = (rows + 2) * ch
    w = lax.broadcasted_iota(jnp.int32, (1, cols), 1)
    first, last = w == 0, w == cols - 1

    def forward(x):
        pres[x % 2] = jnp.dot(kernel[...], feats[x * step : (x + 3) * step, :], preferred_element_type=F32)

    def backward(x):
        term = dot_nt(deltas[x % 2], feats[x * step : (x + 3) * step, :])
        grads[...] = term if x == 0 else grads[...] + term

    gap = (iota(grads.shape, 1) % step) // ch - iota(grads.shape, 0) % rows
    for x in range(depth + 2):
        fill(x)
    for b in range(3):
        keeps[b] = hot(gap == b)
    gather[...] = hot(iota(gather.shape, 0) == iota(gather.shape, 1) // rows)
    m, n = iota(fold.shape, 0), iota(fold.shape, 1)
    fold[...] = hot((m // step == n // ch) & (m % ch == n % ch))
    m, n = iota(spread.shape, 0), iota(spread.shape, 1)
    tap = 9 * (m % (3 * ch) // ch) + m // (3 * ch)
    spread[...] = hot((m % ch == n // TAPS) & (tap == n % TAPS))
    forward(0)
    for x in range(depth):
        if x + 1 < depth:
            forward(x + 1)
        if x > 0:
            backward(x - 1)
        q = pres[x % 2]
        pre = q[group : 2 * group]
        pre = pre + jnp.where(first, 0.0, pltpu.roll(q[:group], 1, 1))
        pre = pre + jnp.where(last, 0.0, pltpu.roll(q[2 * group :], cols - 1, 1))
        act, slope = silu_parts(pre)
        stage[:, x] = act.reshape(ch, rows, cols).astype(BF16)
        pltpu.make_async_copy(stage.at[:, x], out.at[:, x], sems.at[x]).start()
        delta = cot[:, x].astype(F32).reshape(group, cols) * slope
        deltas[x % 2, :group] = jnp.where(last, 0.0, pltpu.roll(delta, cols - 1, 1)).astype(BF16)
        deltas[x % 2, group : 2 * group] = delta.astype(BF16)
        deltas[x % 2, 2 * group :] = jnp.where(first, 0.0, pltpu.roll(delta, 1, 1)).astype(BF16)
    backward(depth - 1)
    total = grads[...].astype(BF16)
    sums = [jnp.dot(gather[...], total * keeps[b], preferred_element_type=F32) for b in range(3)]
    tall = jnp.concatenate([piece for b in range(3) for piece in split(sums[b])], axis=0)
    tall = jnp.dot(tall, fold[...], preferred_element_type=F32)
    blocks = []
    for b in range(3):
        block = tall[6 * b * ch : (6 * b + 3) * ch] + tall[(6 * b + 3) * ch : (6 * b + 6) * ch]
        blocks += [block[e * ch : (e + 1) * ch] for e in range(3)]
    both = jnp.concatenate(split(jnp.concatenate(blocks, axis=1)), axis=0)
    moved = jnp.dot(both, spread[...], preferred_element_type=F32)
    result = moved[:ch] + moved[ch:]
    result = result * scale
    part[...] = result
    o_own, wide = bott_cot.shape
    message[:o_own, :] = bott_cot[...]
    message[o_own:, :] = fold_lanes([result.astype(BF16)], wide)
    for x in range(depth):
        pltpu.make_async_copy(stage.at[:, x], out.at[:, x], sems.at[x]).wait()


def fine_call(scale, known, below, above, left, right, table, kernel, cot, bott_cot, after):
    ch, depth, rows, cols = cot.shape
    o_own, lanes = bott_cot.shape
    more = ch * ch * TAPS // lanes
    S = jax.ShapeDtypeStruct
    return call(
        functools.partial(fine_body, scale),
        [
            S((ch, depth, rows, cols), BF16),
            S((ch, ch * TAPS), F32),
            S((o_own + more, lanes), BF16),
        ],
        [VM] * 10,
        [
            pltpu.VMEM(((depth + 2) * (rows + 2) * ch, cols), BF16),
            pltpu.VMEM((3 * ch * rows, 3 * ch * (rows + 2)), F32),
            pltpu.VMEM((ch, depth, rows, cols), BF16),
            pltpu.SemaphoreType.DMA((depth,)),
            pltpu.VMEM((2, 3 * ch * rows, cols), F32),
            pltpu.VMEM((2, 3 * ch * rows, cols), BF16),
            pltpu.VMEM((3, 3 * ch * rows, 3 * ch * (rows + 2)), BF16),
            pltpu.VMEM((3 * ch, 3 * ch * rows), BF16),
            pltpu.VMEM((3 * ch * (rows + 2), 3 * ch), BF16),
            pltpu.VMEM((27 * ch, ch * TAPS), BF16),
        ],
        6e9,
        4 << 20,
        20,
        [HB, VM, VM],
    )(known, below, above, left, right, table, kernel, cot, bott_cot, after)


def shift_masks(width, sign):
    lane = lax.broadcasted_iota(jnp.int32, (1, width), 1)
    y, w = lane // BW, lane % BW
    masks = []
    for b, e in STEPS:
        yy, ww = y + sign * b, w + sign * e
        masks.append((yy >= 0) & (yy < width // BW) & (ww >= 0) & (ww < BW))
    return masks


def convolve(weight, padded, chunks, before, pre_out, slabs, planes):
    o_own, lanes = pre_out.shape[0], pre_out.shape[1] // slabs
    width = lanes // planes
    masks = shift_masks(width, 1)
    for n in range(slabs):
        base = n * lanes
        at = [base + p * width for p in range(planes)]
        pre = [jnp.zeros((o_own, width), F32) if before is None else before[:, i : i + width] for i in at]
        for k, (b, e) in enumerate(STEPS):
            term = jnp.zeros((o_own, lanes), F32)
            for a in range(3):
                left = pl.ds((a * 9 + k) * o_own, o_own)
                for rows, columns in chunks:
                    win = padded[rows, base + a * width : base + a * width + lanes]
                    term = term + jnp.dot(weight[left, columns], win, preferred_element_type=F32)
            turn = -(b * BW + e) % width
            for p in range(planes):
                block = term[:, p * width : (p + 1) * width]
                if turn:
                    block = jnp.where(masks[k], pltpu.roll(block, turn, 1), 0.0)
                pre[p] = pre[p] + block
        for i, block in zip(at, pre):
            pre_out[:, i : i + width] = block


def lay(padded, row, piece, planes):
    slabs, cb, lanes = piece.shape
    width = lanes // planes
    place = lax.axis_index("space")
    rows = pl.ds(pl.multiple_of(row, cb), cb)
    padded[rows, :width] = jnp.zeros((cb, width), BF16)
    padded[rows, slabs * lanes + width :] = jnp.zeros((cb, width), BF16)
    for r in range(slabs):
        slab = lax.rem(place - r + slabs, slabs)
        padded[rows, pl.ds(pl.multiple_of(slab * lanes + width, width), lanes)] = piece[r]


def chip_body(planes, weight, after, mine, mate, pre_out, padded):
    slabs, cb, lanes = mine.shape
    chan = lax.axis_index("chan")
    lay(padded, (chan & 1) * cb, mine, planes)
    lay(padded, ((chan & 1) ^ 1) * cb, mate, planes)
    columns = pl.ds(pl.multiple_of((chan >> 1) * 2 * cb, 2 * cb), 2 * cb)
    convolve(weight, padded, [(pl.ds(0, 2 * cb), columns)], None, pre_out, slabs, planes)


def chip_call(weight, after, mine, mate, planes):
    slabs, cb, lanes = mine.shape
    return call(
        functools.partial(chip_body, planes),
        [jax.ShapeDtypeStruct((weight.shape[0] // 27, slabs * lanes), F32)],
        [VM] * 4,
        [pltpu.VMEM((2 * cb, (slabs + 1) * lanes), BF16)],
        2.5e9,
        1 << 20,
        16,
    )(weight, after, mine, mate)[0]


def bott_body(planes, weight, before, *refs):
    ins, (pre_out, padded) = refs[:-2], refs[-2:]
    slabs, cb, lanes = ins[0].shape
    chan = lax.axis_index("chan")
    for j, piece in enumerate(ins):
        lay(padded, (chan ^ j) * cb, piece, planes)
    chunks = []
    for other in range(1, len(ins) // 2):
        at = pl.ds(pl.multiple_of(((chan >> 1) ^ other) * 2 * cb, 2 * cb), 2 * cb)
        chunks.append((at, at))
    convolve(weight, padded, chunks, before, pre_out, slabs, planes)


def bott_call(weight, before, ins, planes):
    slabs, cb, lanes = ins[0].shape
    S = jax.ShapeDtypeStruct
    return call(
        functools.partial(bott_body, planes),
        [S(before.shape, F32), S((len(ins) * cb, (slabs + 1) * lanes), BF16)],
        [VM] * (2 + len(ins)),
        [],
        2.5e9,
        1 << 20,
        16,
    )(weight, before, *ins)


def back_body(slabs, planes, weight, pre, part, *refs):
    cots, refs = refs[:slabs], refs[slabs:]
    own_out, deltas, share, mine, part_sum, rows_t, stage, sem = refs
    send = pltpu.make_async_copy(stage, own_out, sem)
    pieces, lanes, cb = mine.shape
    o_own = deltas.shape[0]
    width = lanes // planes
    total = slabs * planes
    place = lax.axis_index("space")
    chan = lax.axis_index("chan")
    deltas[:, :width] = jnp.zeros((o_own, width), F32)
    deltas[:, (total + 1) * width :] = jnp.zeros((o_own, width), F32)
    for r in range(slabs):
        at = pl.multiple_of(lax.rem(place - r + slabs, slabs) * lanes, lanes)
        act, slope = silu_parts(pre[:, pl.ds(at, lanes)])
        delta = (cots[r][:o_own, :].astype(F32) * slope).astype(BF16).astype(F32)
        deltas[:, pl.ds(pl.multiple_of(at + width, width), lanes)] = delta
        if r == 0:
            stage[...] = together(act, planes)
            send.start()
    near = (planes + 2) * width
    turned = deltas[:, pl.ds(pl.multiple_of(place * lanes, width), near)].T
    w = iota((near, 1), 0) % BW
    gap = width + 2 * BW
    for e in (-1, 0, 1):
        moved = turned
        if e:
            moved = jnp.where((w - e >= 0) & (w - e < BW), pltpu.roll(turned, e % near, 0), 0.0)
        moved = moved.astype(BF16)
        for p in range(planes + 2):
            rows_t[e + 1, p * gap : p * gap + BW, :] = jnp.zeros((BW, o_own), BF16)
            rows_t[e + 1, p * gap + BW : p * gap + BW + width, :] = moved[p * width : (p + 1) * width]
            rows_t[e + 1, p * gap + BW + width : (p + 1) * gap, :] = jnp.zeros((BW, o_own), BF16)
    blocks = []
    for a in (-1, 0, 1):
        for b, e in STEPS:
            starts = [(1 + p - a) * gap + BW - b * BW for p in range(planes)]
            blocks.append(jnp.concatenate([rows_t[e + 1, s : s + width, :] for s in starts], axis=0))
    back = jnp.dot(jnp.concatenate(blocks, axis=1), weight[...], preferred_element_type=F32)
    grad = part[...]
    for r in range(1, slabs):
        grad = grad + unfold_lanes(cots[r][o_own:, :], *grad.shape)
    part_sum[...] = grad
    rest = fold_lanes([grad.astype(BF16)], cb)
    for j in range(pieces):
        block = back[:, j * cb : (j + 1) * cb]
        to = lax.rem(j - chan + pieces, pieces)
        mine[to] = block
        share[to, :lanes, :] = block.astype(BF16)
        share[j, lanes:, :] = rest
    send.wait()


def back_call(weight, pre, part, cots, pieces, planes):
    slabs = len(cots)
    o_own, length = pre.shape
    lanes = length // slabs
    width = lanes // planes
    cb = weight.shape[1] // pieces
    S = jax.ShapeDtypeStruct
    return call(
        functools.partial(back_body, slabs, planes),
        [
            S((o_own * planes, width), BF16),
            S((o_own, length + 2 * width), F32),
            S((pieces, lanes + part.size // cb, cb), BF16),
            S((pieces, lanes, cb), F32),
            S(part.shape, F32),
        ],
        [VM] * (3 + slabs),
        [
            pltpu.VMEM((3, (planes + 2) * (width + 2 * BW), o_own), BF16),
            pltpu.VMEM((o_own * planes, width), BF16),
            pltpu.SemaphoreType.DMA,
        ],
        1.8e9,
        1 << 20,
        16,
        [HB, VM, VM, VM, VM],
    )(weight, pre, part, *cots)


PLAN = ((0, 0, 4), (0, 4, 9), (1, 0, 9), (2, 0, 4), (2, 4, 7), (2, 7, 9))


def wgrad_body(scale, delta, full, out, shifted, stage, sems):
    o_own, length = delta.shape[0], delta.shape[1] - 8 * BW
    width = 4 * BW
    total = length // width
    masks = shift_masks(width, -1)
    shifted[:, :width] = jnp.zeros((9 * o_own, width), BF16)
    shifted[:, (total + 1) * width :] = jnp.zeros((9 * o_own, width), BF16)

    def build(some):
        for k in some:
            b, e = STEPS[k]
            turn = (b * BW + e) % width
            for p in range(total):
                moved = delta[:, (p + 1) * width : (p + 2) * width]
                if turn:
                    moved = jnp.where(masks[k], pltpu.roll(moved, turn, 1), 0.0)
                shifted[k * o_own : (k + 1) * o_own, (p + 1) * width : (p + 2) * width] = moved.astype(BF16)

    busy = [[], []]
    built = 0
    right = full[:, width : width + length]
    for a, low, high in PLAN:
        build(range(built, max(built, high)))
        built = max(built, high)
        if low == 0:
            for copy in busy[a % 2]:
                copy.wait()
            busy[a % 2] = []
        left = shifted[low * o_own : high * o_own, (2 - a) * width : (2 - a) * width + length]
        term = dot_nt(left, right) * scale
        stage[a % 2, low:high] = term.reshape((high - low,) + stage.shape[2:])
        to = out.at[a * 9 + low : a * 9 + high]
        copy = pltpu.make_async_copy(stage.at[a % 2, low:high], to, sems.at[a % 2, low])
        copy.start()
        busy[a % 2].append(copy)
    for copies in busy:
        for copy in copies:
            copy.wait()


def wgrad_call(scale, delta, full):
    o_own, length = delta.shape
    c_all = full.shape[0]
    return call(
        functools.partial(wgrad_body, scale),
        [jax.ShapeDtypeStruct((27, o_own, c_all), F32)],
        [VM] * 2,
        [
            pltpu.VMEM((9 * o_own, length), BF16),
            pltpu.VMEM((2, 9, o_own, c_all), F32),
            pltpu.SemaphoreType.DMA((2, 9)),
        ],
        6.6e9,
        8 << 20,
        32,
        [HB],
    )(delta, full)[0]


def last_body(count, mine, part, *refs):
    others, (out, taps) = refs[:count], refs[count:]
    lanes = mine.shape[1]
    total = mine[0]
    grad = part[...]
    for other in others:
        total = total + other[:lanes, :].astype(F32)
        grad = grad + unfold_lanes(other[lanes:, :], *grad.shape)
    out[...] = together(total.T, out.shape[0] // total.shape[1])
    for c in range(taps.shape[0]):
        taps[c] = grad[:, c * TAPS : c * TAPS + taps.shape[2]]


def last_call(mine, part, others, planes):
    lanes, cb = mine.shape[1:]
    ch = part.shape[0]
    return call(
        functools.partial(last_body, len(others)),
        [
            jax.ShapeDtypeStruct((cb * planes, lanes // planes), BF16),
            jax.ShapeDtypeStruct((ch, ch, 27), F32),
        ],
        [VM] * (2 + len(others)),
        [],
        1e9,
        1 << 18,
        12,
    )(mine, part, *others)


def hop(x, axis, offset):
    count = lax.axis_size(axis)
    return lax.ppermute(x, axis, [(i, (i + offset) % count) for i in range(count)])


def swap(x, axis, bit):
    count = lax.axis_size(axis)
    return lax.ppermute(x, axis, [(i, i ^ bit) for i in range(count)])


def shards(labels, table, fine_weight, fine_cot, bott_in, bott_weight, bott_cot):
    depth, rows, cols = labels.shape
    ch = fine_weight.shape[2]
    spaces, chans = lax.axis_size("space"), lax.axis_size("chan")
    cb, planes, width = bott_in.shape
    lanes = planes * width
    o_own = bott_cot.shape[0]

    flat_in, flat_cot = bott_in.reshape(cb * planes, width), bott_cot.reshape(o_own * planes, width)
    slab, first, last, cot, ids, near_table = pack_call(labels, flat_in, flat_cot, table.T, planes)
    taps = fine_weight.reshape(3, 3, 3, ch, ch).transpose(1, 2, 4, 0, 3).reshape(3, 3 * ch, 3 * ch)
    kernel, lookup, known = prep_call(taps, near_table, ids)
    sends = [last] + [flat_in] * (spaces - 3) + [first]
    got = [hop(x, "space", r + 1) for r, x in enumerate(sends)]
    slabs, below, above, top, bottom = unpack_call(ids, slab, got, kernel)
    left = hop(bottom, "chan", 1)
    right = hop(top, "chan", chans - 1)
    scale = (depth * spaces * rows * chans * cols) ** -0.5
    mate = swap(slabs, "chan", 1)
    fine_out, part, message = fine_call(
        scale, known, below, above, left, right, lookup, kernel, fine_cot, cot, mate
    )
    cots = [cot] + [hop(message, "space", r) for r in range(1, spaces)]
    ins = [slabs, mate] + [swap(slabs, "chan", j) for j in range(2, chans)]

    weight = bott_weight.transpose(1, 0, 2).reshape(27 * o_own, cb * chans)
    pre = chip_call(weight, part, slabs, mate, planes)
    pre, full = bott_call(weight, pre, ins, planes)
    bott_out, delta, share, mine, part = back_call(weight, pre, part, cots, chans, planes)
    others = [hop(share[r], "chan", r) for r in range(1, chans)]
    bott_wgrad = wgrad_call((planes * spaces * width) ** -0.5, delta, full).transpose(1, 0, 2)
    bott_dgrad, fine_wgrad = last_call(mine, part, others, planes)
    fine_wgrad = fine_wgrad.transpose(2, 0, 1)
    return fine_out, fine_wgrad, bott_out.reshape(bott_cot.shape), bott_dgrad.reshape(bott_in.shape), bott_wgrad


def solution(mesh):
    placed = (
        P(("groups", "space"), "chan", None),
        P(),
        P(),
        P(None, ("groups", "space"), "chan", None),
        P("chan", ("groups", "space"), None),
        P("chan", None, None),
        P("chan", ("groups", "space"), None),
    )
    return jax.shard_map(
        shards,
        mesh=mesh,
        in_specs=placed,
        out_specs=(
            P(None, ("groups", "space"), "chan", None),
            P("groups", None, None),
            P("chan", ("groups", "space"), None),
            P("chan", ("groups", "space"), None),
            P(("groups", "chan"), None, None),
        ),
        check_vma=False,
    )
```

```python
import functools
import jax
import jax.numpy as jnp
import numpy as np
from jax import lax
from jax.experimental import pallas as pl
from jax.experimental.pallas import tpu as pltpu
from jax.sharding import PartitionSpec as P

BW = 32
TAPS = 32
LOW = 128
F32 = jnp.float32
BF16 = jnp.bfloat16
VM = pl.BlockSpec(memory_space=pltpu.VMEM)
HB = pl.BlockSpec(memory_space=pltpu.HBM)
STEPS = [(b, e) for b in (-1, 0, 1) for e in (-1, 0, 1)]


def silu_parts(pre):
    s = jax.nn.sigmoid(pre)
    return pre * s, s * (1.0 + pre * (1.0 - s))


def dot_nt(a, b):
    return lax.dot_general(a, b, (((1,), (1,)), ((), ())), preferred_element_type=F32)


def call(body, outs, specs, scratch, flops, nbytes, mb, out_specs=None):
    return pl.pallas_call(
        body,
        out_shape=outs,
        in_specs=specs,
        out_specs=out_specs if out_specs is not None else [VM] * len(outs),
        scratch_shapes=scratch,
        compiler_params=pltpu.CompilerParams(vmem_limit_bytes=mb << 20),
        cost_estimate=pl.CostEstimate(flops=int(flops), bytes_accessed=int(nbytes), transcendentals=0),
    )


def iota(shape, dim):
    return lax.broadcasted_iota(jnp.int32, shape, dim)


def hot(condition):
    return condition.astype(F32).astype(BF16)


def pick_rows(rows, count, which, turned=False):
    shape = (rows * count, rows) if turned else (rows, rows * count)
    far, near = (0, 1) if turned else (1, 0)
    return hot(iota(shape, far) == count * iota(shape, near) + which)


def apart(x, planes):
    rows = x.shape[0] // planes
    parts = [jnp.dot(pick_rows(rows, planes, p), x, preferred_element_type=F32) for p in range(planes)]
    return jnp.concatenate(parts, axis=1).astype(BF16)


def together(x, planes):
    width = x.shape[1] // planes
    x = x.astype(BF16)
    parts = [
        jnp.dot(pick_rows(x.shape[0], planes, p, True), x[:, p * width : (p + 1) * width], preferred_element_type=F32)
        for p in range(planes)
    ]
    return sum(parts[1:], parts[0]).astype(BF16)


def pack_body(planes, labels, cells, cots, table, slab, first, last, cot, ids, near_table, raw_cells, raw_cots, sems):
    copies = [
        pltpu.make_async_copy(cells, raw_cells, sems.at[0]),
        pltpu.make_async_copy(labels, ids, sems.at[1]),
        pltpu.make_async_copy(cots, raw_cots, sems.at[2]),
        pltpu.make_async_copy(table, near_table, sems.at[3]),
    ]
    for copy in copies:
        copy.start()
    cb, lanes = slab.shape
    cols = labels.shape[2]
    copies[0].wait()
    block = apart(raw_cells[...], planes)
    for to in (slab, first, last):
        to[:cb, :] = block
    copies[1].wait()
    for to, plane in ((first, ids[0]), (last, ids[labels.shape[0] - 1])):
        parts = [plane & 255, plane >> 8]
        rows = jnp.concatenate([part[:, i : i + lanes] for part in parts for i in range(0, cols, lanes)], axis=0)
        to[cb:, :] = rows.astype(F32).astype(BF16)
    copies[2].wait()
    cot[...] = apart(raw_cots[...], planes)
    copies[3].wait()


def pack_call(labels, cells, cots, table, planes):
    depth, rows, cols = labels.shape
    cb, lanes = cells.shape[0] // planes, cells.shape[1] * planes
    more = 2 * rows * cols // lanes
    S = jax.ShapeDtypeStruct
    outs = [S((cb, lanes), BF16), S((cb + more, lanes), BF16), S((cb + more, lanes), BF16)]
    outs += [S((cots.shape[0] // planes, lanes), BF16), S(labels.shape, jnp.int32), S(table.shape, BF16)]
    scratch = [pltpu.VMEM(cells.shape, BF16), pltpu.VMEM(cots.shape, BF16), pltpu.SemaphoreType.DMA((4,))]
    body = functools.partial(pack_body, planes)
    args = [pltpu.with_memory_space_constraint(x, pltpu.HBM) for x in (labels, cells, cots, table)]
    return call(body, outs, [HB] * 4, scratch, 1e9, 1 << 18, 8)(*args)


def unpack_body(count, *refs):
    labels, slab, got = refs[0], refs[1], refs[2 : 2 + count]
    slabs, below, above, top, bottom = refs[3 + count :]
    cb, lanes = slab.shape
    depth, rows, cols = labels.shape
    slabs[0] = slab[...]
    for r in range(count):
        slabs[r + 1] = got[r][:cb, :] if r in (0, count - 1) else apart(got[r][...], lanes // got[r].shape[1])
    planes = []
    for ref in (got[0], got[count - 1]):
        rest = ref[cb:, :].astype(F32)
        pieces = [rest[i * rows : (i + 1) * rows] for i in range(rest.shape[0] // rows)]
        half = len(pieces) // 2
        low, high = (jnp.concatenate(part, axis=1) for part in (pieces[:half], pieces[half:]))
        planes.append((low + 256.0 * high).astype(jnp.int32))
    below[...] = planes[0]
    above[...] = planes[1]
    all_planes = [planes[0]] + [labels[x] for x in range(depth)] + [planes[1]]
    top[...] = jnp.concatenate([plane[:1] for plane in all_planes], axis=0)
    bottom[...] = jnp.concatenate([plane[rows - 1 :] for plane in all_planes], axis=0)


def unpack_call(labels, slab, got, after):
    depth, rows, cols = labels.shape
    cb, lanes = slab.shape
    S = jax.ShapeDtypeStruct
    outs = [S((len(got) + 1, cb, lanes), BF16)]
    outs += [S((rows, cols), jnp.int32)] * 2 + [S((depth + 2, cols), jnp.int32)] * 2
    body = functools.partial(unpack_body, len(got))
    return call(body, outs, [VM] * (3 + len(got)), [], 2e8, 1 << 18, 12)(labels, slab, *got, after)


def find(lookup, ids, ch):
    low = jnp.where(ids < 0, -1, ids & (LOW - 1)).astype(F32).astype(BF16)
    key = iota((LOW, ids.shape[1]), 0).astype(F32).astype(BF16)
    match = jnp.where(key == low, jnp.ones((), BF16), jnp.zeros((), BF16))
    picked = jnp.dot(lookup[...], match, preferred_element_type=F32)
    bit = 9
    while picked.shape[0] > ch:
        half = picked.shape[0] // 2
        picked = jnp.where(((ids >> bit) & 1) == 1, picked[half:], picked[:half])
        bit -= 1
    return picked.astype(BF16)


def prep_body(taps, table, ids, kernel, lookup, feats):
    ch = table.shape[0]
    depth, rows, cols = ids.shape
    shape = kernel.shape
    step = (rows + 2) * ch
    spread = hot(iota((shape[0], 3 * ch), 0) // rows == iota((shape[0], 3 * ch), 1))
    m, n = iota((3 * ch, shape[1]), 0), iota((3 * ch, shape[1]), 1)
    repeat = hot((m // ch == n // step) & (m % ch == n % ch))
    gap = (iota(shape, 1) % step) // ch - iota(shape, 0) % rows
    total = jnp.zeros(shape, F32)
    for b in range(3):
        tall = jnp.dot(spread, taps[b], preferred_element_type=F32).astype(BF16)
        total = jnp.where(gap == b, jnp.dot(tall, repeat, preferred_element_type=F32), total)
    kernel[...] = total.astype(BF16)
    for high in range(table.shape[1] // LOW):
        lookup[high * ch : (high + 1) * ch, :] = table[:, high * LOW : (high + 1) * LOW]
    for x in range(depth):
        for y in range(rows):
            at = (x * rows + y) * ch
            feats[at : at + ch, :] = find(lookup, ids[x, y : y + 1], ch)


def prep_call(taps, table, ids):
    ch, grains = table.shape
    depth, rows, cols = ids.shape
    return call(
        prep_body,
        [
            jax.ShapeDtypeStruct((3 * ch * rows, 3 * (rows + 2) * ch), BF16),
            jax.ShapeDtypeStruct((grains // LOW * ch, LOW), BF16),
            jax.ShapeDtypeStruct((depth * rows * ch, cols), BF16),
        ],
        [VM] * 3,
        [],
        2.5e9,
        1 << 18,
        16,
    )(taps, table, ids)


def split(x):
    high = x.astype(BF16)
    return high, (x - high.astype(F32)).astype(BF16)


def fold_lanes(blocks, lanes):
    return jnp.concatenate([b[:, i : i + lanes] for b in blocks for i in range(0, b.shape[1], lanes)], axis=0)


def unfold_lanes(x, rows, wide):
    count = wide // x.shape[1]
    cut = [x[i * rows : (i + 1) * rows].astype(F32) for i in range(x.shape[0] // rows)]
    wides = [jnp.concatenate(cut[i : i + count], axis=1) for i in range(0, len(cut), count)]
    return sum(wides[1:], wides[0])


def fine_body(scale, known, below, above, left, right, table, kernel, cot, bott_cot, after, *refs):
    out, part, message, feats, grads, stage, sems, pres, deltas, keeps, gather, fold, spread = refs
    ch, depth, rows, cols = out.shape
    place, count = lax.axis_index("space"), lax.axis_size("space")
    lane, lanes = lax.axis_index("chan"), lax.axis_size("chan")

    def fill(x):
        outer = ((0, left, lane == 0), (rows + 1, right, lane == lanes - 1))
        ids = [(y, jnp.where(off, -1, ref[x : x + 1])) for y, ref, off in outer]
        if 0 < x <= depth:
            at = (x * (rows + 2) + 1) * ch
            feats[at : at + rows * ch, :] = known[(x - 1) * rows * ch : x * rows * ch, :]
        else:
            ref, off = (below, place == 0) if x == 0 else (above, place == count - 1)
            ids = ids + [(y + 1, ref[y : y + 1]) for y in range(rows)]
            ids = [(y, jnp.where(off, -1, row)) for y, row in ids]
        for y, row in ids:
            at = (x * (rows + 2) + y) * ch
            feats[at : at + ch, :] = find(table, row, ch)

    group = ch * rows
    step = (rows + 2) * ch
    w = lax.broadcasted_iota(jnp.int32, (1, cols), 1)
    first, last = w == 0, w == cols - 1

    def forward(x):
        pres[x % 2] = jnp.dot(kernel[...], feats[x * step : (x + 3) * step, :], preferred_element_type=F32)

    def backward(x):
        term = dot_nt(deltas[x % 2], feats[x * step : (x + 3) * step, :])
        grads[...] = term if x == 0 else grads[...] + term

    gap = (iota(grads.shape, 1) % step) // ch - iota(grads.shape, 0) % rows
    for x in range(depth + 2):
        fill(x)
    for b in range(3):
        keeps[b] = hot(gap == b)
    gather[...] = hot(iota(gather.shape, 0) == iota(gather.shape, 1) // rows)
    m, n = iota(fold.shape, 0), iota(fold.shape, 1)
    fold[...] = hot((m // step == n // ch) & (m % ch == n % ch))
    m, n = iota(spread.shape, 0), iota(spread.shape, 1)
    tap = 9 * (m % (3 * ch) // ch) + m // (3 * ch)
    spread[...] = hot((m % ch == n // TAPS) & (tap == n % TAPS))
    forward(0)
    for x in range(depth):
        if x + 1 < depth:
            forward(x + 1)
        if x > 0:
            backward(x - 1)
        q = pres[x % 2]
        pre = q[group : 2 * group]
        pre = pre + jnp.where(first, 0.0, pltpu.roll(q[:group], 1, 1))
        pre = pre + jnp.where(last, 0.0, pltpu.roll(q[2 * group :], cols - 1, 1))
        act, slope = silu_parts(pre)
        stage[:, x] = act.reshape(ch, rows, cols).astype(BF16)
        pltpu.make_async_copy(stage.at[:, x], out.at[:, x], sems.at[x]).start()
        delta = cot[:, x].astype(F32).reshape(group, cols) * slope
        deltas[x % 2, :group] = jnp.where(last, 0.0, pltpu.roll(delta, cols - 1, 1)).astype(BF16)
        deltas[x % 2, group : 2 * group] = delta.astype(BF16)
        deltas[x % 2, 2 * group :] = jnp.where(first, 0.0, pltpu.roll(delta, 1, 1)).astype(BF16)
    backward(depth - 1)
    total = grads[...].astype(BF16)
    sums = [jnp.dot(gather[...], total * keeps[b], preferred_element_type=F32) for b in range(3)]
    tall = jnp.concatenate([piece for b in range(3) for piece in split(sums[b])], axis=0)
    tall = jnp.dot(tall, fold[...], preferred_element_type=F32)
    blocks = []
    for b in range(3):
        block = tall[6 * b * ch : (6 * b + 3) * ch] + tall[(6 * b + 3) * ch : (6 * b + 6) * ch]
        blocks += [block[e * ch : (e + 1) * ch] for e in range(3)]
    both = jnp.concatenate(split(jnp.concatenate(blocks, axis=1)), axis=0)
    moved = jnp.dot(both, spread[...], preferred_element_type=F32)
    result = moved[:ch] + moved[ch:]
    result = result * scale
    part[...] = result
    o_own, wide = bott_cot.shape
    message[:o_own, :] = bott_cot[...]
    message[o_own:, :] = fold_lanes([result.astype(BF16)], wide)
    for x in range(depth):
        pltpu.make_async_copy(stage.at[:, x], out.at[:, x], sems.at[x]).wait()


def fine_call(scale, known, below, above, left, right, table, kernel, cot, bott_cot, after):
    ch, depth, rows, cols = cot.shape
    o_own, lanes = bott_cot.shape
    more = ch * ch * TAPS // lanes
    S = jax.ShapeDtypeStruct
    return call(
        functools.partial(fine_body, scale),
        [
            S((ch, depth, rows, cols), BF16),
            S((ch, ch * TAPS), F32),
            S((o_own + more, lanes), BF16),
        ],
        [VM] * 10,
        [
            pltpu.VMEM(((depth + 2) * (rows + 2) * ch, cols), BF16),
            pltpu.VMEM((3 * ch * rows, 3 * ch * (rows + 2)), F32),
            pltpu.VMEM((ch, depth, rows, cols), BF16),
            pltpu.SemaphoreType.DMA((depth,)),
            pltpu.VMEM((2, 3 * ch * rows, cols), F32),
            pltpu.VMEM((2, 3 * ch * rows, cols), BF16),
            pltpu.VMEM((3, 3 * ch * rows, 3 * ch * (rows + 2)), BF16),
            pltpu.VMEM((3 * ch, 3 * ch * rows), BF16),
            pltpu.VMEM((3 * ch * (rows + 2), 3 * ch), BF16),
            pltpu.VMEM((27 * ch, ch * TAPS), BF16),
        ],
        6e9,
        4 << 20,
        20,
        [HB, VM, VM],
    )(known, below, above, left, right, table, kernel, cot, bott_cot, after)


def shift_masks(width, sign):
    lane = lax.broadcasted_iota(jnp.int32, (1, width), 1)
    y, w = lane // BW, lane % BW
    masks = []
    for b, e in STEPS:
        yy, ww = y + sign * b, w + sign * e
        masks.append((yy >= 0) & (yy < width // BW) & (ww >= 0) & (ww < BW))
    return masks


def convolve(weight, padded, chunks, before, pre_out, slabs, planes):
    o_own, lanes = pre_out.shape[0], pre_out.shape[1] // slabs
    width = lanes // planes
    masks = shift_masks(width, 1)
    for n in range(slabs):
        base = n * lanes
        at = [base + p * width for p in range(planes)]
        pre = [jnp.zeros((o_own, width), F32) if before is None else before[:, i : i + width] for i in at]
        for k, (b, e) in enumerate(STEPS):
            term = jnp.zeros((o_own, lanes), F32)
            for a in range(3):
                left = pl.ds((a * 9 + k) * o_own, o_own)
                for rows, columns in chunks:
                    win = padded[rows, base + a * width : base + a * width + lanes]
                    term = term + jnp.dot(weight[left, columns], win, preferred_element_type=F32)
            turn = -(b * BW + e) % width
            for p in range(planes):
                block = term[:, p * width : (p + 1) * width]
                if turn:
                    block = jnp.where(masks[k], pltpu.roll(block, turn, 1), 0.0)
                pre[p] = pre[p] + block
        for i, block in zip(at, pre):
            pre_out[:, i : i + width] = block


def lay(padded, row, piece, planes):
    slabs, cb, lanes = piece.shape
    width = lanes // planes
    place = lax.axis_index("space")
    rows = pl.ds(pl.multiple_of(row, cb), cb)
    padded[rows, :width] = jnp.zeros((cb, width), BF16)
    padded[rows, slabs * lanes + width :] = jnp.zeros((cb, width), BF16)
    for r in range(slabs):
        slab = lax.rem(place - r + slabs, slabs)
        padded[rows, pl.ds(pl.multiple_of(slab * lanes + width, width), lanes)] = piece[r]


def chip_body(planes, weight, after, mine, mate, pre_out, padded):
    slabs, cb, lanes = mine.shape
    chan = lax.axis_index("chan")
    lay(padded, (chan & 1) * cb, mine, planes)
    lay(padded, ((chan & 1) ^ 1) * cb, mate, planes)
    columns = pl.ds(pl.multiple_of((chan >> 1) * 2 * cb, 2 * cb), 2 * cb)
    convolve(weight, padded, [(pl.ds(0, 2 * cb), columns)], None, pre_out, slabs, planes)


def chip_call(weight, after, mine, mate, planes):
    slabs, cb, lanes = mine.shape
    return call(
        functools.partial(chip_body, planes),
        [jax.ShapeDtypeStruct((weight.shape[0] // 27, slabs * lanes), F32)],
        [VM] * 4,
        [pltpu.VMEM((2 * cb, (slabs + 1) * lanes), BF16)],
        2.5e9,
        1 << 20,
        16,
    )(weight, after, mine, mate)[0]


def bott_body(planes, weight, before, *refs):
    ins, (pre_out, padded) = refs[:-2], refs[-2:]
    slabs, cb, lanes = ins[0].shape
    chan = lax.axis_index("chan")
    for j, piece in enumerate(ins):
        lay(padded, (chan ^ j) * cb, piece, planes)
    chunks = []
    for other in range(1, len(ins) // 2):
        at = pl.ds(pl.multiple_of(((chan >> 1) ^ other) * 2 * cb, 2 * cb), 2 * cb)
        chunks.append((at, at))
    convolve(weight, padded, chunks, before, pre_out, slabs, planes)


def bott_call(weight, before, ins, planes):
    slabs, cb, lanes = ins[0].shape
    S = jax.ShapeDtypeStruct
    return call(
        functools.partial(bott_body, planes),
        [S(before.shape, F32), S((len(ins) * cb, (slabs + 1) * lanes), BF16)],
        [VM] * (2 + len(ins)),
        [],
        2.5e9,
        1 << 20,
        16,
    )(weight, before, *ins)


def spread_rows(rows_t, planes_of):
    width = rows_t.shape[2] - 2 * BW
    voxels = planes_of.T
    w = iota((voxels.shape[0], 1), 0) % BW
    none = jnp.zeros((BW, voxels.shape[1]), BF16)
    for e in (-1, 0, 1):
        moved = voxels
        if e:
            moved = jnp.where((w - e >= 0) & (w - e < BW), pltpu.roll(voxels, e % voxels.shape[0], 0), 0.0)
        moved = moved.astype(BF16)
        for p in range(voxels.shape[0] // width):
            rows_t[e + 1, p, :BW, :] = none
            rows_t[e + 1, p, BW : BW + width, :] = moved[p * width : (p + 1) * width]
            rows_t[e + 1, p, BW + width :, :] = none


def step_rows(rows_t, p, b, e):
    width = rows_t.shape[2] - 2 * BW
    return rows_t[e + 1, p, BW - b * BW : BW - b * BW + width, :]


def own_body(planes, weight, pre, cot, own_out, back, rows_t, stage, sem):
    send = pltpu.make_async_copy(stage, own_out, sem)
    o_own, lanes = cot.shape
    width = lanes // planes
    at = pl.multiple_of(lax.axis_index("space") * lanes, lanes)
    act, slope = silu_parts(pre[:, pl.ds(at, lanes)])
    stage[...] = together(act, planes)
    send.start()
    spread_rows(rows_t, (cot[...].astype(F32) * slope).astype(BF16).astype(F32))
    blocks = []
    for a in (-1, 0, 1):
        for b, e in STEPS:
            column = []
            for p in range(planes):
                inside = 0 <= p - a < planes
                column.append(step_rows(rows_t, p - a, b, e) if inside else jnp.zeros((width, o_own), BF16))
            blocks.append(jnp.concatenate(column, axis=0))
    back[...] = jnp.dot(jnp.concatenate(blocks, axis=1), weight[...], preferred_element_type=F32)
    send.wait()


def own_call(weight, pre, cot, planes):
    o_own, lanes = cot.shape
    width = lanes // planes
    S = jax.ShapeDtypeStruct
    return call(
        functools.partial(own_body, planes),
        [S((o_own * planes, width), BF16), S((lanes, weight.shape[1]), F32)],
        [VM] * 3,
        [
            pltpu.VMEM((3, planes, width + 2 * BW, o_own), BF16),
            pltpu.VMEM((o_own * planes, width), BF16),
            pltpu.SemaphoreType.DMA,
        ],
        1.6e9,
        1 << 20,
        16,
        [HB, VM],
    )(weight, pre, cot)


def back_body(slabs, planes, weight, pre, part, before, *refs):
    messages, (deltas, share, mine, part_sum, rows_t) = refs[:slabs], refs[slabs:]
    pieces, lanes, cb = mine.shape
    o_own = deltas.shape[0]
    width = lanes // planes
    total = slabs * planes
    place = lax.axis_index("space")
    chan = lax.axis_index("chan")
    deltas[:, :width] = jnp.zeros((o_own, width), F32)
    deltas[:, (total + 1) * width :] = jnp.zeros((o_own, width), F32)
    for r in range(slabs):
        at = pl.multiple_of(lax.rem(place - r + slabs, slabs) * lanes, lanes)
        slope = silu_parts(pre[:, pl.ds(at, lanes)])[1]
        delta = (messages[r][:o_own, :].astype(F32) * slope).astype(BF16).astype(F32)
        deltas[:, pl.ds(pl.multiple_of(at + width, width), lanes)] = delta
    base = place * lanes
    sides = [deltas[:, pl.ds(pl.multiple_of(i, width), width)] for i in (base, base + lanes + width)]
    spread_rows(rows_t, jnp.concatenate(sides, axis=1))
    sides = [jnp.concatenate([step_rows(rows_t, p, b, e) for b, e in STEPS], axis=1) for p in (0, 1)]
    first = jnp.dot(sides[0], weight[18 * o_own :, :], preferred_element_type=F32)
    last = jnp.dot(sides[1], weight[: 9 * o_own, :], preferred_element_type=F32)
    rows = [before[p * width : (p + 1) * width, :] for p in range(planes)]
    rows[0] = rows[0] + first
    rows[-1] = rows[-1] + last
    back = jnp.concatenate(rows, axis=0)
    grad = part[...]
    for r in range(1, slabs):
        grad = grad + unfold_lanes(messages[r][o_own:, :], *grad.shape)
    part_sum[...] = grad
    rest = fold_lanes([grad.astype(BF16)], cb)
    for j in range(pieces):
        block = back[:, j * cb : (j + 1) * cb]
        to = lax.rem(j - chan + pieces, pieces)
        mine[to] = block
        share[to, :lanes, :] = block.astype(BF16)
        share[j, lanes:, :] = rest


def back_call(weight, pre, part, before, messages, pieces, planes):
    slabs = len(messages)
    o_own, length = pre.shape
    lanes = length // slabs
    width = lanes // planes
    cb = weight.shape[1] // pieces
    S = jax.ShapeDtypeStruct
    return call(
        functools.partial(back_body, slabs, planes),
        [
            S((o_own, length + 2 * width), F32),
            S((pieces, lanes + part.size // cb, cb), BF16),
            S((pieces, lanes, cb), F32),
            S(part.shape, F32),
        ],
        [VM] * (4 + slabs),
        [pltpu.VMEM((3, 2, width + 2 * BW, o_own), BF16)],
        1.2e9,
        1 << 20,
        16,
    )(weight, pre, part, before, *messages)


PLAN = ((0, 0, 4), (0, 4, 9), (1, 0, 9), (2, 0, 4), (2, 4, 7), (2, 7, 9))


def wgrad_body(scale, delta, full, out, shifted, stage, sems):
    o_own, length = delta.shape[0], delta.shape[1] - 8 * BW
    width = 4 * BW
    total = length // width
    masks = shift_masks(width, -1)
    shifted[:, :width] = jnp.zeros((9 * o_own, width), BF16)
    shifted[:, (total + 1) * width :] = jnp.zeros((9 * o_own, width), BF16)

    def build(some):
        for k in some:
            b, e = STEPS[k]
            turn = (b * BW + e) % width
            for p in range(total):
                moved = delta[:, (p + 1) * width : (p + 2) * width]
                if turn:
                    moved = jnp.where(masks[k], pltpu.roll(moved, turn, 1), 0.0)
                shifted[k * o_own : (k + 1) * o_own, (p + 1) * width : (p + 2) * width] = moved.astype(BF16)

    busy = [[], []]
    built = 0
    right = full[:, width : width + length]
    for a, low, high in PLAN:
        build(range(built, max(built, high)))
        built = max(built, high)
        if low == 0:
            for copy in busy[a % 2]:
                copy.wait()
            busy[a % 2] = []
        left = shifted[low * o_own : high * o_own, (2 - a) * width : (2 - a) * width + length]
        term = dot_nt(left, right) * scale
        stage[a % 2, low:high] = term.reshape((high - low,) + stage.shape[2:])
        to = out.at[a * 9 + low : a * 9 + high]
        copy = pltpu.make_async_copy(stage.at[a % 2, low:high], to, sems.at[a % 2, low])
        copy.start()
        busy[a % 2].append(copy)
    for copies in busy:
        for copy in copies:
            copy.wait()


def wgrad_call(scale, delta, full):
    o_own, length = delta.shape
    c_all = full.shape[0]
    return call(
        functools.partial(wgrad_body, scale),
        [jax.ShapeDtypeStruct((27, o_own, c_all), F32)],
        [VM] * 2,
        [
            pltpu.VMEM((9 * o_own, length), BF16),
            pltpu.VMEM((2, 9, o_own, c_all), F32),
            pltpu.SemaphoreType.DMA((2, 9)),
        ],
        6.6e9,
        8 << 20,
        32,
        [HB],
    )(delta, full)[0]


def last_body(count, mine, part, *refs):
    others, (out, taps) = refs[:count], refs[count:]
    lanes = mine.shape[1]
    total = mine[0]
    grad = part[...]
    for other in others:
        total = total + other[:lanes, :].astype(F32)
        grad = grad + unfold_lanes(other[lanes:, :], *grad.shape)
    out[...] = together(total.T, out.shape[0] // total.shape[1])
    for c in range(taps.shape[0]):
        taps[c] = grad[:, c * TAPS : c * TAPS + taps.shape[2]]


def last_call(mine, part, others, planes):
    lanes, cb = mine.shape[1:]
    ch = part.shape[0]
    return call(
        functools.partial(last_body, len(others)),
        [
            jax.ShapeDtypeStruct((cb * planes, lanes // planes), BF16),
            jax.ShapeDtypeStruct((ch, ch, 27), F32),
        ],
        [VM] * (2 + len(others)),
        [],
        1e9,
        1 << 18,
        12,
    )(mine, part, *others)


def hop(x, axis, offset):
    count = lax.axis_size(axis)
    return lax.ppermute(x, axis, [(i, (i + offset) % count) for i in range(count)])


def swap(x, axis, bit):
    count = lax.axis_size(axis)
    return lax.ppermute(x, axis, [(i, i ^ bit) for i in range(count)])


def shards(labels, table, fine_weight, fine_cot, bott_in, bott_weight, bott_cot):
    depth, rows, cols = labels.shape
    ch = fine_weight.shape[2]
    spaces, chans = lax.axis_size("space"), lax.axis_size("chan")
    cb, planes, width = bott_in.shape
    lanes = planes * width
    o_own = bott_cot.shape[0]

    flat_in, flat_cot = bott_in.reshape(cb * planes, width), bott_cot.reshape(o_own * planes, width)
    slab, first, last, cot, ids, near_table = pack_call(labels, flat_in, flat_cot, table.T, planes)
    taps = fine_weight.reshape(3, 3, 3, ch, ch).transpose(1, 2, 4, 0, 3).reshape(3, 3 * ch, 3 * ch)
    kernel, lookup, known = prep_call(taps, near_table, ids)
    sends = [last] + [flat_in] * (spaces - 3) + [first]
    got = [hop(x, "space", r + 1) for r, x in enumerate(sends)]
    slabs, below, above, top, bottom = unpack_call(ids, slab, got, kernel)
    left = hop(bottom, "chan", 1)
    right = hop(top, "chan", chans - 1)
    scale = (depth * spaces * rows * chans * cols) ** -0.5
    mate = swap(slabs, "chan", 1)
    fine_out, part, message = fine_call(
        scale, known, below, above, left, right, lookup, kernel, fine_cot, cot, mate
    )
    cots = [cot] + [hop(message, "space", r) for r in range(1, spaces)]
    ins = [slabs, mate] + [swap(slabs, "chan", j) for j in range(2, chans)]

    weight = bott_weight.transpose(1, 0, 2).reshape(27 * o_own, cb * chans)
    pre = chip_call(weight, part, slabs, mate, planes)
    pre, full = bott_call(weight, pre, ins, planes)
    bott_out, before = own_call(weight, pre, cot, planes)
    delta, share, mine, part = back_call(weight, pre, part, before, cots, chans, planes)
    others = [hop(share[r], "chan", r) for r in range(1, chans)]
    bott_wgrad = wgrad_call((planes * spaces * width) ** -0.5, delta, full).transpose(1, 0, 2)
    bott_dgrad, fine_wgrad = last_call(mine, part, others, planes)
    fine_wgrad = fine_wgrad.transpose(2, 0, 1)
    return fine_out, fine_wgrad, bott_out.reshape(bott_cot.shape), bott_dgrad.reshape(bott_in.shape), bott_wgrad


def solution(mesh):
    placed = (
        P(("groups", "space"), "chan", None),
        P(),
        P(),
        P(None, ("groups", "space"), "chan", None),
        P("chan", ("groups", "space"), None),
        P("chan", None, None),
        P("chan", ("groups", "space"), None),
    )
    return jax.shard_map(
        shards,
        mesh=mesh,
        in_specs=placed,
        out_specs=(
            P(None, ("groups", "space"), "chan", None),
            P("groups", None, None),
            P("chan", ("groups", "space"), None),
            P("chan", ("groups", "space"), None),
            P(("groups", "chan"), None, None),
        ),
        check_vma=False,
    )
```

```python
import functools
import jax
import jax.numpy as jnp
import numpy as np
from jax import lax
from jax.experimental import pallas as pl
from jax.experimental.pallas import tpu as pltpu
from jax.sharding import PartitionSpec as P

BW = 32
TAPS = 32
LOW = 128
F32 = jnp.float32
BF16 = jnp.bfloat16
VM = pl.BlockSpec(memory_space=pltpu.VMEM)
HB = pl.BlockSpec(memory_space=pltpu.HBM)
STEPS = [(b, e) for b in (-1, 0, 1) for e in (-1, 0, 1)]


def silu_parts(pre):
    s = jax.nn.sigmoid(pre)
    return pre * s, s * (1.0 + pre * (1.0 - s))


def dot_nt(a, b):
    return lax.dot_general(a, b, (((1,), (1,)), ((), ())), preferred_element_type=F32)


def call(body, outs, specs, scratch, flops, nbytes, mb, out_specs=None):
    return pl.pallas_call(
        body,
        out_shape=outs,
        in_specs=specs,
        out_specs=out_specs if out_specs is not None else [VM] * len(outs),
        scratch_shapes=scratch,
        compiler_params=pltpu.CompilerParams(vmem_limit_bytes=mb << 20),
        cost_estimate=pl.CostEstimate(flops=int(flops), bytes_accessed=int(nbytes), transcendentals=0),
    )


def iota(shape, dim):
    return lax.broadcasted_iota(jnp.int32, shape, dim)


def hot(condition):
    return condition.astype(F32).astype(BF16)


def pick_rows(rows, count, which, turned=False):
    shape = (rows * count, rows) if turned else (rows, rows * count)
    far, near = (0, 1) if turned else (1, 0)
    return hot(iota(shape, far) == count * iota(shape, near) + which)


def apart(x, planes):
    rows = x.shape[0] // planes
    parts = [jnp.dot(pick_rows(rows, planes, p), x, preferred_element_type=F32) for p in range(planes)]
    return jnp.concatenate(parts, axis=1).astype(BF16)


def together(x, planes):
    width = x.shape[1] // planes
    x = x.astype(BF16)
    parts = [
        jnp.dot(pick_rows(x.shape[0], planes, p, True), x[:, p * width : (p + 1) * width], preferred_element_type=F32)
        for p in range(planes)
    ]
    return sum(parts[1:], parts[0]).astype(BF16)


def pack_body(planes, labels, cells, cots, table, slab, first, last, cot, ids, near_table, raw_cells, raw_cots, sems):
    copies = [
        pltpu.make_async_copy(cells, raw_cells, sems.at[0]),
        pltpu.make_async_copy(labels, ids, sems.at[1]),
        pltpu.make_async_copy(cots, raw_cots, sems.at[2]),
        pltpu.make_async_copy(table, near_table, sems.at[3]),
    ]
    for copy in copies:
        copy.start()
    cb, lanes = slab.shape
    cols = labels.shape[2]
    copies[0].wait()
    block = apart(raw_cells[...], planes)
    for to in (slab, first, last):
        to[:cb, :] = block
    copies[1].wait()
    for to, plane in ((first, ids[0]), (last, ids[labels.shape[0] - 1])):
        parts = [plane & 255, plane >> 8]
        rows = jnp.concatenate([part[:, i : i + lanes] for part in parts for i in range(0, cols, lanes)], axis=0)
        to[cb:, :] = rows.astype(F32).astype(BF16)
    copies[2].wait()
    cot[...] = apart(raw_cots[...], planes)
    copies[3].wait()


def pack_call(labels, cells, cots, table, planes):
    depth, rows, cols = labels.shape
    cb, lanes = cells.shape[0] // planes, cells.shape[1] * planes
    more = 2 * rows * cols // lanes
    S = jax.ShapeDtypeStruct
    outs = [S((cb, lanes), BF16), S((cb + more, lanes), BF16), S((cb + more, lanes), BF16)]
    outs += [S((cots.shape[0] // planes, lanes), BF16), S(labels.shape, jnp.int32), S(table.shape, BF16)]
    scratch = [pltpu.VMEM(cells.shape, BF16), pltpu.VMEM(cots.shape, BF16), pltpu.SemaphoreType.DMA((4,))]
    body = functools.partial(pack_body, planes)
    args = [pltpu.with_memory_space_constraint(x, pltpu.HBM) for x in (labels, cells, cots, table)]
    return call(body, outs, [HB] * 4, scratch, 1e9, 1 << 18, 8)(*args)


def unpack_body(count, *refs):
    labels, slab, got = refs[0], refs[1], refs[2 : 2 + count]
    slabs, below, above, top, bottom = refs[3 + count :]
    cb, lanes = slab.shape
    depth, rows, cols = labels.shape
    slabs[0] = slab[...]
    for r in range(count):
        slabs[r + 1] = got[r][:cb, :] if r in (0, count - 1) else apart(got[r][...], lanes // got[r].shape[1])
    planes = []
    for ref in (got[0], got[count - 1]):
        rest = ref[cb:, :].astype(F32)
        pieces = [rest[i * rows : (i + 1) * rows] for i in range(rest.shape[0] // rows)]
        half = len(pieces) // 2
        low, high = (jnp.concatenate(part, axis=1) for part in (pieces[:half], pieces[half:]))
        planes.append((low + 256.0 * high).astype(jnp.int32))
    below[...] = planes[0]
    above[...] = planes[1]
    all_planes = [planes[0]] + [labels[x] for x in range(depth)] + [planes[1]]
    top[...] = jnp.concatenate([plane[:1] for plane in all_planes], axis=0)
    bottom[...] = jnp.concatenate([plane[rows - 1 :] for plane in all_planes], axis=0)


def unpack_call(labels, slab, got, after):
    depth, rows, cols = labels.shape
    cb, lanes = slab.shape
    S = jax.ShapeDtypeStruct
    outs = [S((len(got) + 1, cb, lanes), BF16)]
    outs += [S((rows, cols), jnp.int32)] * 2 + [S((depth + 2, cols), jnp.int32)] * 2
    body = functools.partial(unpack_body, len(got))
    return call(body, outs, [VM] * (3 + len(got)), [], 2e8, 1 << 18, 12)(labels, slab, *got, after)


def find(lookup, ids, ch):
    low = jnp.where(ids < 0, -1, ids & (LOW - 1)).astype(F32).astype(BF16)
    key = iota((LOW, ids.shape[1]), 0).astype(F32).astype(BF16)
    match = jnp.where(key == low, jnp.ones((), BF16), jnp.zeros((), BF16))
    picked = jnp.dot(lookup[...], match, preferred_element_type=F32)
    bit = 9
    while picked.shape[0] > ch:
        half = picked.shape[0] // 2
        picked = jnp.where(((ids >> bit) & 1) == 1, picked[half:], picked[:half])
        bit -= 1
    return picked.astype(BF16)


def prep_body(taps, table, ids, kernel, lookup, feats):
    ch = table.shape[0]
    depth, rows, cols = ids.shape
    shape = kernel.shape
    step = (rows + 2) * ch
    spread = hot(iota((shape[0], 3 * ch), 0) // rows == iota((shape[0], 3 * ch), 1))
    m, n = iota((3 * ch, shape[1]), 0), iota((3 * ch, shape[1]), 1)
    repeat = hot((m // ch == n // step) & (m % ch == n % ch))
    gap = (iota(shape, 1) % step) // ch - iota(shape, 0) % rows
    total = jnp.zeros(shape, F32)
    for b in range(3):
        tall = jnp.dot(spread, taps[b], preferred_element_type=F32).astype(BF16)
        total = jnp.where(gap == b, jnp.dot(tall, repeat, preferred_element_type=F32), total)
    kernel[...] = total.astype(BF16)
    for high in range(table.shape[1] // LOW):
        lookup[high * ch : (high + 1) * ch, :] = table[:, high * LOW : (high + 1) * LOW]
    for x in range(depth):
        for y in range(rows):
            at = (x * rows + y) * ch
            feats[at : at + ch, :] = find(lookup, ids[x, y : y + 1], ch)


def prep_call(taps, table, ids):
    ch, grains = table.shape
    depth, rows, cols = ids.shape
    return call(
        prep_body,
        [
            jax.ShapeDtypeStruct((3 * ch * rows, 3 * (rows + 2) * ch), BF16),
            jax.ShapeDtypeStruct((grains // LOW * ch, LOW), BF16),
            jax.ShapeDtypeStruct((depth * rows * ch, cols), BF16),
        ],
        [VM] * 3,
        [],
        2.5e9,
        1 << 18,
        16,
    )(taps, table, ids)


def split(x):
    high = x.astype(BF16)
    return high, (x - high.astype(F32)).astype(BF16)


def fold_lanes(blocks, lanes):
    return jnp.concatenate([b[:, i : i + lanes] for b in blocks for i in range(0, b.shape[1], lanes)], axis=0)


def unfold_lanes(x, rows, wide):
    count = wide // x.shape[1]
    cut = [x[i * rows : (i + 1) * rows].astype(F32) for i in range(x.shape[0] // rows)]
    wides = [jnp.concatenate(cut[i : i + count], axis=1) for i in range(0, len(cut), count)]
    return sum(wides[1:], wides[0])


def fine_body(scale, known, below, above, left, right, table, kernel, cot, bott_cot, after, *refs):
    out, part, message, feats, grads, stage, sems, pres, deltas, keeps, gather, fold, spread = refs
    ch, depth, rows, cols = out.shape
    place, count = lax.axis_index("space"), lax.axis_size("space")
    lane, lanes = lax.axis_index("chan"), lax.axis_size("chan")

    def fill(x):
        outer = ((0, left, lane == 0), (rows + 1, right, lane == lanes - 1))
        ids = [(y, jnp.where(off, -1, ref[x : x + 1])) for y, ref, off in outer]
        if 0 < x <= depth:
            at = (x * (rows + 2) + 1) * ch
            feats[at : at + rows * ch, :] = known[(x - 1) * rows * ch : x * rows * ch, :]
        else:
            ref, off = (below, place == 0) if x == 0 else (above, place == count - 1)
            ids = ids + [(y + 1, ref[y : y + 1]) for y in range(rows)]
            ids = [(y, jnp.where(off, -1, row)) for y, row in ids]
        for y, row in ids:
            at = (x * (rows + 2) + y) * ch
            feats[at : at + ch, :] = find(table, row, ch)

    group = ch * rows
    step = (rows + 2) * ch
    w = lax.broadcasted_iota(jnp.int32, (1, cols), 1)
    first, last = w == 0, w == cols - 1

    def forward(x):
        pres[x % 2] = jnp.dot(kernel[...], feats[x * step : (x + 3) * step, :], preferred_element_type=F32)

    def backward(x):
        term = dot_nt(deltas[x % 2], feats[x * step : (x + 3) * step, :])
        grads[...] = term if x == 0 else grads[...] + term

    gap = (iota(grads.shape, 1) % step) // ch - iota(grads.shape, 0) % rows
    for x in range(3):
        fill(x)
    for b in range(3):
        keeps[b] = hot(gap == b)
    gather[...] = hot(iota(gather.shape, 0) == iota(gather.shape, 1) // rows)
    m, n = iota(fold.shape, 0), iota(fold.shape, 1)
    fold[...] = hot((m // step == n // ch) & (m % ch == n % ch))
    m, n = iota(spread.shape, 0), iota(spread.shape, 1)
    tap = 9 * (m % (3 * ch) // ch) + m // (3 * ch)
    spread[...] = hot((m % ch == n // TAPS) & (tap == n % TAPS))
    forward(0)
    for x in range(depth):
        if x + 1 < depth:
            fill(x + 3)
            forward(x + 1)
        if x > 0:
            backward(x - 1)
        q = pres[x % 2]
        pre = q[group : 2 * group]
        pre = pre + jnp.where(first, 0.0, pltpu.roll(q[:group], 1, 1))
        pre = pre + jnp.where(last, 0.0, pltpu.roll(q[2 * group :], cols - 1, 1))
        act, slope = silu_parts(pre)
        stage[:, x] = act.reshape(ch, rows, cols).astype(BF16)
        pltpu.make_async_copy(stage.at[:, x], out.at[:, x], sems.at[x]).start()
        delta = cot[:, x].astype(F32).reshape(group, cols) * slope
        deltas[x % 2, :group] = jnp.where(last, 0.0, pltpu.roll(delta, cols - 1, 1)).astype(BF16)
        deltas[x % 2, group : 2 * group] = delta.astype(BF16)
        deltas[x % 2, 2 * group :] = jnp.where(first, 0.0, pltpu.roll(delta, 1, 1)).astype(BF16)
    backward(depth - 1)
    total = grads[...].astype(BF16)
    sums = [jnp.dot(gather[...], total * keeps[b], preferred_element_type=F32) for b in range(3)]
    tall = jnp.concatenate([piece for b in range(3) for piece in split(sums[b])], axis=0)
    tall = jnp.dot(tall, fold[...], preferred_element_type=F32)
    blocks = []
    for b in range(3):
        block = tall[6 * b * ch : (6 * b + 3) * ch] + tall[(6 * b + 3) * ch : (6 * b + 6) * ch]
        blocks += [block[e * ch : (e + 1) * ch] for e in range(3)]
    both = jnp.concatenate(split(jnp.concatenate(blocks, axis=1)), axis=0)
    moved = jnp.dot(both, spread[...], preferred_element_type=F32)
    result = moved[:ch] + moved[ch:]
    result = result * scale
    part[...] = result
    o_own, wide = bott_cot.shape
    message[:o_own, :] = bott_cot[...]
    message[o_own:, :] = fold_lanes([result.astype(BF16)], wide)
    for x in range(depth):
        pltpu.make_async_copy(stage.at[:, x], out.at[:, x], sems.at[x]).wait()


def fine_call(scale, known, below, above, left, right, table, kernel, cot, bott_cot, after):
    ch, depth, rows, cols = cot.shape
    o_own, lanes = bott_cot.shape
    more = ch * ch * TAPS // lanes
    S = jax.ShapeDtypeStruct
    return call(
        functools.partial(fine_body, scale),
        [
            S((ch, depth, rows, cols), BF16),
            S((ch, ch * TAPS), F32),
            S((o_own + more, lanes), BF16),
        ],
        [VM] * 10,
        [
            pltpu.VMEM(((depth + 2) * (rows + 2) * ch, cols), BF16),
            pltpu.VMEM((3 * ch * rows, 3 * ch * (rows + 2)), F32),
            pltpu.VMEM((ch, depth, rows, cols), BF16),
            pltpu.SemaphoreType.DMA((depth,)),
            pltpu.VMEM((2, 3 * ch * rows, cols), F32),
            pltpu.VMEM((2, 3 * ch * rows, cols), BF16),
            pltpu.VMEM((3, 3 * ch * rows, 3 * ch * (rows + 2)), BF16),
            pltpu.VMEM((3 * ch, 3 * ch * rows), BF16),
            pltpu.VMEM((3 * ch * (rows + 2), 3 * ch), BF16),
            pltpu.VMEM((27 * ch, ch * TAPS), BF16),
        ],
        6e9,
        4 << 20,
        20,
        [HB, VM, VM],
    )(known, below, above, left, right, table, kernel, cot, bott_cot, after)


def shift_masks(width, sign):
    lane = lax.broadcasted_iota(jnp.int32, (1, width), 1)
    y, w = lane // BW, lane % BW
    masks = []
    for b, e in STEPS:
        yy, ww = y + sign * b, w + sign * e
        masks.append((yy >= 0) & (yy < width // BW) & (ww >= 0) & (ww < BW))
    return masks


def convolve(weight, padded, chunks, before, pre_out, slabs, planes):
    o_own, lanes = pre_out.shape[0], pre_out.shape[1] // slabs
    width = lanes // planes
    masks = shift_masks(width, 1)
    for n in range(slabs):
        base = n * lanes
        at = [base + p * width for p in range(planes)]
        pre = [jnp.zeros((o_own, width), F32) if before is None else before[:, i : i + width] for i in at]
        for k, (b, e) in enumerate(STEPS):
            term = jnp.zeros((o_own, lanes), F32)
            for a in range(3):
                left = pl.ds((a * 9 + k) * o_own, o_own)
                for rows, columns in chunks:
                    win = padded[rows, base + a * width : base + a * width + lanes]
                    term = term + jnp.dot(weight[left, columns], win, preferred_element_type=F32)
            turn = -(b * BW + e) % width
            for p in range(planes):
                block = term[:, p * width : (p + 1) * width]
                if turn:
                    block = jnp.where(masks[k], pltpu.roll(block, turn, 1), 0.0)
                pre[p] = pre[p] + block
        for i, block in zip(at, pre):
            pre_out[:, i : i + width] = block


def lay(padded, row, piece, planes):
    slabs, cb, lanes = piece.shape
    width = lanes // planes
    place = lax.axis_index("space")
    rows = pl.ds(pl.multiple_of(row, cb), cb)
    padded[rows, :width] = jnp.zeros((cb, width), BF16)
    padded[rows, slabs * lanes + width :] = jnp.zeros((cb, width), BF16)
    for r in range(slabs):
        slab = lax.rem(place - r + slabs, slabs)
        padded[rows, pl.ds(pl.multiple_of(slab * lanes + width, width), lanes)] = piece[r]


def chip_body(planes, weight, after, mine, mate, pre_out, padded):
    slabs, cb, lanes = mine.shape
    chan = lax.axis_index("chan")
    lay(padded, (chan & 1) * cb, mine, planes)
    lay(padded, ((chan & 1) ^ 1) * cb, mate, planes)
    columns = pl.ds(pl.multiple_of((chan >> 1) * 2 * cb, 2 * cb), 2 * cb)
    convolve(weight, padded, [(pl.ds(0, 2 * cb), columns)], None, pre_out, slabs, planes)


def chip_call(weight, after, mine, mate, planes):
    slabs, cb, lanes = mine.shape
    return call(
        functools.partial(chip_body, planes),
        [jax.ShapeDtypeStruct((weight.shape[0] // 27, slabs * lanes), F32)],
        [VM] * 4,
        [pltpu.VMEM((2 * cb, (slabs + 1) * lanes), BF16)],
        2.5e9,
        1 << 20,
        16,
    )(weight, after, mine, mate)[0]


def bott_body(planes, weight, before, *refs):
    ins, (pre_out, padded) = refs[:-2], refs[-2:]
    slabs, cb, lanes = ins[0].shape
    chan = lax.axis_index("chan")
    for j, piece in enumerate(ins):
        lay(padded, (chan ^ j) * cb, piece, planes)
    chunks = []
    for other in range(1, len(ins) // 2):
        at = pl.ds(pl.multiple_of(((chan >> 1) ^ other) * 2 * cb, 2 * cb), 2 * cb)
        chunks.append((at, at))
    convolve(weight, padded, chunks, before, pre_out, slabs, planes)


def bott_call(weight, before, ins, planes):
    slabs, cb, lanes = ins[0].shape
    S = jax.ShapeDtypeStruct
    return call(
        functools.partial(bott_body, planes),
        [S(before.shape, F32), S((len(ins) * cb, (slabs + 1) * lanes), BF16)],
        [VM] * (2 + len(ins)),
        [],
        2.5e9,
        1 << 20,
        16,
    )(weight, before, *ins)


def spread_rows(rows_t, planes_of):
    width = rows_t.shape[2] - 2 * BW
    voxels = planes_of.T
    w = iota((voxels.shape[0], 1), 0) % BW
    none = jnp.zeros((BW, voxels.shape[1]), BF16)
    for e in (-1, 0, 1):
        moved = voxels
        if e:
            moved = jnp.where((w - e >= 0) & (w - e < BW), pltpu.roll(voxels, e % voxels.shape[0], 0), 0.0)
        moved = moved.astype(BF16)
        for p in range(voxels.shape[0] // width):
            rows_t[e + 1, p, :BW, :] = none
            rows_t[e + 1, p, BW : BW + width, :] = moved[p * width : (p + 1) * width]
            rows_t[e + 1, p, BW + width :, :] = none


def step_rows(rows_t, p, b, e):
    width = rows_t.shape[2] - 2 * BW
    return rows_t[e + 1, p, BW - b * BW : BW - b * BW + width, :]


def own_body(planes, weight, pre, cot, own_out, back, rows_t, stage, sem):
    send = pltpu.make_async_copy(stage, own_out, sem)
    o_own, lanes = cot.shape
    width = lanes // planes
    at = pl.multiple_of(lax.axis_index("space") * lanes, lanes)
    act, slope = silu_parts(pre[:, pl.ds(at, lanes)])
    stage[...] = together(act, planes)
    send.start()
    spread_rows(rows_t, (cot[...].astype(F32) * slope).astype(BF16).astype(F32))
    blocks = []
    for a in (-1, 0, 1):
        for b, e in STEPS:
            column = []
            for p in range(planes):
                inside = 0 <= p - a < planes
                column.append(step_rows(rows_t, p - a, b, e) if inside else jnp.zeros((width, o_own), BF16))
            blocks.append(jnp.concatenate(column, axis=0))
    back[...] = jnp.dot(jnp.concatenate(blocks, axis=1), weight[...], preferred_element_type=F32)
    send.wait()


def own_call(weight, pre, cot, planes):
    o_own, lanes = cot.shape
    width = lanes // planes
    S = jax.ShapeDtypeStruct
    return call(
        functools.partial(own_body, planes),
        [S((o_own * planes, width), BF16), S((lanes, weight.shape[1]), F32)],
        [VM] * 3,
        [
            pltpu.VMEM((3, planes, width + 2 * BW, o_own), BF16),
            pltpu.VMEM((o_own * planes, width), BF16),
            pltpu.SemaphoreType.DMA,
        ],
        1.6e9,
        1 << 20,
        16,
        [HB, VM],
    )(weight, pre, cot)


def back_body(slabs, planes, weight, pre, part, before, *refs):
    messages, (deltas, share, mine, part_sum, rows_t) = refs[:slabs], refs[slabs:]
    pieces, lanes, cb = mine.shape
    o_own = deltas.shape[0]
    width = lanes // planes
    total = slabs * planes
    place = lax.axis_index("space")
    chan = lax.axis_index("chan")
    deltas[:, :width] = jnp.zeros((o_own, width), F32)
    deltas[:, (total + 1) * width :] = jnp.zeros((o_own, width), F32)
    for r in range(slabs):
        at = pl.multiple_of(lax.rem(place - r + slabs, slabs) * lanes, lanes)
        slope = silu_parts(pre[:, pl.ds(at, lanes)])[1]
        delta = (messages[r][:o_own, :].astype(F32) * slope).astype(BF16).astype(F32)
        deltas[:, pl.ds(pl.multiple_of(at + width, width), lanes)] = delta
    base = place * lanes
    sides = [deltas[:, pl.ds(pl.multiple_of(i, width), width)] for i in (base, base + lanes + width)]
    spread_rows(rows_t, jnp.concatenate(sides, axis=1))
    sides = [jnp.concatenate([step_rows(rows_t, p, b, e) for b, e in STEPS], axis=1) for p in (0, 1)]
    first = jnp.dot(sides[0], weight[18 * o_own :, :], preferred_element_type=F32)
    last = jnp.dot(sides[1], weight[: 9 * o_own, :], preferred_element_type=F32)
    rows = [before[p * width : (p + 1) * width, :] for p in range(planes)]
    rows[0] = rows[0] + first
    rows[-1] = rows[-1] + last
    back = jnp.concatenate(rows, axis=0)
    grad = part[...]
    for r in range(1, slabs):
        grad = grad + unfold_lanes(messages[r][o_own:, :], *grad.shape)
    part_sum[...] = grad
    rest = fold_lanes([grad.astype(BF16)], cb)
    for j in range(pieces):
        block = back[:, j * cb : (j + 1) * cb]
        to = lax.rem(j - chan + pieces, pieces)
        mine[to] = block
        share[to, :lanes, :] = block.astype(BF16)
        share[j, lanes:, :] = rest


def back_call(weight, pre, part, before, messages, pieces, planes):
    slabs = len(messages)
    o_own, length = pre.shape
    lanes = length // slabs
    width = lanes // planes
    cb = weight.shape[1] // pieces
    S = jax.ShapeDtypeStruct
    return call(
        functools.partial(back_body, slabs, planes),
        [
            S((o_own, length + 2 * width), F32),
            S((pieces, lanes + part.size // cb, cb), BF16),
            S((pieces, lanes, cb), F32),
            S(part.shape, F32),
        ],
        [VM] * (4 + slabs),
        [pltpu.VMEM((3, 2, width + 2 * BW, o_own), BF16)],
        1.2e9,
        1 << 20,
        16,
    )(weight, pre, part, before, *messages)


PLAN = ((0, 0, 4), (0, 4, 9), (1, 0, 9), (2, 0, 4), (2, 4, 7), (2, 7, 9))


def wgrad_body(scale, delta, full, out, shifted, stage, sems):
    o_own, length = delta.shape[0], delta.shape[1] - 8 * BW
    width = 4 * BW
    total = length // width
    masks = shift_masks(width, -1)
    shifted[:, :width] = jnp.zeros((9 * o_own, width), BF16)
    shifted[:, (total + 1) * width :] = jnp.zeros((9 * o_own, width), BF16)

    def build(some):
        for k in some:
            b, e = STEPS[k]
            turn = (b * BW + e) % width
            for p in range(total):
                moved = delta[:, (p + 1) * width : (p + 2) * width]
                if turn:
                    moved = jnp.where(masks[k], pltpu.roll(moved, turn, 1), 0.0)
                shifted[k * o_own : (k + 1) * o_own, (p + 1) * width : (p + 2) * width] = moved.astype(BF16)

    busy = [[], []]
    built = 0
    right = full[:, width : width + length]
    for a, low, high in PLAN:
        build(range(built, max(built, high)))
        built = max(built, high)
        if low == 0:
            for copy in busy[a % 2]:
                copy.wait()
            busy[a % 2] = []
        left = shifted[low * o_own : high * o_own, (2 - a) * width : (2 - a) * width + length]
        term = dot_nt(left, right) * scale
        stage[a % 2, low:high] = term.reshape((high - low,) + stage.shape[2:])
        to = out.at[a * 9 + low : a * 9 + high]
        copy = pltpu.make_async_copy(stage.at[a % 2, low:high], to, sems.at[a % 2, low])
        copy.start()
        busy[a % 2].append(copy)
    for copies in busy:
        for copy in copies:
            copy.wait()


def wgrad_call(scale, delta, full):
    o_own, length = delta.shape
    c_all = full.shape[0]
    return call(
        functools.partial(wgrad_body, scale),
        [jax.ShapeDtypeStruct((27, o_own, c_all), F32)],
        [VM] * 2,
        [
            pltpu.VMEM((9 * o_own, length), BF16),
            pltpu.VMEM((2, 9, o_own, c_all), F32),
            pltpu.SemaphoreType.DMA((2, 9)),
        ],
        6.6e9,
        8 << 20,
        32,
        [HB],
    )(delta, full)[0]


def last_body(count, mine, part, *refs):
    others, (out, taps) = refs[:count], refs[count:]
    lanes = mine.shape[1]
    total = mine[0]
    grad = part[...]
    for other in others:
        total = total + other[:lanes, :].astype(F32)
        grad = grad + unfold_lanes(other[lanes:, :], *grad.shape)
    out[...] = together(total.T, out.shape[0] // total.shape[1])
    for c in range(taps.shape[0]):
        taps[c] = grad[:, c * TAPS : c * TAPS + taps.shape[2]]


def last_call(mine, part, others, planes):
    lanes, cb = mine.shape[1:]
    ch = part.shape[0]
    return call(
        functools.partial(last_body, len(others)),
        [
            jax.ShapeDtypeStruct((cb * planes, lanes // planes), BF16),
            jax.ShapeDtypeStruct((ch, ch, 27), F32),
        ],
        [VM] * (2 + len(others)),
        [],
        1e9,
        1 << 18,
        12,
    )(mine, part, *others)


def hop(x, axis, offset):
    count = lax.axis_size(axis)
    return lax.ppermute(x, axis, [(i, (i + offset) % count) for i in range(count)])


def swap(x, axis, bit):
    count = lax.axis_size(axis)
    return lax.ppermute(x, axis, [(i, i ^ bit) for i in range(count)])


def shards(labels, table, fine_weight, fine_cot, bott_in, bott_weight, bott_cot):
    depth, rows, cols = labels.shape
    ch = fine_weight.shape[2]
    spaces, chans = lax.axis_size("space"), lax.axis_size("chan")
    cb, planes, width = bott_in.shape
    lanes = planes * width
    o_own = bott_cot.shape[0]

    flat_in, flat_cot = bott_in.reshape(cb * planes, width), bott_cot.reshape(o_own * planes, width)
    slab, first, last, cot, ids, near_table = pack_call(labels, flat_in, flat_cot, table.T, planes)
    taps = fine_weight.reshape(3, 3, 3, ch, ch).transpose(1, 2, 4, 0, 3).reshape(3, 3 * ch, 3 * ch)
    kernel, lookup, known = prep_call(taps, near_table, ids)
    sends = [last] + [flat_in] * (spaces - 3) + [first]
    got = [hop(x, "space", r + 1) for r, x in enumerate(sends)]
    slabs, below, above, top, bottom = unpack_call(ids, slab, got, kernel)
    left = hop(bottom, "chan", 1)
    right = hop(top, "chan", chans - 1)
    scale = (depth * spaces * rows * chans * cols) ** -0.5
    mate = swap(slabs, "chan", 1)
    fine_out, part, message = fine_call(
        scale, known, below, above, left, right, lookup, kernel, fine_cot, cot, mate
    )
    cots = [cot] + [hop(message, "space", r) for r in range(1, spaces)]
    ins = [slabs, mate] + [swap(slabs, "chan", j) for j in range(2, chans)]

    weight = bott_weight.transpose(1, 0, 2).reshape(27 * o_own, cb * chans)
    pre = chip_call(weight, part, slabs, mate, planes)
    pre, full = bott_call(weight, pre, ins, planes)
    bott_out, before = own_call(weight, pre, cot, planes)
    delta, share, mine, part = back_call(weight, pre, part, before, cots, chans, planes)
    others = [hop(share[r], "chan", r) for r in range(1, chans)]
    bott_wgrad = wgrad_call((planes * spaces * width) ** -0.5, delta, full).transpose(1, 0, 2)
    bott_dgrad, fine_wgrad = last_call(mine, part, others, planes)
    fine_wgrad = fine_wgrad.transpose(2, 0, 1)
    return fine_out, fine_wgrad, bott_out.reshape(bott_cot.shape), bott_dgrad.reshape(bott_in.shape), bott_wgrad


def solution(mesh):
    placed = (
        P(("groups", "space"), "chan", None),
        P(),
        P(),
        P(None, ("groups", "space"), "chan", None),
        P("chan", ("groups", "space"), None),
        P("chan", None, None),
        P("chan", ("groups", "space"), None),
    )
    return jax.shard_map(
        shards,
        mesh=mesh,
        in_specs=placed,
        out_specs=(
            P(None, ("groups", "space"), "chan", None),
            P("groups", None, None),
            P("chan", ("groups", "space"), None),
            P("chan", ("groups", "space"), None),
            P(("groups", "chan"), None, None),
        ),
        check_vma=False,
    )
```

```python
import functools
import jax
import jax.numpy as jnp
import numpy as np
from jax import lax
from jax.experimental import pallas as pl
from jax.experimental.pallas import tpu as pltpu
from jax.sharding import PartitionSpec as P

BW = 32
TAPS = 32
LOW = 128
F32 = jnp.float32
BF16 = jnp.bfloat16
VM = pl.BlockSpec(memory_space=pltpu.VMEM)
HB = pl.BlockSpec(memory_space=pltpu.HBM)
STEPS = [(b, e) for b in (-1, 0, 1) for e in (-1, 0, 1)]


def silu_parts(pre):
    s = jax.nn.sigmoid(pre)
    return pre * s, s * (1.0 + pre * (1.0 - s))


def dot_nt(a, b):
    return lax.dot_general(a, b, (((1,), (1,)), ((), ())), preferred_element_type=F32)


def call(body, outs, specs, scratch, flops, nbytes, mb, out_specs=None):
    return pl.pallas_call(
        body,
        out_shape=outs,
        in_specs=specs,
        out_specs=out_specs if out_specs is not None else [VM] * len(outs),
        scratch_shapes=scratch,
        compiler_params=pltpu.CompilerParams(vmem_limit_bytes=mb << 20),
        cost_estimate=pl.CostEstimate(flops=int(flops), bytes_accessed=int(nbytes), transcendentals=0),
    )


def iota(shape, dim):
    return lax.broadcasted_iota(jnp.int32, shape, dim)


def hot(condition):
    return condition.astype(F32).astype(BF16)


def pick_rows(rows, count, which, turned=False):
    shape = (rows * count, rows) if turned else (rows, rows * count)
    far, near = (0, 1) if turned else (1, 0)
    return hot(iota(shape, far) == count * iota(shape, near) + which)


def apart(x, planes):
    rows = x.shape[0] // planes
    parts = [jnp.dot(pick_rows(rows, planes, p), x, preferred_element_type=F32) for p in range(planes)]
    return jnp.concatenate(parts, axis=1).astype(BF16)


def together(x, planes):
    width = x.shape[1] // planes
    x = x.astype(BF16)
    parts = [
        jnp.dot(pick_rows(x.shape[0], planes, p, True), x[:, p * width : (p + 1) * width], preferred_element_type=F32)
        for p in range(planes)
    ]
    return sum(parts[1:], parts[0]).astype(BF16)


def pack_body(planes, labels, cells, cots, table, slab, first, last, cot, ids, near_table, raw_cells, raw_cots, sems):
    copies = [
        pltpu.make_async_copy(cells, raw_cells, sems.at[0]),
        pltpu.make_async_copy(labels, ids, sems.at[1]),
        pltpu.make_async_copy(cots, raw_cots, sems.at[2]),
        pltpu.make_async_copy(table, near_table, sems.at[3]),
    ]
    for copy in copies:
        copy.start()
    cb, lanes = slab.shape
    cols = labels.shape[2]
    copies[0].wait()
    block = apart(raw_cells[...], planes)
    for to in (slab, first, last):
        to[:cb, :] = block
    copies[1].wait()
    for to, plane in ((first, ids[0]), (last, ids[labels.shape[0] - 1])):
        coded = ((plane & 127) + 128) << (plane >> 7)
        rows = jnp.concatenate([coded[:, i : i + lanes] for i in range(0, cols, lanes)], axis=0)
        to[cb:, :] = rows.astype(F32).astype(BF16)
    copies[2].wait()
    cot[...] = apart(raw_cots[...], planes)
    copies[3].wait()


def pack_call(labels, cells, cots, table, planes):
    depth, rows, cols = labels.shape
    cb, lanes = cells.shape[0] // planes, cells.shape[1] * planes
    more = rows * cols // lanes
    S = jax.ShapeDtypeStruct
    outs = [S((cb, lanes), BF16), S((cb + more, lanes), BF16), S((cb + more, lanes), BF16)]
    outs += [S((cots.shape[0] // planes, lanes), BF16), S(labels.shape, jnp.int32), S(table.shape, BF16)]
    scratch = [pltpu.VMEM(cells.shape, BF16), pltpu.VMEM(cots.shape, BF16), pltpu.SemaphoreType.DMA((4,))]
    body = functools.partial(pack_body, planes)
    args = [pltpu.with_memory_space_constraint(x, pltpu.HBM) for x in (labels, cells, cots, table)]
    return call(body, outs, [HB] * 4, scratch, 1e9, 1 << 18, 8)(*args)


def unpack_body(count, *refs):
    labels, slab, got = refs[0], refs[1], refs[2 : 2 + count]
    slabs, below, above, top, bottom = refs[3 + count :]
    cb, lanes = slab.shape
    depth, rows, cols = labels.shape
    slabs[0] = slab[...]
    for r in range(count):
        slabs[r + 1] = got[r][:cb, :] if r in (0, count - 1) else apart(got[r][...], lanes // got[r].shape[1])
    planes = []
    for ref in (got[0], got[count - 1]):
        rest = ref[cb:, :].astype(F32)
        pieces = [rest[i * rows : (i + 1) * rows] for i in range(rest.shape[0] // rows)]
        coded = jnp.concatenate(pieces, axis=1).astype(jnp.int32)
        high = sum((coded >= (128 << t)).astype(jnp.int32) for t in range(1, 8))
        planes.append(high * 128 + (coded >> high) - 128)
    below[...] = planes[0]
    above[...] = planes[1]
    all_planes = [planes[0]] + [labels[x] for x in range(depth)] + [planes[1]]
    top[...] = jnp.concatenate([plane[:1] for plane in all_planes], axis=0)
    bottom[...] = jnp.concatenate([plane[rows - 1 :] for plane in all_planes], axis=0)


def unpack_call(labels, slab, got, after):
    depth, rows, cols = labels.shape
    cb, lanes = slab.shape
    S = jax.ShapeDtypeStruct
    outs = [S((len(got) + 1, cb, lanes), BF16)]
    outs += [S((rows, cols), jnp.int32)] * 2 + [S((depth + 2, cols), jnp.int32)] * 2
    body = functools.partial(unpack_body, len(got))
    return call(body, outs, [VM] * (3 + len(got)), [], 2e8, 1 << 18, 12)(labels, slab, *got, after)


def find(lookup, ids, ch):
    low = jnp.where(ids < 0, -1, ids & (LOW - 1)).astype(F32).astype(BF16)
    key = iota((LOW, ids.shape[1]), 0).astype(F32).astype(BF16)
    match = jnp.where(key == low, jnp.ones((), BF16), jnp.zeros((), BF16))
    picked = jnp.dot(lookup[...], match, preferred_element_type=F32)
    bit = 9
    while picked.shape[0] > ch:
        half = picked.shape[0] // 2
        picked = jnp.where(((ids >> bit) & 1) == 1, picked[half:], picked[:half])
        bit -= 1
    return picked.astype(BF16)


def prep_body(taps, table, ids, kernel, lookup, feats):
    ch = table.shape[0]
    depth, rows, cols = ids.shape
    shape = kernel.shape
    step = (rows + 2) * ch
    spread = hot(iota((shape[0], 3 * ch), 0) // rows == iota((shape[0], 3 * ch), 1))
    m, n = iota((3 * ch, shape[1]), 0), iota((3 * ch, shape[1]), 1)
    repeat = hot((m // ch == n // step) & (m % ch == n % ch))
    gap = (iota(shape, 1) % step) // ch - iota(shape, 0) % rows
    total = jnp.zeros(shape, F32)
    for b in range(3):
        tall = jnp.dot(spread, taps[b], preferred_element_type=F32).astype(BF16)
        total = jnp.where(gap == b, jnp.dot(tall, repeat, preferred_element_type=F32), total)
    kernel[...] = total.astype(BF16)
    for high in range(table.shape[1] // LOW):
        lookup[high * ch : (high + 1) * ch, :] = table[:, high * LOW : (high + 1) * LOW]
    for x in range(depth):
        for y in range(rows):
            at = (x * rows + y) * ch
            feats[at : at + ch, :] = find(lookup, ids[x, y : y + 1], ch)


def prep_call(taps, table, ids):
    ch, grains = table.shape
    depth, rows, cols = ids.shape
    return call(
        prep_body,
        [
            jax.ShapeDtypeStruct((3 * ch * rows, 3 * (rows + 2) * ch), BF16),
            jax.ShapeDtypeStruct((grains // LOW * ch, LOW), BF16),
            jax.ShapeDtypeStruct((depth * rows * ch, cols), BF16),
        ],
        [VM] * 3,
        [],
        2.5e9,
        1 << 18,
        16,
    )(taps, table, ids)


def split(x):
    high = x.astype(BF16)
    return high, (x - high.astype(F32)).astype(BF16)


def fold_lanes(blocks, lanes):
    return jnp.concatenate([b[:, i : i + lanes] for b in blocks for i in range(0, b.shape[1], lanes)], axis=0)


def unfold_lanes(x, rows, wide):
    count = wide // x.shape[1]
    cut = [x[i * rows : (i + 1) * rows].astype(F32) for i in range(x.shape[0] // rows)]
    wides = [jnp.concatenate(cut[i : i + count], axis=1) for i in range(0, len(cut), count)]
    return sum(wides[1:], wides[0])


def fine_body(scale, known, below, above, left, right, table, kernel, cot, bott_cot, after, *refs):
    out, part, message, feats, grads, stage, sems, pres, deltas, keeps, gather, fold, spread = refs
    ch, depth, rows, cols = out.shape
    place, count = lax.axis_index("space"), lax.axis_size("space")
    lane, lanes = lax.axis_index("chan"), lax.axis_size("chan")

    def fill(x):
        outer = ((0, left, lane == 0), (rows + 1, right, lane == lanes - 1))
        ids = [(y, jnp.where(off, -1, ref[x : x + 1])) for y, ref, off in outer]
        if 0 < x <= depth:
            at = (x * (rows + 2) + 1) * ch
            feats[at : at + rows * ch, :] = known[(x - 1) * rows * ch : x * rows * ch, :]
        else:
            ref, off = (below, place == 0) if x == 0 else (above, place == count - 1)
            ids = ids + [(y + 1, ref[y : y + 1]) for y in range(rows)]
            ids = [(y, jnp.where(off, -1, row)) for y, row in ids]
        for y, row in ids:
            at = (x * (rows + 2) + y) * ch
            feats[at : at + ch, :] = find(table, row, ch)

    group = ch * rows
    step = (rows + 2) * ch
    w = lax.broadcasted_iota(jnp.int32, (1, cols), 1)
    first, last = w == 0, w == cols - 1

    def forward(x):
        pres[x % 2] = jnp.dot(kernel[...], feats[x * step : (x + 3) * step, :], preferred_element_type=F32)

    def backward(x):
        term = dot_nt(deltas[x % 2], feats[x * step : (x + 3) * step, :])
        grads[...] = term if x == 0 else grads[...] + term

    gap = (iota(grads.shape, 1) % step) // ch - iota(grads.shape, 0) % rows
    for x in range(depth + 2):
        fill(x)
    for b in range(3):
        keeps[b] = hot(gap == b)
    gather[...] = hot(iota(gather.shape, 0) == iota(gather.shape, 1) // rows)
    m, n = iota(fold.shape, 0), iota(fold.shape, 1)
    fold[...] = hot((m // step == n // ch) & (m % ch == n % ch))
    m, n = iota(spread.shape, 0), iota(spread.shape, 1)
    tap = 9 * (m % (3 * ch) // ch) + m // (3 * ch)
    spread[...] = hot((m % ch == n // TAPS) & (tap == n % TAPS))
    forward(0)
    for x in range(depth):
        if x + 1 < depth:
            forward(x + 1)
        if x > 0:
            backward(x - 1)
        q = pres[x % 2]
        pre = q[group : 2 * group]
        pre = pre + jnp.where(first, 0.0, pltpu.roll(q[:group], 1, 1))
        pre = pre + jnp.where(last, 0.0, pltpu.roll(q[2 * group :], cols - 1, 1))
        act, slope = silu_parts(pre)
        stage[:, x] = act.reshape(ch, rows, cols).astype(BF16)
        pltpu.make_async_copy(stage.at[:, x], out.at[:, x], sems.at[x]).start()
        delta = cot[:, x].astype(F32).reshape(group, cols) * slope
        deltas[x % 2, :group] = jnp.where(last, 0.0, pltpu.roll(delta, cols - 1, 1)).astype(BF16)
        deltas[x % 2, group : 2 * group] = delta.astype(BF16)
        deltas[x % 2, 2 * group :] = jnp.where(first, 0.0, pltpu.roll(delta, 1, 1)).astype(BF16)
    backward(depth - 1)
    total = grads[...].astype(BF16)
    sums = [jnp.dot(gather[...], total * keeps[b], preferred_element_type=F32) for b in range(3)]
    tall = jnp.concatenate([piece for b in range(3) for piece in split(sums[b])], axis=0)
    tall = jnp.dot(tall, fold[...], preferred_element_type=F32)
    blocks = []
    for b in range(3):
        block = tall[6 * b * ch : (6 * b + 3) * ch] + tall[(6 * b + 3) * ch : (6 * b + 6) * ch]
        blocks += [block[e * ch : (e + 1) * ch] for e in range(3)]
    both = jnp.concatenate(split(jnp.concatenate(blocks, axis=1)), axis=0)
    moved = jnp.dot(both, spread[...], preferred_element_type=F32)
    result = moved[:ch] + moved[ch:]
    result = result * scale
    part[...] = result
    o_own, wide = bott_cot.shape
    message[:o_own, :] = bott_cot[...]
    message[o_own:, :] = fold_lanes([result.astype(BF16)], wide)
    for x in range(depth):
        pltpu.make_async_copy(stage.at[:, x], out.at[:, x], sems.at[x]).wait()


def fine_call(scale, known, below, above, left, right, table, kernel, cot, bott_cot, after):
    ch, depth, rows, cols = cot.shape
    o_own, lanes = bott_cot.shape
    more = ch * ch * TAPS // lanes
    S = jax.ShapeDtypeStruct
    return call(
        functools.partial(fine_body, scale),
        [
            S((ch, depth, rows, cols), BF16),
            S((ch, ch * TAPS), F32),
            S((o_own + more, lanes), BF16),
        ],
        [VM] * 10,
        [
            pltpu.VMEM(((depth + 2) * (rows + 2) * ch, cols), BF16),
            pltpu.VMEM((3 * ch * rows, 3 * ch * (rows + 2)), F32),
            pltpu.VMEM((ch, depth, rows, cols), BF16),
            pltpu.SemaphoreType.DMA((depth,)),
            pltpu.VMEM((2, 3 * ch * rows, cols), F32),
            pltpu.VMEM((2, 3 * ch * rows, cols), BF16),
            pltpu.VMEM((3, 3 * ch * rows, 3 * ch * (rows + 2)), BF16),
            pltpu.VMEM((3 * ch, 3 * ch * rows), BF16),
            pltpu.VMEM((3 * ch * (rows + 2), 3 * ch), BF16),
            pltpu.VMEM((27 * ch, ch * TAPS), BF16),
        ],
        6e9,
        4 << 20,
        20,
        [HB, VM, VM],
    )(known, below, above, left, right, table, kernel, cot, bott_cot, after)


def shift_masks(width, sign):
    lane = lax.broadcasted_iota(jnp.int32, (1, width), 1)
    y, w = lane // BW, lane % BW
    masks = []
    for b, e in STEPS:
        yy, ww = y + sign * b, w + sign * e
        masks.append((yy >= 0) & (yy < width // BW) & (ww >= 0) & (ww < BW))
    return masks


def convolve(weight, padded, chunks, before, pre_out, slabs, planes):
    o_own, lanes = pre_out.shape[0], pre_out.shape[1] // slabs
    width = lanes // planes
    masks = shift_masks(width, 1)
    for n in range(slabs):
        base = n * lanes
        at = [base + p * width for p in range(planes)]
        pre = [jnp.zeros((o_own, width), F32) if before is None else before[:, i : i + width] for i in at]
        for k, (b, e) in enumerate(STEPS):
            term = jnp.zeros((o_own, lanes), F32)
            for a in range(3):
                left = pl.ds((a * 9 + k) * o_own, o_own)
                for rows, columns in chunks:
                    win = padded[rows, base + a * width : base + a * width + lanes]
                    term = term + jnp.dot(weight[left, columns], win, preferred_element_type=F32)
            turn = -(b * BW + e) % width
            for p in range(planes):
                block = term[:, p * width : (p + 1) * width]
                if turn:
                    block = jnp.where(masks[k], pltpu.roll(block, turn, 1), 0.0)
                pre[p] = pre[p] + block
        for i, block in zip(at, pre):
            pre_out[:, i : i + width] = block


def lay(padded, row, piece, planes):
    slabs, cb, lanes = piece.shape
    width = lanes // planes
    place = lax.axis_index("space")
    rows = pl.ds(pl.multiple_of(row, cb), cb)
    padded[rows, :width] = jnp.zeros((cb, width), BF16)
    padded[rows, slabs * lanes + width :] = jnp.zeros((cb, width), BF16)
    for r in range(slabs):
        slab = lax.rem(place - r + slabs, slabs)
        padded[rows, pl.ds(pl.multiple_of(slab * lanes + width, width), lanes)] = piece[r]


def chip_body(planes, weight, after, mine, mate, pre_out, padded):
    slabs, cb, lanes = mine.shape
    chan = lax.axis_index("chan")
    lay(padded, (chan & 1) * cb, mine, planes)
    lay(padded, ((chan & 1) ^ 1) * cb, mate, planes)
    columns = pl.ds(pl.multiple_of((chan >> 1) * 2 * cb, 2 * cb), 2 * cb)
    convolve(weight, padded, [(pl.ds(0, 2 * cb), columns)], None, pre_out, slabs, planes)


def chip_call(weight, after, mine, mate, planes):
    slabs, cb, lanes = mine.shape
    return call(
        functools.partial(chip_body, planes),
        [jax.ShapeDtypeStruct((weight.shape[0] // 27, slabs * lanes), F32)],
        [VM] * 4,
        [pltpu.VMEM((2 * cb, (slabs + 1) * lanes), BF16)],
        2.5e9,
        1 << 20,
        16,
    )(weight, after, mine, mate)[0]


def bott_body(planes, weight, before, *refs):
    ins, (pre_out, padded) = refs[:-2], refs[-2:]
    slabs, cb, lanes = ins[0].shape
    chan = lax.axis_index("chan")
    for j, piece in enumerate(ins):
        lay(padded, (chan ^ j) * cb, piece, planes)
    chunks = []
    for other in range(1, len(ins) // 2):
        at = pl.ds(pl.multiple_of(((chan >> 1) ^ other) * 2 * cb, 2 * cb), 2 * cb)
        chunks.append((at, at))
    convolve(weight, padded, chunks, before, pre_out, slabs, planes)


def bott_call(weight, before, ins, planes):
    slabs, cb, lanes = ins[0].shape
    S = jax.ShapeDtypeStruct
    return call(
        functools.partial(bott_body, planes),
        [S(before.shape, F32), S((len(ins) * cb, (slabs + 1) * lanes), BF16)],
        [VM] * (2 + len(ins)),
        [],
        2.5e9,
        1 << 20,
        16,
    )(weight, before, *ins)


def spread_rows(rows_t, planes_of):
    width = rows_t.shape[2] - 2 * BW
    voxels = planes_of.T
    w = iota((voxels.shape[0], 1), 0) % BW
    none = jnp.zeros((BW, voxels.shape[1]), BF16)
    for e in (-1, 0, 1):
        moved = voxels
        if e:
            moved = jnp.where((w - e >= 0) & (w - e < BW), pltpu.roll(voxels, e % voxels.shape[0], 0), 0.0)
        moved = moved.astype(BF16)
        for p in range(voxels.shape[0] // width):
            rows_t[e + 1, p, :BW, :] = none
            rows_t[e + 1, p, BW : BW + width, :] = moved[p * width : (p + 1) * width]
            rows_t[e + 1, p, BW + width :, :] = none


def step_rows(rows_t, p, b, e):
    width = rows_t.shape[2] - 2 * BW
    return rows_t[e + 1, p, BW - b * BW : BW - b * BW + width, :]


def own_body(planes, weight, pre, cot, own_out, back, rows_t, stage, sem):
    send = pltpu.make_async_copy(stage, own_out, sem)
    o_own, lanes = cot.shape
    width = lanes // planes
    at = pl.multiple_of(lax.axis_index("space") * lanes, lanes)
    act, slope = silu_parts(pre[:, pl.ds(at, lanes)])
    stage[...] = together(act, planes)
    send.start()
    spread_rows(rows_t, (cot[...].astype(F32) * slope).astype(BF16).astype(F32))
    blocks = []
    for a in (-1, 0, 1):
        for b, e in STEPS:
            column = []
            for p in range(planes):
                inside = 0 <= p - a < planes
                column.append(step_rows(rows_t, p - a, b, e) if inside else jnp.zeros((width, o_own), BF16))
            blocks.append(jnp.concatenate(column, axis=0))
    back[...] = jnp.dot(jnp.concatenate(blocks, axis=1), weight[...], preferred_element_type=F32)
    send.wait()


def own_call(weight, pre, cot, planes):
    o_own, lanes = cot.shape
    width = lanes // planes
    S = jax.ShapeDtypeStruct
    return call(
        functools.partial(own_body, planes),
        [S((o_own * planes, width), BF16), S((lanes, weight.shape[1]), F32)],
        [VM] * 3,
        [
            pltpu.VMEM((3, planes, width + 2 * BW, o_own), BF16),
            pltpu.VMEM((o_own * planes, width), BF16),
            pltpu.SemaphoreType.DMA,
        ],
        1.6e9,
        1 << 20,
        16,
        [HB, VM],
    )(weight, pre, cot)


def back_body(slabs, planes, weight, pre, part, before, *refs):
    messages, (deltas, share, mine, part_sum, rows_t) = refs[:slabs], refs[slabs:]
    pieces, lanes, cb = mine.shape
    o_own = deltas.shape[0]
    width = lanes // planes
    total = slabs * planes
    place = lax.axis_index("space")
    chan = lax.axis_index("chan")
    deltas[:, :width] = jnp.zeros((o_own, width), F32)
    deltas[:, (total + 1) * width :] = jnp.zeros((o_own, width), F32)
    for r in range(slabs):
        at = pl.multiple_of(lax.rem(place - r + slabs, slabs) * lanes, lanes)
        slope = silu_parts(pre[:, pl.ds(at, lanes)])[1]
        delta = (messages[r][:o_own, :].astype(F32) * slope).astype(BF16).astype(F32)
        deltas[:, pl.ds(pl.multiple_of(at + width, width), lanes)] = delta
    base = place * lanes
    sides = [deltas[:, pl.ds(pl.multiple_of(i, width), width)] for i in (base, base + lanes + width)]
    spread_rows(rows_t, jnp.concatenate(sides, axis=1))
    sides = [jnp.concatenate([step_rows(rows_t, p, b, e) for b, e in STEPS], axis=1) for p in (0, 1)]
    first = jnp.dot(sides[0], weight[18 * o_own :, :], preferred_element_type=F32)
    last = jnp.dot(sides[1], weight[: 9 * o_own, :], preferred_element_type=F32)
    rows = [before[p * width : (p + 1) * width, :] for p in range(planes)]
    rows[0] = rows[0] + first
    rows[-1] = rows[-1] + last
    back = jnp.concatenate(rows, axis=0)
    grad = part[...]
    for r in range(1, slabs):
        grad = grad + unfold_lanes(messages[r][o_own:, :], *grad.shape)
    part_sum[...] = grad
    rest = fold_lanes([grad.astype(BF16)], cb)
    for j in range(pieces):
        block = back[:, j * cb : (j + 1) * cb]
        to = lax.rem(j - chan + pieces, pieces)
        mine[to] = block
        share[to, :lanes, :] = block.astype(BF16)
        share[j, lanes:, :] = rest


def back_call(weight, pre, part, before, messages, pieces, planes):
    slabs = len(messages)
    o_own, length = pre.shape
    lanes = length // slabs
    width = lanes // planes
    cb = weight.shape[1] // pieces
    S = jax.ShapeDtypeStruct
    return call(
        functools.partial(back_body, slabs, planes),
        [
            S((o_own, length + 2 * width), F32),
            S((pieces, lanes + part.size // cb, cb), BF16),
            S((pieces, lanes, cb), F32),
            S(part.shape, F32),
        ],
        [VM] * (4 + slabs),
        [pltpu.VMEM((3, 2, width + 2 * BW, o_own), BF16)],
        1.2e9,
        1 << 20,
        16,
    )(weight, pre, part, before, *messages)


PLAN = ((0, 0, 4), (0, 4, 9), (1, 0, 9), (2, 0, 4), (2, 4, 7), (2, 7, 9))


def wgrad_body(scale, delta, full, out, shifted, stage, sems):
    o_own, length = delta.shape[0], delta.shape[1] - 8 * BW
    width = 4 * BW
    total = length // width
    masks = shift_masks(width, -1)
    shifted[:, :width] = jnp.zeros((9 * o_own, width), BF16)
    shifted[:, (total + 1) * width :] = jnp.zeros((9 * o_own, width), BF16)

    def build(some):
        for k in some:
            b, e = STEPS[k]
            turn = (b * BW + e) % width
            for p in range(total):
                moved = delta[:, (p + 1) * width : (p + 2) * width]
                if turn:
                    moved = jnp.where(masks[k], pltpu.roll(moved, turn, 1), 0.0)
                shifted[k * o_own : (k + 1) * o_own, (p + 1) * width : (p + 2) * width] = moved.astype(BF16)

    busy = [[], []]
    built = 0
    right = full[:, width : width + length]
    for a, low, high in PLAN:
        build(range(built, max(built, high)))
        built = max(built, high)
        if low == 0:
            for copy in busy[a % 2]:
                copy.wait()
            busy[a % 2] = []
        left = shifted[low * o_own : high * o_own, (2 - a) * width : (2 - a) * width + length]
        term = dot_nt(left, right) * scale
        stage[a % 2, low:high] = term.reshape((high - low,) + stage.shape[2:])
        to = out.at[a * 9 + low : a * 9 + high]
        copy = pltpu.make_async_copy(stage.at[a % 2, low:high], to, sems.at[a % 2, low])
        copy.start()
        busy[a % 2].append(copy)
    for copies in busy:
        for copy in copies:
            copy.wait()


def wgrad_call(scale, delta, full):
    o_own, length = delta.shape
    c_all = full.shape[0]
    return call(
        functools.partial(wgrad_body, scale),
        [jax.ShapeDtypeStruct((27, o_own, c_all), F32)],
        [VM] * 2,
        [
            pltpu.VMEM((9 * o_own, length), BF16),
            pltpu.VMEM((2, 9, o_own, c_all), F32),
            pltpu.SemaphoreType.DMA((2, 9)),
        ],
        6.6e9,
        8 << 20,
        32,
        [HB],
    )(delta, full)[0]


def last_body(count, mine, part, *refs):
    others, (out, taps) = refs[:count], refs[count:]
    lanes = mine.shape[1]
    total = mine[0]
    grad = part[...]
    for other in others:
        total = total + other[:lanes, :].astype(F32)
        grad = grad + unfold_lanes(other[lanes:, :], *grad.shape)
    out[...] = together(total.T, out.shape[0] // total.shape[1])
    for c in range(taps.shape[0]):
        taps[c] = grad[:, c * TAPS : c * TAPS + taps.shape[2]]


def last_call(mine, part, others, planes):
    lanes, cb = mine.shape[1:]
    ch = part.shape[0]
    return call(
        functools.partial(last_body, len(others)),
        [
            jax.ShapeDtypeStruct((cb * planes, lanes // planes), BF16),
            jax.ShapeDtypeStruct((ch, ch, 27), F32),
        ],
        [VM] * (2 + len(others)),
        [],
        1e9,
        1 << 18,
        12,
    )(mine, part, *others)


def hop(x, axis, offset):
    count = lax.axis_size(axis)
    return lax.ppermute(x, axis, [(i, (i + offset) % count) for i in range(count)])


def swap(x, axis, bit):
    count = lax.axis_size(axis)
    return lax.ppermute(x, axis, [(i, i ^ bit) for i in range(count)])


def shards(labels, table, fine_weight, fine_cot, bott_in, bott_weight, bott_cot):
    depth, rows, cols = labels.shape
    ch = fine_weight.shape[2]
    spaces, chans = lax.axis_size("space"), lax.axis_size("chan")
    cb, planes, width = bott_in.shape
    lanes = planes * width
    o_own = bott_cot.shape[0]

    flat_in, flat_cot = bott_in.reshape(cb * planes, width), bott_cot.reshape(o_own * planes, width)
    slab, first, last, cot, ids, near_table = pack_call(labels, flat_in, flat_cot, table.T, planes)
    taps = fine_weight.reshape(3, 3, 3, ch, ch).transpose(1, 2, 4, 0, 3).reshape(3, 3 * ch, 3 * ch)
    kernel, lookup, known = prep_call(taps, near_table, ids)
    sends = [last] + [flat_in] * (spaces - 3) + [first]
    got = [hop(x, "space", r + 1) for r, x in enumerate(sends)]
    slabs, below, above, top, bottom = unpack_call(ids, slab, got, kernel)
    left = hop(bottom, "chan", 1)
    right = hop(top, "chan", chans - 1)
    scale = (depth * spaces * rows * chans * cols) ** -0.5
    mate = swap(slabs, "chan", 1)
    fine_out, part, message = fine_call(
        scale, known, below, above, left, right, lookup, kernel, fine_cot, cot, mate
    )
    cots = [cot] + [hop(message, "space", r) for r in range(1, spaces)]
    ins = [slabs, mate] + [swap(slabs, "chan", j) for j in range(2, chans)]

    weight = bott_weight.transpose(1, 0, 2).reshape(27 * o_own, cb * chans)
    pre = chip_call(weight, part, slabs, mate, planes)
    pre, full = bott_call(weight, pre, ins, planes)
    bott_out, before = own_call(weight, pre, cot, planes)
    delta, share, mine, part = back_call(weight, pre, part, before, cots, chans, planes)
    others = [hop(share[r], "chan", r) for r in range(1, chans)]
    bott_wgrad = wgrad_call((planes * spaces * width) ** -0.5, delta, full).transpose(1, 0, 2)
    bott_dgrad, fine_wgrad = last_call(mine, part, others, planes)
    fine_wgrad = fine_wgrad.transpose(2, 0, 1)
    return fine_out, fine_wgrad, bott_out.reshape(bott_cot.shape), bott_dgrad.reshape(bott_in.shape), bott_wgrad


def solution(mesh):
    placed = (
        P(("groups", "space"), "chan", None),
        P(),
        P(),
        P(None, ("groups", "space"), "chan", None),
        P("chan", ("groups", "space"), None),
        P("chan", None, None),
        P("chan", ("groups", "space"), None),
    )
    return jax.shard_map(
        shards,
        mesh=mesh,
        in_specs=placed,
        out_specs=(
            P(None, ("groups", "space"), "chan", None),
            P("groups", None, None),
            P("chan", ("groups", "space"), None),
            P("chan", ("groups", "space"), None),
            P(("groups", "chan"), None, None),
        ),
        check_vma=False,
    )
```
